256 devices in a mesh: space: 256 (over z, y, x, core).
Axes of the slice: x: 4, y: 4, z: 8, core: 2. Of those that a mesh axis runs over, the one named last changes fastest.
Arguments:
- positions: float32 [3, 32768], P(None, 'space'), may hold values from 0 to 2560, as said below
- species: int32 [32768], P('space'), may hold values from 0 to 5
- neighbours: int32 [24, 32768], P(None, 'space'), may hold values from 0 to 255, as said below
- counts: int32 [32768], P('space'), may hold values from 1 to 24, as said below
- ghost_index: int32 [2, 16384], P(None, 'space'), may hold values from 0 to 127, as said below
- embed: float32 [6, 64], replicated, may hold values from -6 to 6
- radial_in: float32 [2, 8, 64], replicated, may hold values from -2 to 2
- radial_mid: float32 [2, 64, 64], replicated, may hold values from -0.75 to 0.75
- radial_out: float32 [2, 64, 128], replicated, may hold values from -0.75 to 0.75
- mix_one: float32 [3, 64, 64], replicated, may hold values from -0.75 to 0.75
- vec_mix: float32 [64, 64], replicated, may hold values from -0.75 to 0.75
- mix_two: float32 [2, 64, 64], replicated, may hold values from -0.75 to 0.75
- readout: float32 [2, 64], replicated, may hold values from -0.75 to 0.75
Outputs:
- atom_energy: float32 [32768], P('space')
- forces: float32 [3, 32768], P(None, 'space')
The draws below stay inside these ranges and needn't reach their ends.
Inputs may be any that keep to these rules, and one draw needn't show every extreme that they name: `neighbours`: entries index the owning domain's table: local atoms first, then the 64 lower ghosts in the order of ghost_index row 0, then the 64 upper ghosts in the order of row 1; never the atom itself. `counts`: slots at or beyond an atom's count are padding; the first atom of every domain uses all 24 slots. `ghost_index`: row 0 of domain d holds each local index of 64 or more of domain d-1 once, row 1 each local index under 64 of domain d+1 once, in orders drawn from the seed. `positions`: the first coordinate of an atom of domain d lies in [10 d, 10 d + 10], the second in [0, 32], the third in [0, 4]; a domain holds 0.1 atoms per cubic angstrom.
All inputs are finite; a program needn't handle non-finite values.
Results may differ from the reference program's by a relative error of at most 0.0003.
Values sent between devices are 32-bit elements; how exact they have to be, the bound alone decides.
No kernel may reach another device: no remote copies, remote signals or barrier semaphores. Data moves between devices by JAX's collectives and lax.ppermute only.
A program may use at most 64 MiB of HBM per device.

```python
import jax
import jax.numpy as jnp
from jax import lax

C = 64
B = 8
H = 64
S = 6
K = 24
NY = 16
A_DEV = 128
NZ = 2
G_DEV = 64
ATOMS = 32768
GHOSTS = 16384
N_SPACE = 256


THICKNESS = 10.0


DEPTH_STEP = 2.5


SIDE_STEP = 2.0


JITTER = 0.4


def lattice(atom):
    local = atom % A_DEV
    return (atom // A_DEV, local // (NY * NZ), local // NZ % NY, local % NZ)


def reflect(value, limit):
    return jnp.where(value < 0, -value, jnp.where(value >= limit, 2 * (limit - 1) - value, value))


def ghost_orders(key):
    key = jax.random.fold_in(key, 21)
    shape = (2, N_SPACE, G_DEV)
    scores = jax.random.randint(key, shape, 0, 1 << 16) * G_DEV + lax.broadcasted_iota(jnp.int32, shape, 2)
    return jnp.argsort(scores, axis=2, stable=True).astype(jnp.int32)


def draw_positions(key, part):
    key = jax.random.fold_in(key, 11)
    atom = lax.broadcasted_iota(jnp.int32, (ATOMS,), 0)
    domain, layer, row, column = lattice(atom)
    noise = jax.random.uniform(key, (3, ATOMS), jnp.float32, -1.0, 1.0)
    first = domain.astype(jnp.float32) * THICKNESS + (layer.astype(jnp.float32) + 0.5) * DEPTH_STEP
    second = (row.astype(jnp.float32) + 0.5) * SIDE_STEP
    third = (column.astype(jnp.float32) + 0.5) * SIDE_STEP
    return jnp.stack([first, second, third], axis=0) + JITTER * noise


def draw_neighbours(key, part):
    orders = ghost_orders(key)
    inverse = jnp.argsort(orders, axis=2, stable=True).astype(jnp.int32).reshape(2, N_SPACE * G_DEV)
    key = jax.random.fold_in(key, 12)
    offsets_total = 44
    scores = jax.random.randint(key, (ATOMS, offsets_total), 0, 1 << 16) * offsets_total
    scores = scores + lax.broadcasted_iota(jnp.int32, (ATOMS, offsets_total), 1)
    picked = jnp.argsort(scores, axis=1, stable=True)[:, :K].astype(jnp.int32)
    code = picked + (picked >= 22).astype(jnp.int32)
    step_x = code // 9 - 2
    step_y = code // 3 % 3 - 1
    step_z = code % 3 - 1
    atom = lax.broadcasted_iota(jnp.int32, (ATOMS,), 0)
    domain, layer, row, column = lattice(atom)
    target_x = layer[:, None] + step_x
    target_y = reflect(row[:, None] + step_y, NY)
    target_z = reflect(column[:, None] + step_z, NZ)
    plane = target_y * NZ + target_z
    plane_size = NY * NZ
    own = target_x * plane_size + plane
    lower_pos = jnp.clip(target_x + 2, 0, 1) * plane_size + plane
    upper_pos = jnp.clip(target_x - 4, 0, 1) * plane_size + plane
    base = domain[:, None] * G_DEV
    lower_slot = jnp.take(inverse[0], base + lower_pos)
    upper_slot = jnp.take(inverse[1], base + upper_pos)
    entry = jnp.where(target_x < 0, A_DEV + lower_slot, jnp.where(target_x > 3, A_DEV + G_DEV + upper_slot, own))
    return entry.T.astype(jnp.int32)


def draw_counts(key, part):
    key = jax.random.fold_in(key, 13)
    row = lax.broadcasted_iota(jnp.int32, (ATOMS,), 0)
    band = row // A_DEV * 8 // N_SPACE
    dense = (band == 3) | (band == 4)
    low = jnp.where(dense, 3 * K // 4, 1)
    high = jnp.where(dense, K + 1, max(K // 4, 1) + 1)
    drawn = jax.random.randint(key, (ATOMS,), low, high)
    return jnp.where(row % A_DEV == 0, K, drawn).astype(jnp.int32)


def draw_ghost_index(key, part):
    orders = ghost_orders(key)
    first_row = lax.broadcasted_iota(jnp.int32, orders.shape, 0) == 0
    rows = jnp.where(first_row, orders + G_DEV, orders)
    return rows.reshape(2, GHOSTS).astype(jnp.int32)


def set_ends(result, stream_key, low, high):
    place = [jax.random.randint(jax.random.fold_in(stream_key, axis), (), 0, length) for axis, length in enumerate(result.shape)]
    longest = result.shape.index(max(result.shape))
    next_to = place[:longest] + [(place[longest] + 1) % result.shape[longest]] + place[longest + 1:]
    return result.at[tuple(place)].set(low).at[tuple(next_to)].set(high)


def normal_values(key, dims, deviation, reach, kind=jnp.bfloat16):
    entries = jax.random.normal(key, dims, jnp.float32) * deviation
    return jnp.minimum(jnp.maximum(entries, -reach), reach).astype(kind)


def setup_inputs(seed: int = 0) -> dict:
    arg_keys = jax.random.split(jax.random.key(seed), 14)
    positions = draw_positions(jax.random.fold_in(arg_keys[13], 71), 0)
    species = set_ends(jax.random.randint(arg_keys[1], (ATOMS,), 0, S), jax.random.fold_in(arg_keys[1], 1), 0, S - 1).astype(jnp.int32)
    neighbours = draw_neighbours(jax.random.fold_in(arg_keys[13], 71), 0)
    counts = draw_counts(jax.random.fold_in(arg_keys[13], 71), 0)
    ghost_index = draw_ghost_index(jax.random.fold_in(arg_keys[13], 71), 0)
    embed = normal_values(arg_keys[5], (S, C), 1.0, 6.0, jnp.float32)
    radial_in = normal_values(arg_keys[6], (2, B, H), B ** -0.5, 2.0, jnp.float32)
    radial_mid = normal_values(arg_keys[7], (2, H, H), H ** -0.5, 0.75, jnp.float32)
    radial_out = normal_values(arg_keys[8], (2, H, 2 * C), H ** -0.5, 0.75, jnp.float32)
    mix_one = normal_values(arg_keys[9], (3, C, C), C ** -0.5, 0.75, jnp.float32)
    vec_mix = normal_values(arg_keys[10], (C, C), C ** -0.5, 0.75, jnp.float32)
    mix_two = normal_values(arg_keys[11], (2, C, C), C ** -0.5, 0.75, jnp.float32)
    readout = normal_values(arg_keys[12], (2, C), C ** -0.5, 0.75, jnp.float32)
    return {"positions": positions, "species": species, "neighbours": neighbours, "counts": counts, "ghost_index": ghost_index, "embed": embed, "radial_in": radial_in, "radial_mid": radial_mid, "radial_out": radial_out, "mix_one": mix_one, "vec_mix": vec_mix, "mix_two": mix_two, "readout": readout}


RADIUS = 5.0
SOFTEN = 0.25

def silu(v):
    return v * jax.nn.sigmoid(v)

def hdot(a, b):
    return jnp.dot(a, b, precision=lax.Precision.HIGHEST, preferred_element_type=jnp.float32)

def edge_terms(pos_table, neighbours, counts):
    slots, atoms = neighbours.shape
    flat = neighbours.reshape(-1)
    pos_own = pos_table[:, :atoms]
    far = jnp.take(pos_table, flat, axis=1).reshape(3, slots, atoms)
    vector = far - pos_own[:, None, :]
    dist = jnp.sqrt(lax.optimization_barrier(jnp.sum(vector * vector, axis=0)) + SOFTEN)
    unit = vector / dist[None]
    ratio = jnp.minimum(dist / RADIUS, 1.0)
    envelope = 1.0 - 21.0 * ratio ** 5 + 35.0 * ratio ** 6 - 15.0 * ratio ** 7
    valid = (lax.broadcasted_iota(jnp.int32, (slots, atoms), 0) < counts[None, :]).astype(jnp.float32)
    order = (lax.broadcasted_iota(jnp.int32, (B, 1, 1), 0) + 1).astype(jnp.float32)
    basis = jnp.sin(order * (jnp.pi / RADIUS) * dist[None]) * (RADIUS / dist * envelope * valid)[None]
    return (unit, basis.reshape(B, slots * atoms))

def radial(basis, layer, radial_in, radial_mid, radial_out):
    hidden = silu(hdot(radial_in[layer].T, basis))
    hidden = silu(hdot(radial_mid[layer].T, hidden))
    return hdot(radial_out[layer].T, hidden)

def layer_one(pos_table, h0_table, neighbours, counts, radial_in, radial_mid, radial_out, mix_one, vec_mix):
    slots, atoms = neighbours.shape
    width = h0_table.shape[0]
    unit, basis = edge_terms(pos_table, neighbours, counts)
    weights = radial(basis, 0, radial_in, radial_mid, radial_out)
    w_a = weights[:width].reshape(width, slots, atoms)
    w_b = weights[width:].reshape(width, slots, atoms)
    h_far = jnp.take(h0_table, neighbours.reshape(-1), axis=1).reshape(width, slots, atoms)
    scale = 1.0 / jnp.sqrt(jnp.float32(slots))
    scalar_msg = lax.optimization_barrier(jnp.sum(w_a * h_far, axis=1)) * scale
    carried = w_b * h_far
    vector_msg = lax.optimization_barrier(jnp.sum(carried[None] * unit[:, None], axis=2)) * scale
    square = lax.optimization_barrier(jnp.sum(vector_msg * vector_msg, axis=0))
    h0_own = h0_table[:, :atoms]
    s_one = silu(hdot(mix_one[0].T, scalar_msg) + hdot(mix_one[1].T, h0_own) + hdot(mix_one[2].T, square))
    v_one = jnp.einsum('cd,xca->xda', vec_mix, vector_msg, precision=lax.Precision.HIGHEST)
    return jnp.concatenate([s_one[None], v_one], axis=0)

def layer_two(pos_table, feat_table, neighbours, counts, radial_in, radial_mid, radial_out, mix_two, readout):
    slots, atoms = neighbours.shape
    width = feat_table.shape[1]
    unit, basis = edge_terms(pos_table, neighbours, counts)
    weights = radial(basis, 1, radial_in, radial_mid, radial_out)
    w_a = weights[:width].reshape(width, slots, atoms)
    w_b = weights[width:].reshape(width, slots, atoms)
    far = jnp.take(feat_table, neighbours.reshape(-1), axis=2).reshape(4, width, slots, atoms)
    along = lax.optimization_barrier(jnp.sum(far[1:] * unit[:, None], axis=0))
    scale = 1.0 / jnp.sqrt(jnp.float32(slots))
    message = lax.optimization_barrier(jnp.sum(w_a * far[0] + w_b * along, axis=1)) * scale
    s_own = feat_table[0, :, :atoms]
    s_two = silu(hdot(mix_two[0].T, message) + hdot(mix_two[1].T, s_own))
    return hdot(readout[0][None], s_own)[0] + hdot(readout[1][None], s_two)[0]

def blocks_of(x):
    lead = x.shape[:-1]
    moved = x.reshape(lead + (N_SPACE, A_DEV))
    return jnp.moveaxis(moved, -2, 0)

def with_ghosts(blocks, lower_rows, upper_rows):
    zero = jnp.zeros_like(blocks[:1])
    below = jnp.concatenate([zero, blocks[:-1]], axis=0)
    above = jnp.concatenate([blocks[1:], zero], axis=0)
    lower = jax.vmap(lambda b, i: jnp.take(b, i, axis=-1))(below, lower_rows)
    upper = jax.vmap(lambda b, i: jnp.take(b, i, axis=-1))(above, upper_rows)
    return jnp.concatenate([blocks, lower, upper], axis=-1)

def reference(positions, species, neighbours, counts, ghost_index, embed, radial_in, radial_mid, radial_out, mix_one, vec_mix, mix_two, readout):
    rows = ghost_index.reshape(2, N_SPACE, G_DEV)
    lower_rows = rows[0].astype(jnp.int32)
    upper_rows = rows[1].astype(jnp.int32)
    nb_blocks = blocks_of(neighbours)
    count_blocks = counts.reshape(N_SPACE, A_DEV)
    onehot = (species[None, :] == lax.broadcasted_iota(jnp.int32, (S, species.shape[0]), 0)).astype(jnp.float32)
    h0 = hdot(embed.T, onehot)
    h0_tables = with_ghosts(blocks_of(h0), lower_rows, upper_rows)

    def first(args):
        pt, ht, nb, ct = args
        return layer_one(pt, ht, nb, ct, radial_in, radial_mid, radial_out, mix_one, vec_mix)

    def second(args):
        pt, ft, nb, ct = args
        return layer_two(pt, ft, nb, ct, radial_in, radial_mid, radial_out, mix_two, readout)

    def energy(pos):
        pos_tables = with_ghosts(blocks_of(pos), lower_rows, upper_rows)
        feats = lax.map(jax.checkpoint(first), (pos_tables, h0_tables, nb_blocks, count_blocks))
        feat_tables = with_ghosts(feats, lower_rows, upper_rows)
        energies = lax.map(jax.checkpoint(second), (pos_tables, feat_tables, nb_blocks, count_blocks))
        return energies.reshape(-1)
    atom_energy, pull = jax.vjp(energy, positions)
    grads = pull(jnp.ones_like(atom_energy))[0]
    return (atom_energy, -grads)
```

```python
import functools

import jax
import jax.numpy as jnp
from jax import lax
from jax.experimental import pallas as pl
from jax.experimental.pallas import tpu as pltpu
from jax.sharding import PartitionSpec as P

RADIUS = 5.0
SOFTEN = 0.25
F32 = jnp.float32
BF16 = jnp.bfloat16
HALF = 64
CHUNK = 4
MIB = 1024 * 1024


def hdot(a, b, dims=(((1,), (0,)), ((), ()))):
    return lax.dot_general(
        a, b, dims, precision=lax.Precision.HIGHEST, preferred_element_type=F32
    )


def hdot_t(a, b):
    return hdot(a, b, (((0,), (0,)), ((), ())))


def bdot(a, b):
    return jnp.dot(a, b, preferred_element_type=F32)


def bdot_nt(a, b):
    return lax.dot_general(a, b, (((1,), (1,)), ((), ())), preferred_element_type=F32)


def high(x):
    return x.astype(BF16).astype(F32)


def split_rows(x):
    hi = x.astype(BF16)
    lo = (x - hi.astype(F32)).astype(BF16)
    return hi, lo


def stack3(x):
    hi, lo = split_rows(x)
    return jnp.concatenate([hi, lo, hi], axis=0)


def sigmoid(v):
    return 0.5 + 0.5 * jnp.tanh(0.5 * v)


def roll64(x):
    return pltpu.roll(x, HALF, 1)


def lane_low(rows):
    return lax.broadcasted_iota(jnp.int32, (rows, 128), 1) < HALF


def parity_odd(rows):
    odd = lax.rem(lax.axis_index("space"), 2)
    return jnp.full((rows, 128), odd, jnp.int32) > 0


def prep_kernel(nb_ref, gi_ref, rin_ref, rmid_ref, rout_ref, sel_ref, win_ref, wmid_ref, wout_ref):
    atoms = nb_ref.shape[1]
    slots = nb_ref.shape[0]
    rows = lax.broadcasted_iota(jnp.int32, (atoms, atoms), 0)
    perm = (rows == jnp.broadcast_to(gi_ref[...], (atoms, atoms))).astype(F32).astype(BF16)
    for k in range(slots):
        nb = jnp.broadcast_to(nb_ref[k : k + 1, :], (atoms, atoms))
        lanes = pl.ds(k * atoms, atoms)
        sel_ref[0:atoms, lanes] = (rows == nb).astype(F32).astype(BF16)
        ghost = (rows + atoms == nb).astype(F32).astype(BF16)
        sel_ref[atoms : 2 * atoms, lanes] = bdot(perm, ghost).astype(BF16)
    for layer in range(2):
        w = rin_ref[layer]
        h = high(w)
        lo = w - h
        win_ref[layer] = jnp.concatenate([h, h, lo, lo], axis=0).T.astype(BF16)
        w = rmid_ref[layer]
        h = high(w)
        wmid_ref[layer] = jnp.concatenate([h, h, w - h], axis=0).T.astype(BF16)
        w = rout_ref[layer]
        h = high(w)
        wout_ref[layer] = jnp.concatenate([h, h, w - h], axis=0).T.astype(BF16)


def basis_rows(b):
    h = high(b)
    lo = b - h
    return jnp.concatenate([h, lo, h, lo], axis=0).astype(BF16)


def radial(win, wmid, wout, b):
    v1 = bdot(win, basis_rows(b))
    z1 = v1 * sigmoid(v1)
    v2 = bdot(wmid, stack3(z1))
    z2 = v2 * sigmoid(v2)
    return bdot(wout, stack3(z2))


def silu_pair(v, t):
    s = sigmoid(v)
    z = v * s
    return z, (s + z * (1.0 - s)) * t


def radial_pair(win, wmid, wout, b, db):
    z1, t1 = silu_pair(bdot(win, basis_rows(b)), bdot(win, basis_rows(db)))
    z2, t2 = silu_pair(bdot(wmid, stack3(z1)), bdot(wmid, stack3(t1)))
    return bdot(wout, stack3(z2)), bdot(wout, stack3(t2))


def tile8(x, times):
    return jnp.concatenate([x] * times, axis=0)


def geometry(far, own, valid):
    vec = [f - o for f, o in zip(far, own)]
    r2 = vec[0] * vec[0] + vec[1] * vec[1] + vec[2] * vec[2] + SOFTEN
    inv = lax.rsqrt(r2)
    inv = inv * (1.5 - 0.5 * r2 * inv * inv)
    rho = r2 * inv
    unit = [v * inv for v in vec]
    x = jnp.minimum(rho * (1.0 / RADIUS), 1.0)
    y = 1.0 - x
    x2 = x * x
    env = y * y * y * (1.0 + x * (3.0 + x * (6.0 + x * (10.0 + x * 15.0))))
    denv = (-105.0 / RADIUS) * x2 * x2 * y * y
    f = RADIUS * inv * env * valid
    df = RADIUS * inv * (denv - env * inv) * valid
    n = (lax.broadcasted_iota(jnp.int32, rho.shape, 0) + 1).astype(F32)
    turns = n * x
    whole = jnp.floor(turns + 0.5)
    frac = (turns - whole) * jnp.pi
    parity = whole - 2.0 * jnp.floor(0.5 * whole)
    sign = 1.0 - 2.0 * parity
    q = frac * frac
    sin = frac * (
        1.0
        + q * (-1 / 6 + q * (1 / 120 + q * (-1 / 5040 + q * (1 / 362880 + q * (-1 / 39916800)))))
    )
    cos = 1.0 + q * (
        -1 / 2
        + q * (1 / 24 + q * (-1 / 720 + q * (1 / 40320 + q * (-1 / 3628800 + q * (1 / 479001600)))))
    )
    sin = sin * sign
    cos = cos * sign
    return unit, inv, sin * f, sin * df + (n * (jnp.pi / RADIUS)) * cos * f


def layer_one_kernel(
    own_ref,
    near_ref,
    far_ref,
    sel_ref,
    counts_ref,
    embed_ref,
    win_ref,
    wmid_ref,
    wout_ref,
    mix_ref,
    vec_ref,
    feats_ref,
    near_out,
    far_out,
    geom_ref,
    pre_ref,
    b_ref,
    hfar_ref,
    tab_ref,
):
    atoms = own_ref.shape[1]
    slots = counts_ref.shape[0] and sel_ref.shape[1] // atoms
    width = embed_ref.shape[1]
    species = embed_ref.shape[0]
    odd4 = parity_odd(4)
    low4 = lane_low(4)
    own = own_ref[...]
    from_far = jnp.logical_xor(odd4, jnp.logical_not(low4))
    ghost = jnp.where(from_far, far_ref[...], near_ref[...])
    table = jnp.concatenate([own, ghost], axis=1)
    for c in range(3):
        p = jnp.broadcast_to(table[c : c + 1], (8, 2 * atoms))
        h = p.astype(BF16)
        rest = p - h.astype(F32)
        m = rest.astype(BF16)
        lo = (rest - m.astype(F32)).astype(BF16)
        part = jnp.concatenate([h.astype(F32), m.astype(F32), lo.astype(F32)], axis=0)
        tab_ref[c * 24 : c * 24 + 24, :] = part
    kind = jnp.broadcast_to(table[3:4], (species, 2 * atoms))
    onehot = (
        kind == (lax.broadcasted_iota(jnp.int32, (species, 2 * atoms), 0) + 1).astype(F32)
    ).astype(F32)
    h0 = hdot_t(embed_ref[...], onehot)
    h0_hi = high(h0)
    tab_ref[72 : 72 + width, :] = h0_hi
    tab_ref[72 + width : 72 + 2 * width, :] = h0 - h0_hi
    tab = tab_ref[...].astype(BF16)
    h0_own = h0[:, :atoms]

    step = CHUNK * atoms
    own_rep = [
        jnp.concatenate([jnp.broadcast_to(own[c : c + 1], (8, atoms))] * CHUNK, axis=1)
        for c in range(3)
    ]
    counts = jnp.broadcast_to(counts_ref[...], (8, atoms))
    a_sum = jnp.zeros((width, atoms), F32)
    b_sum = [jnp.zeros((width, atoms), F32) for _ in range(3)]
    for j in range(slots // CHUNK):
        lanes = pl.ds(j * step, step)
        g = bdot(tab, sel_ref[:, lanes])
        far = [g[24 * c : 24 * c + 8] + g[24 * c + 8 : 24 * c + 16] + g[24 * c + 16 : 24 * c + 24] for c in range(3)]
        h_far = g[72 : 72 + width] + g[72 + width : 72 + 2 * width]
        hfar_ref[:, lanes] = h_far
        valid = jnp.concatenate(
            [(counts > (j * CHUNK + k)).astype(F32) for k in range(CHUNK)], axis=1
        )
        unit, inv, b, db = geometry(far, own_rep, valid)
        for c in range(3):
            geom_ref[c, :, lanes] = unit[c]
        geom_ref[3, :, lanes] = inv
        geom_ref[4, :, lanes] = b
        geom_ref[5, :, lanes] = db
        w = radial(win_ref[0], wmid_ref[0], wout_ref[0], b)
        wa = w[:width] * h_far
        wb = w[width:] * h_far
        for k in range(CHUNK):
            s = slice(k * atoms, (k + 1) * atoms)
            a_sum = a_sum + wa[:, s]
            for c in range(3):
                b_sum[c] = b_sum[c] + wb[:, s] * tile8(unit[c][:, s], width // 8)
    scale = 1.0 / jnp.sqrt(F32(slots))
    a_sum = a_sum * scale
    b_all = jnp.concatenate([x * scale for x in b_sum], axis=1)
    sq = b_all * b_all
    q = sq[:, :atoms] + sq[:, atoms : 2 * atoms] + sq[:, 2 * atoms :]
    pre = hdot_t(mix_ref[0], a_sum) + hdot_t(mix_ref[1], h0_own) + hdot_t(mix_ref[2], q)
    pre_ref[...] = pre
    b_ref[...] = b_all
    s1 = pre * sigmoid(pre)
    v1 = hdot_t(vec_ref[...], b_all)
    lo_part = jnp.concatenate([s1, v1[:, :atoms]], axis=0)
    hi_part = jnp.concatenate([v1[:, atoms : 2 * atoms], v1[:, 2 * atoms :]], axis=0)
    feats_ref[0 : 2 * width] = lo_part
    feats_ref[2 * width :] = hi_part
    pack_halves(lo_part, hi_part, near_out, far_out)


def pack_halves(lo_part, hi_part, near_out, far_out):
    rows = lo_part.shape[0]
    low = lane_low(rows)
    odd = parity_odd(rows)
    lo_roll = roll64(lo_part)
    hi_roll = roll64(hi_part)
    low_lanes = jnp.where(low, lo_part, hi_roll)
    high_lanes = jnp.where(low, lo_roll, hi_part)
    near_out[...] = jnp.where(odd, low_lanes, high_lanes)
    far_out[...] = jnp.where(odd, high_lanes, low_lanes)


def radial_two_kernel(geom_ref, win_ref, wmid_ref, wout_ref, w_ref, dw_ref):
    n = geom_ref.shape[2]
    step = CHUNK * 128
    for j in range(n // step):
        lanes = pl.ds(j * step, step)
        w, dw = radial_pair(
            win_ref[1], wmid_ref[1], wout_ref[1], geom_ref[4, :, lanes], geom_ref[5, :, lanes]
        )
        w_ref[:, lanes] = w
        dw_ref[:, lanes] = dw


def edge_gradient(unit, inv, drho, du):
    dot = unit[0] * du[0] + unit[1] * du[1] + unit[2] * du[2]
    radial_part = drho - dot * inv
    return [unit[c] * radial_part + du[c] * inv for c in range(3)]


def sum_rows(x):
    return jnp.sum(x, axis=0, keepdims=True)


def position_rows(grads):
    g = jnp.concatenate([jnp.broadcast_to(x, (8, x.shape[1])) for x in grads], axis=0)
    x = jnp.concatenate([g[0:1], g[8:9], g[16:17], jnp.zeros((5, g.shape[1]), F32)], axis=0)
    h = high(x)
    return jnp.concatenate([h, x - h], axis=0).astype(BF16)


def layer_two_kernel(
    feats_ref,
    near_ref,
    far_ref,
    sel_ref,
    geom_ref,
    w_ref,
    dw_ref,
    mix_ref,
    read_ref,
    energy_ref,
    gown_ref,
    near_out,
    far_out,
    gpos_ref,
    far_scr,
    along_scr,
):
    atoms = feats_ref.shape[1]
    width = mix_ref.shape[1]
    slots = sel_ref.shape[1] // atoms
    rows = 2 * width
    low = lane_low(rows)
    odd = parity_odd(rows)
    near = near_ref[...]
    far = far_ref[...]
    upper = jnp.where(odd, far, near)
    lower = jnp.where(odd, near, far)
    g_lo = jnp.where(low, upper, roll64(lower))
    g_hi = jnp.where(low, roll64(upper), lower)
    feats = feats_ref[...]
    table = jnp.concatenate([feats, jnp.concatenate([g_lo, g_hi], axis=0)], axis=1)
    t_hi, t_lo = split_rows(table)
    tab = jnp.concatenate([t_hi, t_lo], axis=0)
    step = CHUNK * atoms
    m = jnp.zeros((width, atoms), F32)
    for j in range(slots // CHUNK):
        lanes = pl.ds(j * step, step)
        g = bdot(tab, sel_ref[:, lanes])
        f = g[: 4 * width] + g[4 * width :]
        far_scr[:, lanes] = f
        along = f[width : 2 * width] * tile8(geom_ref[0, :, lanes], width // 8)
        along = along + f[2 * width : 3 * width] * tile8(geom_ref[1, :, lanes], width // 8)
        along = along + f[3 * width :] * tile8(geom_ref[2, :, lanes], width // 8)
        along_scr[:, lanes] = along
        msg = w_ref[0:width, lanes] * f[:width] + w_ref[width : 2 * width, lanes] * along
        for k in range(CHUNK):
            m = m + msg[:, k * atoms : (k + 1) * atoms]
    scale = 1.0 / jnp.sqrt(F32(slots))
    s1 = feats[:width]
    pre = hdot_t(mix_ref[0], m * scale) + hdot_t(mix_ref[1], s1)
    sg = sigmoid(pre)
    s2 = pre * sg
    energy_ref[...] = hdot(read_ref[0:1], s1) + hdot(read_ref[1:2], s2)
    read = read_ref[...].T
    r_one = jnp.broadcast_to(read[:, 0:1], (width, atoms))
    r_two = jnp.broadcast_to(read[:, 1:2], (width, atoms))
    gpre = r_two * (sg + s2 * (1.0 - sg))
    gm = hdot(mix_ref[0], gpre) * scale
    gs_own = r_one + hdot(mix_ref[1], gpre)
    gm_rep = jnp.concatenate([gm] * CHUNK, axis=1)
    acc = jnp.zeros((8 * width + 16, 2 * atoms), F32)
    own_pos = [jnp.zeros((1, atoms), F32) for _ in range(3)]
    for j in range(slots // CHUNK):
        lanes = pl.ds(j * step, step)
        unit = [geom_ref[c, :, lanes] for c in range(3)]
        ga = w_ref[0:width, lanes] * gm_rep
        gb = w_ref[width : 2 * width, lanes] * gm_rep
        gv = [gb * tile8(unit[c], width // 8) for c in range(3)]
        drho = gm_rep * (
            dw_ref[0:width, lanes] * far_scr[0:width, lanes]
            + dw_ref[width : 2 * width, lanes] * along_scr[:, lanes]
        )
        du = [sum_rows(gb * far_scr[(c + 1) * width : (c + 2) * width, lanes]) for c in range(3)]
        gp = edge_gradient(
            [u[0:1] for u in unit], geom_ref[3, 0:1, lanes], sum_rows(drho), du
        )
        for k in range(CHUNK):
            for c in range(3):
                own_pos[c] = own_pos[c] + gp[c][:, k * atoms : (k + 1) * atoms]
        grads = jnp.concatenate([ga] + gv, axis=0)
        hi, lo = split_rows(grads)
        acc = acc + bdot_nt(
            jnp.concatenate([hi, lo, position_rows(gp)], axis=0), sel_ref[:, lanes]
        )
    grads = acc[: 4 * width] + acc[4 * width : 8 * width]
    own = grads[:, :atoms]
    gown_ref[0:width] = own[0:width] + gs_own
    gown_ref[width:] = own[width:]
    ghost = grads[:, atoms:]
    pack_halves_by_lane(ghost[: 2 * width], ghost[2 * width :], near_out, far_out)
    pos = acc[8 * width : 8 * width + 8] + acc[8 * width + 8 :]
    centre = jnp.concatenate(own_pos + [jnp.zeros((5, atoms), F32)], axis=0)
    gpos_ref[:, :atoms] = pos[:, :atoms] - centre
    gpos_ref[:, atoms:] = pos[:, atoms:]


def pack_halves_by_lane(lo_part, hi_part, near_out, far_out):
    rows = lo_part.shape[0]
    low = lane_low(rows)
    odd = parity_odd(rows)
    to_upper = jnp.where(low, lo_part, roll64(hi_part))
    to_lower = jnp.where(low, roll64(lo_part), hi_part)
    near_out[...] = jnp.where(odd, to_lower, to_upper)
    far_out[...] = jnp.where(odd, to_upper, to_lower)


def tangent_one_kernel(geom_ref, hfar_ref, win_ref, wmid_ref, wout_ref, out_ref):
    n = geom_ref.shape[2]
    width = hfar_ref.shape[0]
    step = CHUNK * 128
    for j in range(n // step):
        lanes = pl.ds(j * step, step)
        w, dw = radial_pair(
            win_ref[0], wmid_ref[0], wout_ref[0], geom_ref[4, :, lanes], geom_ref[5, :, lanes]
        )
        h = hfar_ref[:, lanes]
        out_ref[0:width, lanes] = dw[:width] * h
        out_ref[width : 2 * width, lanes] = dw[width:] * h
        out_ref[2 * width :, lanes] = w[width:] * h


def back_one_kernel(
    gown_ref,
    near_ref,
    far_ref,
    sel_ref,
    geom_ref,
    edge_ref,
    pre_ref,
    b_ref,
    mix_ref,
    vec_ref,
    gpos_in,
    gpos_ref,
):
    atoms = gown_ref.shape[1]
    width = mix_ref.shape[1]
    slots = sel_ref.shape[1] // atoms
    rows = 2 * width
    low = lane_low(rows)
    odd = parity_odd(rows)
    near = near_ref[...]
    far = far_ref[...]
    upper = jnp.where(odd, far, near)
    lower = jnp.where(odd, near, far)
    g_lo = gown_ref[0:rows] + jnp.where(low, lower, roll64(upper))
    g_hi = gown_ref[rows:] + jnp.where(low, roll64(lower), upper)
    scale = 1.0 / jnp.sqrt(F32(slots))
    pre = pre_ref[...]
    sg = sigmoid(pre)
    gpre = g_lo[:width] * (sg + pre * sg * (1.0 - sg))
    ga = hdot(mix_ref[0], gpre) * scale
    gq = hdot(mix_ref[2], gpre)
    gv = jnp.concatenate([g_lo[width:], g_hi[:width], g_hi[width:]], axis=1)
    gb_all = hdot(vec_ref[...], gv) + 2.0 * b_ref[...] * jnp.concatenate([gq] * 3, axis=1)
    gb = [gb_all[:, c * atoms : (c + 1) * atoms] * scale for c in range(3)]
    ga_rep = jnp.concatenate([ga] * CHUNK, axis=1)
    gb_rep = [jnp.concatenate([g] * CHUNK, axis=1) for g in gb]
    step = CHUNK * atoms
    acc = jnp.zeros((16, 2 * atoms), F32)
    own_pos = [jnp.zeros((1, atoms), F32) for _ in range(3)]
    for j in range(slots // CHUNK):
        lanes = pl.ds(j * step, step)
        unit = [geom_ref[c, :, lanes] for c in range(3)]
        gbu = gb_rep[0] * tile8(unit[0], width // 8)
        gbu = gbu + gb_rep[1] * tile8(unit[1], width // 8)
        gbu = gbu + gb_rep[2] * tile8(unit[2], width // 8)
        drho = edge_ref[0:width, lanes] * ga_rep + edge_ref[width : 2 * width, lanes] * gbu
        carried = edge_ref[2 * width :, lanes]
        du = [sum_rows(carried * gb_rep[c]) for c in range(3)]
        gp = edge_gradient(
            [u[0:1] for u in unit], geom_ref[3, 0:1, lanes], sum_rows(drho), du
        )
        for k in range(CHUNK):
            for c in range(3):
                own_pos[c] = own_pos[c] + gp[c][:, k * atoms : (k + 1) * atoms]
        acc = acc + bdot_nt(position_rows(gp), sel_ref[:, lanes])
    pos = acc[0:8] + acc[8:16] + gpos_in[...]
    centre = jnp.concatenate(own_pos + [jnp.zeros((5, atoms), F32)], axis=0)
    gpos_ref[:, :atoms] = pos[:, :atoms] - centre
    gpos_ref[:, atoms:] = pos[:, atoms:]


def call(kernel, out_shapes, args, scratch=(), flops=0, transcendentals=0):
    moved = sum(x.size * x.dtype.itemsize for x in list(args) + list(out_shapes))
    return pl.pallas_call(
        kernel,
        out_shape=out_shapes,
        in_specs=[pl.BlockSpec(memory_space=pltpu.VMEM)] * len(args),
        out_specs=[pl.BlockSpec(memory_space=pltpu.VMEM)] * len(out_shapes),
        scratch_shapes=list(scratch),
        cost_estimate=pl.CostEstimate(
            flops=flops, bytes_accessed=moved, transcendentals=transcendentals
        ),
        compiler_params=pltpu.CompilerParams(vmem_limit_bytes=48 * MIB),
    )(*args)


def shape(dims, dtype=F32):
    return jax.ShapeDtypeStruct(dims, dtype)


def body(
    positions,
    species,
    neighbours,
    counts,
    ghost_index,
    embed,
    radial_in,
    radial_mid,
    radial_out,
    mix_one,
    vec_mix,
    mix_two,
    readout,
):
    atoms = positions.shape[1]
    slots = neighbours.shape[0]
    edges = slots * atoms
    nbasis, hidden = radial_in.shape[1:]
    width = embed.shape[1]
    devices = lax.axis_size("space")
    near_route = [(i, i ^ 1) for i in range(devices)]
    far_route = [(i, ((i + 1) ^ 1) - 1) for i in range(1, devices - 1)]

    def swap_near(x):
        return lax.ppermute(x, "space", near_route)

    def swap_far(x):
        return lax.ppermute(x, "space", far_route)

    own = jnp.concatenate([positions, (species + 1).astype(F32)[None]], axis=0)
    near = swap_near(own)
    far = swap_far(own)
    sel, win, wmid, wout = call(
        prep_kernel,
        [
            shape((2 * atoms, edges), BF16),
            shape((2, hidden, 4 * nbasis), BF16),
            shape((2, hidden, 3 * hidden), BF16),
            shape((2, 2 * width, 3 * hidden), BF16),
        ],
        [neighbours, ghost_index.reshape(1, atoms), radial_in, radial_mid, radial_out],
        flops=10**8,
    )
    feats, near_f, far_f, geom, pre, b_all, h_far = call(
        layer_one_kernel,
        [
            shape((4 * width, atoms)),
            shape((2 * width, atoms)),
            shape((2 * width, atoms)),
            shape((6, 8, edges)),
            shape((width, atoms)),
            shape((width, 3 * atoms)),
            shape((width, edges)),
        ],
        [own, near, far, sel, counts[None], embed, win, wmid, wout, mix_one, vec_mix],
        scratch=[pltpu.VMEM((72 + 2 * width, 2 * atoms), F32)],
        flops=10**9,
    )
    near_f = swap_near(near_f)
    far_f = swap_far(far_f)
    w, dw = call(
        radial_two_kernel,
        [shape((2 * width, edges)), shape((2 * width, edges))],
        [geom, win, wmid, wout],
        flops=2 * 10**9,
    )
    energy, g_own, near_g, far_g, gpos = call(
        layer_two_kernel,
        [
            shape((1, atoms)),
            shape((4 * width, atoms)),
            shape((2 * width, atoms)),
            shape((2 * width, atoms)),
            shape((8, 2 * atoms)),
        ],
        [feats, near_f, far_f, sel, geom, w, dw, mix_two, readout],
        scratch=[pltpu.VMEM((4 * width, edges), F32), pltpu.VMEM((width, edges), F32)],
        flops=10**9,
    )
    near_g = swap_near(near_g)
    far_g = swap_far(far_g)
    (edge,) = call(
        tangent_one_kernel,
        [shape((3 * width, edges))],
        [geom, h_far, win, wmid, wout],
        flops=2 * 10**9,
    )
    (gpos,) = call(
        back_one_kernel,
        [shape((8, 2 * atoms))],
        [g_own, near_g, far_g, sel, geom, edge, pre, b_all, mix_one, vec_mix, gpos],
        flops=10**9,
    )
    ghost = gpos[:3, atoms:]
    near_p = swap_near(ghost)
    far_p = swap_far(ghost)
    odd = lax.rem(lax.axis_index("space"), 2) == 1
    low = lax.broadcasted_iota(jnp.int32, (3, atoms), 1) < HALF
    come = jnp.where(low == odd, near_p, far_p)
    return (energy[0], -(gpos[:3, :atoms] + come))


def solution(mesh):
    placed = (
        P(None, "space"),
        P("space"),
        P(None, "space"),
        P("space"),
        P(None, "space"),
        P(),
        P(),
        P(),
        P(),
        P(),
        P(),
        P(),
        P(),
    )
    return jax.shard_map(
        body, mesh=mesh, in_specs=placed, out_specs=(P("space"), P(None, "space")), check_vma=False
    )
```

```python
import functools

import jax
import jax.numpy as jnp
from jax import lax
from jax.experimental import pallas as pl
from jax.experimental.pallas import tpu as pltpu
from jax.sharding import PartitionSpec as P

RADIUS = 5.0
SOFTEN = 0.25
F32 = jnp.float32
BF16 = jnp.bfloat16
HALF = 64
CHUNK = 4
MIB = 1024 * 1024


def hdot(a, b, dims=(((1,), (0,)), ((), ()))):
    return lax.dot_general(
        a, b, dims, precision=lax.Precision.HIGHEST, preferred_element_type=F32
    )


def hdot_t(a, b):
    return hdot(a, b, (((0,), (0,)), ((), ())))


def bdot(a, b):
    return jnp.dot(a, b, preferred_element_type=F32)


def bdot_nt(a, b):
    return lax.dot_general(a, b, (((1,), (1,)), ((), ())), preferred_element_type=F32)


def high(x):
    return x.astype(BF16).astype(F32)


def split_rows(x):
    hi = x.astype(BF16)
    lo = (x - hi.astype(F32)).astype(BF16)
    return hi, lo


def stack3(x):
    hi, lo = split_rows(x)
    return jnp.concatenate([hi, lo, hi], axis=0)


def sigmoid(v):
    return 0.5 + 0.5 * jnp.tanh(0.5 * v)


def roll64(x):
    return pltpu.roll(x, HALF, 1)


def lane_low(rows):
    return lax.broadcasted_iota(jnp.int32, (rows, 128), 1) < HALF


def parity_odd(rows):
    odd = lax.rem(lax.axis_index("space"), 2)
    return jnp.full((rows, 128), odd, jnp.int32) > 0


def pack_kernel(pos_hbm, kind_hbm, own_ref, pos_ref, kind_ref, sems):
    copies = [
        pltpu.make_async_copy(pos_hbm, pos_ref, sems.at[0]),
        pltpu.make_async_copy(kind_hbm, kind_ref, sems.at[1]),
    ]
    for c in copies:
        c.start()
    for c in copies:
        c.wait()
    own_ref[0:3, :] = pos_ref[...]
    own_ref[3:4, :] = (kind_ref[...] + 1).astype(F32)


def prep_kernel(
    nb_hbm,
    gi_hbm,
    rin_hbm,
    rmid_hbm,
    rout_hbm,
    counts_hbm,
    embed_hbm,
    mix_one_hbm,
    vec_hbm,
    mix_two_hbm,
    read_hbm,
    sel_ref,
    win_ref,
    wmid_ref,
    wout_ref,
    counts_ref,
    embed_ref,
    mix_one_ref,
    vec_ref,
    mix_two_ref,
    read_ref,
    nb_ref,
    gi_ref,
    rin_ref,
    rmid_ref,
    rout_ref,
    sems,
):
    moves = [
        (nb_hbm, nb_ref),
        (gi_hbm, gi_ref),
        (rin_hbm, rin_ref),
        (rmid_hbm, rmid_ref),
        (rout_hbm, rout_ref),
        (counts_hbm, counts_ref),
        (embed_hbm, embed_ref),
        (mix_one_hbm, mix_one_ref),
        (vec_hbm, vec_ref),
        (mix_two_hbm, mix_two_ref),
        (read_hbm, read_ref),
    ]
    copies = [
        pltpu.make_async_copy(src, dst, sems.at[i]) for i, (src, dst) in enumerate(moves)
    ]
    for c in copies:
        c.start()
    for c in copies:
        c.wait()
    atoms = nb_ref.shape[1]
    slots = nb_ref.shape[0]
    rows = lax.broadcasted_iota(jnp.int32, (atoms, atoms), 0)
    half_rows = lax.broadcasted_iota(jnp.int32, (atoms, HALF), 0)
    perm = jnp.concatenate(
        [
            (half_rows == jnp.broadcast_to(gi_ref[i : i + 1, :], (atoms, HALF))).astype(F32)
            for i in range(2)
        ],
        axis=1,
    ).astype(BF16)
    for k in range(slots):
        nb = jnp.broadcast_to(nb_ref[k : k + 1, :], (atoms, atoms))
        lanes = pl.ds(k * atoms, atoms)
        sel_ref[0:atoms, lanes] = (rows == nb).astype(F32).astype(BF16)
        ghost = (rows + atoms == nb).astype(F32).astype(BF16)
        sel_ref[atoms : 2 * atoms, lanes] = bdot(perm, ghost).astype(BF16)
    for layer in range(2):
        w = rin_ref[layer]
        h = high(w)
        lo = w - h
        win_ref[layer] = jnp.concatenate([h, h, lo, lo], axis=0).T.astype(BF16)
        w = rmid_ref[layer]
        h = high(w)
        wmid_ref[layer] = jnp.concatenate([h, h, w - h], axis=0).T.astype(BF16)
        w = rout_ref[layer]
        h = high(w)
        wout_ref[layer] = jnp.concatenate([h, h, w - h], axis=0).T.astype(BF16)


def basis_rows(b):
    h = high(b)
    lo = b - h
    return jnp.concatenate([h, lo, h, lo], axis=0).astype(BF16)


def radial(win, wmid, wout, b):
    v1 = bdot(win, basis_rows(b))
    z1 = v1 * sigmoid(v1)
    v2 = bdot(wmid, stack3(z1))
    z2 = v2 * sigmoid(v2)
    return bdot(wout, stack3(z2))


def silu_pair(v, t):
    s = sigmoid(v)
    z = v * s
    return z, (s + z * (1.0 - s)) * t


def radial_pair(win, wmid, wout, b, db):
    z1, t1 = silu_pair(bdot(win, basis_rows(b)), bdot(win, basis_rows(db)))
    z2, t2 = silu_pair(bdot(wmid, stack3(z1)), bdot(wmid, stack3(t1)))
    return bdot(wout, stack3(z2)), bdot(wout, stack3(t2))


def tile8(x, times):
    return jnp.concatenate([x] * times, axis=0)


def geometry(far, own, valid):
    vec = [f - o for f, o in zip(far, own)]
    r2 = vec[0] * vec[0] + vec[1] * vec[1] + vec[2] * vec[2] + SOFTEN
    inv = lax.rsqrt(r2)
    inv = inv * (1.5 - 0.5 * r2 * inv * inv)
    rho = r2 * inv
    unit = [v * inv for v in vec]
    x = jnp.minimum(rho * (1.0 / RADIUS), 1.0)
    y = 1.0 - x
    x2 = x * x
    env = y * y * y * (1.0 + x * (3.0 + x * (6.0 + x * (10.0 + x * 15.0))))
    denv = (-105.0 / RADIUS) * x2 * x2 * y * y
    f = RADIUS * inv * env * valid
    df = RADIUS * inv * (denv - env * inv) * valid
    n = (lax.broadcasted_iota(jnp.int32, rho.shape, 0) + 1).astype(F32)
    turns = n * x
    whole = jnp.floor(turns + 0.5)
    frac = (turns - whole) * jnp.pi
    parity = whole - 2.0 * jnp.floor(0.5 * whole)
    sign = 1.0 - 2.0 * parity
    q = frac * frac
    sin = frac * (
        1.0
        + q * (-1 / 6 + q * (1 / 120 + q * (-1 / 5040 + q * (1 / 362880 + q * (-1 / 39916800)))))
    )
    cos = 1.0 + q * (
        -1 / 2
        + q * (1 / 24 + q * (-1 / 720 + q * (1 / 40320 + q * (-1 / 3628800 + q * (1 / 479001600)))))
    )
    sin = sin * sign
    cos = cos * sign
    return unit, inv, sin * f, sin * df + (n * (jnp.pi / RADIUS)) * cos * f


def layer_one_kernel(
    own_ref,
    near_ref,
    far_ref,
    sel_ref,
    counts_ref,
    embed_ref,
    win_ref,
    wmid_ref,
    wout_ref,
    mix_ref,
    vec_ref,
    feats_ref,
    near_out,
    far_out,
    geom_ref,
    pre_ref,
    b_ref,
    hfar_ref,
    tab_ref,
):
    atoms = own_ref.shape[1]
    slots = counts_ref.shape[0] and sel_ref.shape[1] // atoms
    width = embed_ref.shape[1]
    species = embed_ref.shape[0]
    odd4 = parity_odd(4)
    low4 = lane_low(4)
    own = own_ref[...]
    from_far = jnp.logical_xor(odd4, jnp.logical_not(low4))
    ghost = jnp.where(from_far, far_ref[...], near_ref[...])
    table = jnp.concatenate([own, ghost], axis=1)
    for c in range(3):
        p = jnp.broadcast_to(table[c : c + 1], (8, 2 * atoms))
        h = p.astype(BF16)
        rest = p - h.astype(F32)
        m = rest.astype(BF16)
        lo = (rest - m.astype(F32)).astype(BF16)
        part = jnp.concatenate([h.astype(F32), m.astype(F32), lo.astype(F32)], axis=0)
        tab_ref[c * 24 : c * 24 + 24, :] = part
    kind = jnp.broadcast_to(table[3:4], (species, 2 * atoms))
    onehot = (
        kind == (lax.broadcasted_iota(jnp.int32, (species, 2 * atoms), 0) + 1).astype(F32)
    ).astype(F32)
    h0 = hdot_t(embed_ref[...], onehot)
    h0_hi = high(h0)
    tab_ref[72 : 72 + width, :] = h0_hi
    tab_ref[72 + width : 72 + 2 * width, :] = h0 - h0_hi
    tab = tab_ref[...].astype(BF16)
    h0_own = h0[:, :atoms]

    step = CHUNK * atoms
    own_rep = [
        jnp.concatenate([jnp.broadcast_to(own[c : c + 1], (8, atoms))] * CHUNK, axis=1)
        for c in range(3)
    ]
    counts = jnp.broadcast_to(counts_ref[...], (8, atoms))
    a_sum = jnp.zeros((width, atoms), F32)
    b_sum = [jnp.zeros((width, atoms), F32) for _ in range(3)]
    for j in range(slots // CHUNK):
        lanes = pl.ds(j * step, step)
        g = bdot(tab, sel_ref[:, lanes])
        far = [g[24 * c : 24 * c + 8] + g[24 * c + 8 : 24 * c + 16] + g[24 * c + 16 : 24 * c + 24] for c in range(3)]
        h_far = g[72 : 72 + width] + g[72 + width : 72 + 2 * width]
        hfar_ref[:, lanes] = h_far
        valid = jnp.concatenate(
            [(counts > (j * CHUNK + k)).astype(F32) for k in range(CHUNK)], axis=1
        )
        unit, inv, b, db = geometry(far, own_rep, valid)
        for c in range(3):
            geom_ref[c, :, lanes] = unit[c]
        geom_ref[3, :, lanes] = inv
        geom_ref[4, :, lanes] = b
        geom_ref[5, :, lanes] = db
        w = radial(win_ref[0], wmid_ref[0], wout_ref[0], b)
        wa = w[:width] * h_far
        wb = w[width:] * h_far
        for k in range(CHUNK):
            s = slice(k * atoms, (k + 1) * atoms)
            a_sum = a_sum + wa[:, s]
            for c in range(3):
                b_sum[c] = b_sum[c] + wb[:, s] * tile8(unit[c][:, s], width // 8)
    scale = 1.0 / jnp.sqrt(F32(slots))
    a_sum = a_sum * scale
    b_all = jnp.concatenate([x * scale for x in b_sum], axis=1)
    sq = b_all * b_all
    q = sq[:, :atoms] + sq[:, atoms : 2 * atoms] + sq[:, 2 * atoms :]
    pre = hdot_t(mix_ref[0], a_sum) + hdot_t(mix_ref[1], h0_own) + hdot_t(mix_ref[2], q)
    pre_ref[...] = pre
    b_ref[...] = b_all
    s1 = pre * sigmoid(pre)
    v1 = hdot_t(vec_ref[...], b_all)
    lo_part = jnp.concatenate([s1, v1[:, :atoms]], axis=0)
    hi_part = jnp.concatenate([v1[:, atoms : 2 * atoms], v1[:, 2 * atoms :]], axis=0)
    feats_ref[0 : 2 * width] = lo_part
    feats_ref[2 * width :] = hi_part
    pack_halves(lo_part, hi_part, near_out, far_out)


def pack_halves(lo_part, hi_part, near_out, far_out):
    rows = lo_part.shape[0]
    low = lane_low(rows)
    odd = parity_odd(rows)
    lo_roll = roll64(lo_part)
    hi_roll = roll64(hi_part)
    low_lanes = jnp.where(low, lo_part, hi_roll)
    high_lanes = jnp.where(low, lo_roll, hi_part)
    near_out[...] = jnp.where(odd, low_lanes, high_lanes)
    far_out[...] = jnp.where(odd, high_lanes, low_lanes)


def radial_two_kernel(geom_ref, win_ref, wmid_ref, wout_ref, w_ref, dw_ref):
    n = geom_ref.shape[2]
    step = CHUNK * 128
    for j in range(n // step):
        lanes = pl.ds(j * step, step)
        w, dw = radial_pair(
            win_ref[1], wmid_ref[1], wout_ref[1], geom_ref[4, :, lanes], geom_ref[5, :, lanes]
        )
        w_ref[:, lanes] = w
        dw_ref[:, lanes] = dw


def edge_gradient(unit, inv, drho, du):
    dot = unit[0] * du[0] + unit[1] * du[1] + unit[2] * du[2]
    radial_part = drho - dot * inv
    return [unit[c] * radial_part + du[c] * inv for c in range(3)]


def sum_rows(x):
    return jnp.sum(x, axis=0, keepdims=True)


def position_rows(grads):
    g = jnp.concatenate([jnp.broadcast_to(x, (8, x.shape[1])) for x in grads], axis=0)
    x = jnp.concatenate([g[0:1], g[8:9], g[16:17], jnp.zeros((5, g.shape[1]), F32)], axis=0)
    h = high(x)
    return jnp.concatenate([h, x - h], axis=0).astype(BF16)


def layer_two_kernel(
    feats_ref,
    near_ref,
    far_ref,
    sel_ref,
    geom_ref,
    w_ref,
    dw_ref,
    mix_ref,
    read_ref,
    energy_ref,
    gown_ref,
    near_out,
    far_out,
    gpos_ref,
    far_scr,
    along_scr,
):
    atoms = feats_ref.shape[1]
    width = mix_ref.shape[1]
    slots = sel_ref.shape[1] // atoms
    rows = 2 * width
    low = lane_low(rows)
    odd = parity_odd(rows)
    near = near_ref[...]
    far = far_ref[...]
    upper = jnp.where(odd, far, near)
    lower = jnp.where(odd, near, far)
    g_lo = jnp.where(low, upper, roll64(lower))
    g_hi = jnp.where(low, roll64(upper), lower)
    feats = feats_ref[...]
    table = jnp.concatenate([feats, jnp.concatenate([g_lo, g_hi], axis=0)], axis=1)
    t_hi, t_lo = split_rows(table)
    tab = jnp.concatenate([t_hi, t_lo], axis=0)
    step = CHUNK * atoms
    m = jnp.zeros((width, atoms), F32)
    for j in range(slots // CHUNK):
        lanes = pl.ds(j * step, step)
        g = bdot(tab, sel_ref[:, lanes])
        f = g[: 4 * width] + g[4 * width :]
        far_scr[:, lanes] = f
        along = f[width : 2 * width] * tile8(geom_ref[0, :, lanes], width // 8)
        along = along + f[2 * width : 3 * width] * tile8(geom_ref[1, :, lanes], width // 8)
        along = along + f[3 * width :] * tile8(geom_ref[2, :, lanes], width // 8)
        along_scr[:, lanes] = along
        msg = w_ref[0:width, lanes] * f[:width] + w_ref[width : 2 * width, lanes] * along
        for k in range(CHUNK):
            m = m + msg[:, k * atoms : (k + 1) * atoms]
    scale = 1.0 / jnp.sqrt(F32(slots))
    s1 = feats[:width]
    pre = hdot_t(mix_ref[0], m * scale) + hdot_t(mix_ref[1], s1)
    sg = sigmoid(pre)
    s2 = pre * sg
    energy_ref[...] = hdot(read_ref[0:1], s1) + hdot(read_ref[1:2], s2)
    read = read_ref[...].T
    r_one = jnp.broadcast_to(read[:, 0:1], (width, atoms))
    r_two = jnp.broadcast_to(read[:, 1:2], (width, atoms))
    gpre = r_two * (sg + s2 * (1.0 - sg))
    gm = hdot(mix_ref[0], gpre) * scale
    gs_own = r_one + hdot(mix_ref[1], gpre)
    gm_rep = jnp.concatenate([gm] * CHUNK, axis=1)
    acc = jnp.zeros((8 * width + 16, 2 * atoms), F32)
    own_pos = [jnp.zeros((1, atoms), F32) for _ in range(3)]
    for j in range(slots // CHUNK):
        lanes = pl.ds(j * step, step)
        unit = [geom_ref[c, :, lanes] for c in range(3)]
        ga = w_ref[0:width, lanes] * gm_rep
        gb = w_ref[width : 2 * width, lanes] * gm_rep
        gv = [gb * tile8(unit[c], width // 8) for c in range(3)]
        drho = gm_rep * (
            dw_ref[0:width, lanes] * far_scr[0:width, lanes]
            + dw_ref[width : 2 * width, lanes] * along_scr[:, lanes]
        )
        du = [sum_rows(gb * far_scr[(c + 1) * width : (c + 2) * width, lanes]) for c in range(3)]
        gp = edge_gradient(
            [u[0:1] for u in unit], geom_ref[3, 0:1, lanes], sum_rows(drho), du
        )
        for k in range(CHUNK):
            for c in range(3):
                own_pos[c] = own_pos[c] + gp[c][:, k * atoms : (k + 1) * atoms]
        grads = jnp.concatenate([ga] + gv, axis=0)
        hi, lo = split_rows(grads)
        acc = acc + bdot_nt(
            jnp.concatenate([hi, lo, position_rows(gp)], axis=0), sel_ref[:, lanes]
        )
    grads = acc[: 4 * width] + acc[4 * width : 8 * width]
    own = grads[:, :atoms]
    gown_ref[0:width] = own[0:width] + gs_own
    gown_ref[width:] = own[width:]
    ghost = grads[:, atoms:]
    pack_halves_by_lane(ghost[: 2 * width], ghost[2 * width :], near_out, far_out)
    pos = acc[8 * width : 8 * width + 8] + acc[8 * width + 8 :]
    centre = jnp.concatenate(own_pos + [jnp.zeros((5, atoms), F32)], axis=0)
    gpos_ref[:, :atoms] = pos[:, :atoms] - centre
    gpos_ref[:, atoms:] = pos[:, atoms:]


def pack_halves_by_lane(lo_part, hi_part, near_out, far_out):
    rows = lo_part.shape[0]
    low = lane_low(rows)
    odd = parity_odd(rows)
    to_upper = jnp.where(low, lo_part, roll64(hi_part))
    to_lower = jnp.where(low, roll64(lo_part), hi_part)
    near_out[...] = jnp.where(odd, to_lower, to_upper)
    far_out[...] = jnp.where(odd, to_upper, to_lower)


def tangent_one_kernel(geom_ref, hfar_ref, win_ref, wmid_ref, wout_ref, out_ref):
    n = geom_ref.shape[2]
    width = hfar_ref.shape[0]
    step = CHUNK * 128
    for j in range(n // step):
        lanes = pl.ds(j * step, step)
        w, dw = radial_pair(
            win_ref[0], wmid_ref[0], wout_ref[0], geom_ref[4, :, lanes], geom_ref[5, :, lanes]
        )
        h = hfar_ref[:, lanes]
        out_ref[0:width, lanes] = dw[:width] * h
        out_ref[width : 2 * width, lanes] = dw[width:] * h
        out_ref[2 * width :, lanes] = w[width:] * h


def back_one_kernel(
    gown_ref,
    near_ref,
    far_ref,
    sel_ref,
    geom_ref,
    edge_ref,
    pre_ref,
    b_ref,
    mix_ref,
    vec_ref,
    gpos_in,
    gown_out,
    ghost_out,
):
    atoms = gown_ref.shape[1]
    width = mix_ref.shape[1]
    slots = sel_ref.shape[1] // atoms
    rows = 2 * width
    low = lane_low(rows)
    odd = parity_odd(rows)
    near = near_ref[...]
    far = far_ref[...]
    upper = jnp.where(odd, far, near)
    lower = jnp.where(odd, near, far)
    g_lo = gown_ref[0:rows] + jnp.where(low, lower, roll64(upper))
    g_hi = gown_ref[rows:] + jnp.where(low, roll64(lower), upper)
    scale = 1.0 / jnp.sqrt(F32(slots))
    pre = pre_ref[...]
    sg = sigmoid(pre)
    gpre = g_lo[:width] * (sg + pre * sg * (1.0 - sg))
    ga = hdot(mix_ref[0], gpre) * scale
    gq = hdot(mix_ref[2], gpre)
    gv = jnp.concatenate([g_lo[width:], g_hi[:width], g_hi[width:]], axis=1)
    gb_all = hdot(vec_ref[...], gv) + 2.0 * b_ref[...] * jnp.concatenate([gq] * 3, axis=1)
    gb = [gb_all[:, c * atoms : (c + 1) * atoms] * scale for c in range(3)]
    ga_rep = jnp.concatenate([ga] * CHUNK, axis=1)
    gb_rep = [jnp.concatenate([g] * CHUNK, axis=1) for g in gb]
    step = CHUNK * atoms
    acc = jnp.zeros((16, 2 * atoms), F32)
    own_pos = [jnp.zeros((1, atoms), F32) for _ in range(3)]
    for j in range(slots // CHUNK):
        lanes = pl.ds(j * step, step)
        unit = [geom_ref[c, :, lanes] for c in range(3)]
        gbu = gb_rep[0] * tile8(unit[0], width // 8)
        gbu = gbu + gb_rep[1] * tile8(unit[1], width // 8)
        gbu = gbu + gb_rep[2] * tile8(unit[2], width // 8)
        drho = edge_ref[0:width, lanes] * ga_rep + edge_ref[width : 2 * width, lanes] * gbu
        carried = edge_ref[2 * width :, lanes]
        du = [sum_rows(carried * gb_rep[c]) for c in range(3)]
        gp = edge_gradient(
            [u[0:1] for u in unit], geom_ref[3, 0:1, lanes], sum_rows(drho), du
        )
        for k in range(CHUNK):
            for c in range(3):
                own_pos[c] = own_pos[c] + gp[c][:, k * atoms : (k + 1) * atoms]
        acc = acc + bdot_nt(position_rows(gp), sel_ref[:, lanes])
    pos = acc[0:8] + acc[8:16] + gpos_in[...]
    centre = jnp.concatenate(own_pos + [jnp.zeros((5, atoms), F32)], axis=0)
    gown_out[...] = pos[:, :atoms] - centre
    ghost_out[...] = pos[:, atoms:]


def call(kernel, out_shapes, args, scratch=(), flops=0, transcendentals=0, space=pltpu.VMEM):
    if space is pltpu.HBM:
        args = [pltpu.with_memory_space_constraint(x, pltpu.HBM) for x in args]
    moved = sum(x.size * x.dtype.itemsize for x in list(args) + list(out_shapes))
    return pl.pallas_call(
        kernel,
        out_shape=out_shapes,
        in_specs=[pl.BlockSpec(memory_space=space)] * len(args),
        out_specs=[pl.BlockSpec(memory_space=pltpu.VMEM)] * len(out_shapes),
        scratch_shapes=list(scratch),
        cost_estimate=pl.CostEstimate(
            flops=flops, bytes_accessed=moved, transcendentals=transcendentals
        ),
        compiler_params=pltpu.CompilerParams(vmem_limit_bytes=48 * MIB),
    )(*args)


def shape(dims, dtype=F32):
    return jax.ShapeDtypeStruct(dims, dtype)


def body(
    positions,
    species,
    neighbours,
    counts,
    ghost_index,
    embed,
    radial_in,
    radial_mid,
    radial_out,
    mix_one,
    vec_mix,
    mix_two,
    readout,
):
    atoms = positions.shape[1]
    slots = neighbours.shape[0]
    edges = slots * atoms
    nbasis, hidden = radial_in.shape[1:]
    width = embed.shape[1]
    devices = lax.axis_size("space")
    near_route = [(i, i ^ 1) for i in range(devices)]
    far_route = [(i, ((i + 1) ^ 1) - 1) for i in range(1, devices - 1)]

    def swap_near(x):
        return lax.ppermute(x, "space", near_route)

    def swap_far(x):
        return lax.ppermute(x, "space", far_route)

    own = call(
        pack_kernel,
        [shape((4, atoms))],
        [positions, species[None]],
        scratch=[
            pltpu.VMEM((3, atoms), F32),
            pltpu.VMEM((1, atoms), jnp.int32),
            pltpu.SemaphoreType.DMA((2,)),
        ],
        space=pltpu.HBM,
    )[0]
    near = swap_near(own)
    far = swap_far(own)
    weights = [radial_in, radial_mid, radial_out]
    passed = [counts[None], embed, mix_one, vec_mix, mix_two, readout]
    moved = [neighbours, ghost_index] + weights + passed
    sel, win, wmid, wout, counts, embed, mix_one, vec_mix, mix_two, readout = call(
        prep_kernel,
        [
            shape((2 * atoms, edges), BF16),
            shape((2, hidden, 4 * nbasis), BF16),
            shape((2, hidden, 3 * hidden), BF16),
            shape((2, 2 * width, 3 * hidden), BF16),
        ]
        + [shape(x.shape, x.dtype) for x in passed],
        moved,
        scratch=[pltpu.VMEM(x.shape, x.dtype) for x in [neighbours, ghost_index] + weights]
        + [pltpu.SemaphoreType.DMA((len(moved),))],
        flops=10**8,
        space=pltpu.HBM,
    )
    feats, near_f, far_f, geom, pre, b_all, h_far = call(
        layer_one_kernel,
        [
            shape((4 * width, atoms)),
            shape((2 * width, atoms)),
            shape((2 * width, atoms)),
            shape((6, 8, edges)),
            shape((width, atoms)),
            shape((width, 3 * atoms)),
            shape((width, edges)),
        ],
        [own, near, far, sel, counts, embed, win, wmid, wout, mix_one, vec_mix],
        scratch=[pltpu.VMEM((72 + 2 * width, 2 * atoms), F32)],
        flops=10**9,
    )
    near_f = swap_near(near_f)
    far_f = swap_far(far_f)
    w, dw = call(
        radial_two_kernel,
        [shape((2 * width, edges)), shape((2 * width, edges))],
        [geom, win, wmid, wout],
        flops=2 * 10**9,
    )
    energy, g_own, near_g, far_g, gpos = call(
        layer_two_kernel,
        [
            shape((1, atoms)),
            shape((4 * width, atoms)),
            shape((2 * width, atoms)),
            shape((2 * width, atoms)),
            shape((8, 2 * atoms)),
        ],
        [feats, near_f, far_f, sel, geom, w, dw, mix_two, readout],
        scratch=[pltpu.VMEM((4 * width, edges), F32), pltpu.VMEM((width, edges), F32)],
        flops=10**9,
    )
    near_g = swap_near(near_g)
    far_g = swap_far(far_g)
    (edge,) = call(
        tangent_one_kernel,
        [shape((3 * width, edges))],
        [geom, h_far, win, wmid, wout],
        flops=2 * 10**9,
    )
    g_centre, ghost = call(
        back_one_kernel,
        [shape((8, atoms)), shape((8, atoms))],
        [g_own, near_g, far_g, sel, geom, edge, pre, b_all, mix_one, vec_mix, gpos],
        flops=10**9,
    )
    near_p = swap_near(ghost)
    far_p = swap_far(ghost)
    odd = lax.rem(lax.axis_index("space"), 2) == 1
    low = lax.broadcasted_iota(jnp.int32, (3, atoms), 1) < HALF
    come = jnp.where(low == odd, near_p[:3], far_p[:3])
    return (energy[0], -(g_centre[:3] + come))


def solution(mesh):
    placed = (
        P(None, "space"),
        P("space"),
        P(None, "space"),
        P("space"),
        P(None, "space"),
        P(),
        P(),
        P(),
        P(),
        P(),
        P(),
        P(),
        P(),
    )
    return jax.shard_map(
        body, mesh=mesh, in_specs=placed, out_specs=(P("space"), P(None, "space")), check_vma=False
    )
```

```python
import functools

import jax
import jax.numpy as jnp
from jax import lax
from jax.experimental import pallas as pl
from jax.experimental.pallas import tpu as pltpu
from jax.sharding import PartitionSpec as P

RADIUS = 5.0
SOFTEN = 0.25
F32 = jnp.float32
BF16 = jnp.bfloat16
HALF = 64
CHUNK = 24
MIB = 1024 * 1024


def hdot(a, b, dims=(((1,), (0,)), ((), ()))):
    return lax.dot_general(
        a, b, dims, precision=lax.Precision.HIGHEST, preferred_element_type=F32
    )


def hdot_t(a, b):
    return hdot(a, b, (((0,), (0,)), ((), ())))


def bdot(a, b):
    return jnp.dot(a, b, preferred_element_type=F32)


def bdot_nt(a, b):
    return lax.dot_general(a, b, (((1,), (1,)), ((), ())), preferred_element_type=F32)


def high(x):
    return x.astype(BF16).astype(F32)


def split_rows(x):
    hi = x.astype(BF16)
    lo = (x - hi.astype(F32)).astype(BF16)
    return hi, lo


def stack3(x):
    hi, lo = split_rows(x)
    return jnp.concatenate([hi, lo, hi], axis=0)


def sigmoid(v):
    return 0.5 + 0.5 * jnp.tanh(0.5 * v)


def roll64(x):
    return pltpu.roll(x, HALF, 1)


def lane_low(rows):
    return lax.broadcasted_iota(jnp.int32, (rows, 128), 1) < HALF


def parity_odd(rows):
    odd = lax.rem(lax.axis_index("space"), 2)
    return jnp.full((rows, 128), odd, jnp.int32) > 0


def pack_kernel(pos_hbm, kind_hbm, own_ref, pos_ref, kind_ref, sems):
    copies = [
        pltpu.make_async_copy(pos_hbm, pos_ref, sems.at[0]),
        pltpu.make_async_copy(kind_hbm, kind_ref, sems.at[1]),
    ]
    for c in copies:
        c.start()
    for c in copies:
        c.wait()
    own_ref[0:3, :] = pos_ref[...]
    own_ref[3:4, :] = (kind_ref[...] + 1).astype(F32)


def prep_kernel(
    nb_hbm,
    gi_hbm,
    rin_hbm,
    rmid_hbm,
    rout_hbm,
    counts_hbm,
    embed_hbm,
    mix_one_hbm,
    vec_hbm,
    mix_two_hbm,
    read_hbm,
    sel_ref,
    win_ref,
    wmid_ref,
    wout_ref,
    counts_ref,
    embed_ref,
    mix_one_ref,
    vec_ref,
    mix_two_ref,
    read_ref,
    nb_ref,
    gi_ref,
    rin_ref,
    rmid_ref,
    rout_ref,
    sems,
):
    moves = [
        (nb_hbm, nb_ref),
        (gi_hbm, gi_ref),
        (rin_hbm, rin_ref),
        (rmid_hbm, rmid_ref),
        (rout_hbm, rout_ref),
        (counts_hbm, counts_ref),
        (embed_hbm, embed_ref),
        (mix_one_hbm, mix_one_ref),
        (vec_hbm, vec_ref),
        (mix_two_hbm, mix_two_ref),
        (read_hbm, read_ref),
    ]
    copies = [
        pltpu.make_async_copy(src, dst, sems.at[i]) for i, (src, dst) in enumerate(moves)
    ]
    for c in copies:
        c.start()
    for c in copies:
        c.wait()
    atoms = nb_ref.shape[1]
    slots = nb_ref.shape[0]
    rows = lax.broadcasted_iota(jnp.int32, (atoms, atoms), 0)
    half_rows = lax.broadcasted_iota(jnp.int32, (atoms, HALF), 0)
    perm = jnp.concatenate(
        [
            (half_rows == jnp.broadcast_to(gi_ref[i : i + 1, :], (atoms, HALF))).astype(F32)
            for i in range(2)
        ],
        axis=1,
    ).astype(BF16)
    for k in range(slots):
        nb = jnp.broadcast_to(nb_ref[k : k + 1, :], (atoms, atoms))
        lanes = pl.ds(k * atoms, atoms)
        sel_ref[0:atoms, lanes] = (rows == nb).astype(F32).astype(BF16)
        ghost = (rows + atoms == nb).astype(F32).astype(BF16)
        sel_ref[atoms : 2 * atoms, lanes] = bdot(perm, ghost).astype(BF16)
    for layer in range(2):
        w = rin_ref[layer]
        h = high(w)
        lo = w - h
        win_ref[layer] = jnp.concatenate([h, h, lo, lo], axis=0).T.astype(BF16)
        w = rmid_ref[layer]
        h = high(w)
        wmid_ref[layer] = jnp.concatenate([h, h, w - h], axis=0).T.astype(BF16)
        w = rout_ref[layer]
        h = high(w)
        wout_ref[layer] = jnp.concatenate([h, h, w - h], axis=0).T.astype(BF16)


def basis_rows(b):
    h = high(b)
    lo = b - h
    return jnp.concatenate([h, lo, h, lo], axis=0).astype(BF16)


def radial(win, wmid, wout, b):
    v1 = bdot(win, basis_rows(b))
    z1 = v1 * sigmoid(v1)
    v2 = bdot(wmid, stack3(z1))
    z2 = v2 * sigmoid(v2)
    return bdot(wout, stack3(z2))


def silu_pair(v, t):
    s = sigmoid(v)
    z = v * s
    return z, (s + z * (1.0 - s)) * t


def radial_pair(win, wmid, wout, b, db):
    z1, t1 = silu_pair(bdot(win, basis_rows(b)), bdot(win, basis_rows(db)))
    z2, t2 = silu_pair(bdot(wmid, stack3(z1)), bdot(wmid, stack3(t1)))
    return bdot(wout, stack3(z2)), bdot(wout, stack3(t2))


def tile8(x, times):
    return jnp.concatenate([x] * times, axis=0)


def geometry(far, own, valid):
    vec = [f - o for f, o in zip(far, own)]
    r2 = vec[0] * vec[0] + vec[1] * vec[1] + vec[2] * vec[2] + SOFTEN
    inv = lax.rsqrt(r2)
    inv = inv * (1.5 - 0.5 * r2 * inv * inv)
    rho = r2 * inv
    unit = [v * inv for v in vec]
    x = jnp.minimum(rho * (1.0 / RADIUS), 1.0)
    y = 1.0 - x
    x2 = x * x
    env = y * y * y * (1.0 + x * (3.0 + x * (6.0 + x * (10.0 + x * 15.0))))
    denv = (-105.0 / RADIUS) * x2 * x2 * y * y
    f = RADIUS * inv * env * valid
    df = RADIUS * inv * (denv - env * inv) * valid
    n = (lax.broadcasted_iota(jnp.int32, rho.shape, 0) + 1).astype(F32)
    turns = n * x
    whole = jnp.floor(turns + 0.5)
    frac = (turns - whole) * jnp.pi
    parity = whole - 2.0 * jnp.floor(0.5 * whole)
    sign = 1.0 - 2.0 * parity
    q = frac * frac
    sin = frac * (
        1.0
        + q * (-1 / 6 + q * (1 / 120 + q * (-1 / 5040 + q * (1 / 362880 + q * (-1 / 39916800)))))
    )
    cos = 1.0 + q * (
        -1 / 2
        + q * (1 / 24 + q * (-1 / 720 + q * (1 / 40320 + q * (-1 / 3628800 + q * (1 / 479001600)))))
    )
    sin = sin * sign
    cos = cos * sign
    return unit, inv, sin * f, sin * df + (n * (jnp.pi / RADIUS)) * cos * f


def layer_one_kernel(
    own_ref,
    near_ref,
    far_ref,
    sel_ref,
    counts_ref,
    embed_ref,
    win_ref,
    wmid_ref,
    wout_ref,
    mix_ref,
    vec_ref,
    feats_ref,
    near_out,
    far_out,
    geom_ref,
    pre_ref,
    b_ref,
    hfar_ref,
    tab_ref,
):
    atoms = own_ref.shape[1]
    slots = counts_ref.shape[0] and sel_ref.shape[1] // atoms
    width = embed_ref.shape[1]
    species = embed_ref.shape[0]
    odd4 = parity_odd(4)
    low4 = lane_low(4)
    own = own_ref[...]
    from_far = jnp.logical_xor(odd4, jnp.logical_not(low4))
    ghost = jnp.where(from_far, far_ref[...], near_ref[...])
    table = jnp.concatenate([own, ghost], axis=1)
    for c in range(3):
        p = jnp.broadcast_to(table[c : c + 1], (8, 2 * atoms))
        h = p.astype(BF16)
        rest = p - h.astype(F32)
        m = rest.astype(BF16)
        lo = (rest - m.astype(F32)).astype(BF16)
        part = jnp.concatenate([h.astype(F32), m.astype(F32), lo.astype(F32)], axis=0)
        tab_ref[c * 24 : c * 24 + 24, :] = part
    kind = jnp.broadcast_to(table[3:4], (species, 2 * atoms))
    onehot = (
        kind == (lax.broadcasted_iota(jnp.int32, (species, 2 * atoms), 0) + 1).astype(F32)
    ).astype(F32)
    h0 = hdot_t(embed_ref[...], onehot)
    h0_hi = high(h0)
    tab_ref[72 : 72 + width, :] = h0_hi
    tab_ref[72 + width : 72 + 2 * width, :] = h0 - h0_hi
    tab = tab_ref[...].astype(BF16)
    h0_own = h0[:, :atoms]

    step = CHUNK * atoms
    own_rep = [
        jnp.concatenate([jnp.broadcast_to(own[c : c + 1], (8, atoms))] * CHUNK, axis=1)
        for c in range(3)
    ]
    counts = jnp.broadcast_to(counts_ref[...], (8, atoms))
    a_sum = jnp.zeros((width, atoms), F32)
    b_sum = [jnp.zeros((width, atoms), F32) for _ in range(3)]
    for j in range(slots // CHUNK):
        lanes = pl.ds(j * step, step)
        g = bdot(tab, sel_ref[:, lanes])
        far = [g[24 * c : 24 * c + 8] + g[24 * c + 8 : 24 * c + 16] + g[24 * c + 16 : 24 * c + 24] for c in range(3)]
        h_far = g[72 : 72 + width] + g[72 + width : 72 + 2 * width]
        hfar_ref[:, lanes] = h_far
        valid = jnp.concatenate(
            [(counts > (j * CHUNK + k)).astype(F32) for k in range(CHUNK)], axis=1
        )
        unit, inv, b, db = geometry(far, own_rep, valid)
        for c in range(3):
            geom_ref[c, :, lanes] = unit[c]
        geom_ref[3, :, lanes] = inv
        geom_ref[4, :, lanes] = b
        geom_ref[5, :, lanes] = db
        w = radial(win_ref[0], wmid_ref[0], wout_ref[0], b)
        wa = w[:width] * h_far
        wb = w[width:] * h_far
        for k in range(CHUNK):
            s = slice(k * atoms, (k + 1) * atoms)
            a_sum = a_sum + wa[:, s]
            for c in range(3):
                b_sum[c] = b_sum[c] + wb[:, s] * tile8(unit[c][:, s], width // 8)
    scale = 1.0 / jnp.sqrt(F32(slots))
    a_sum = a_sum * scale
    b_all = jnp.concatenate([x * scale for x in b_sum], axis=1)
    sq = b_all * b_all
    q = sq[:, :atoms] + sq[:, atoms : 2 * atoms] + sq[:, 2 * atoms :]
    pre = hdot_t(mix_ref[0], a_sum) + hdot_t(mix_ref[1], h0_own) + hdot_t(mix_ref[2], q)
    pre_ref[...] = pre
    b_ref[...] = b_all
    s1 = pre * sigmoid(pre)
    v1 = hdot_t(vec_ref[...], b_all)
    lo_part = jnp.concatenate([s1, v1[:, :atoms]], axis=0)
    hi_part = jnp.concatenate([v1[:, atoms : 2 * atoms], v1[:, 2 * atoms :]], axis=0)
    feats_ref[0 : 2 * width] = lo_part
    feats_ref[2 * width :] = hi_part
    pack_halves(lo_part, hi_part, near_out, far_out)


def pack_halves(lo_part, hi_part, near_out, far_out):
    rows = lo_part.shape[0]
    low = lane_low(rows)
    odd = parity_odd(rows)
    lo_roll = roll64(lo_part)
    hi_roll = roll64(hi_part)
    low_lanes = jnp.where(low, lo_part, hi_roll)
    high_lanes = jnp.where(low, lo_roll, hi_part)
    near_out[...] = jnp.where(odd, low_lanes, high_lanes)
    far_out[...] = jnp.where(odd, high_lanes, low_lanes)


def radial_two_kernel(geom_ref, win_ref, wmid_ref, wout_ref, w_ref, dw_ref):
    n = geom_ref.shape[2]
    step = CHUNK * 128
    for j in range(n // step):
        lanes = pl.ds(j * step, step)
        w, dw = radial_pair(
            win_ref[1], wmid_ref[1], wout_ref[1], geom_ref[4, :, lanes], geom_ref[5, :, lanes]
        )
        w_ref[:, lanes] = w
        dw_ref[:, lanes] = dw


def edge_gradient(unit, inv, drho, du):
    dot = unit[0] * du[0] + unit[1] * du[1] + unit[2] * du[2]
    radial_part = drho - dot * inv
    return [unit[c] * radial_part + du[c] * inv for c in range(3)]


def sum_rows(x):
    return jnp.sum(x, axis=0, keepdims=True)


def position_rows(grads):
    g = jnp.concatenate([jnp.broadcast_to(x, (8, x.shape[1])) for x in grads], axis=0)
    x = jnp.concatenate([g[0:1], g[8:9], g[16:17], jnp.zeros((5, g.shape[1]), F32)], axis=0)
    h = high(x)
    return jnp.concatenate([h, x - h], axis=0).astype(BF16)


def layer_two_kernel(
    feats_ref,
    near_ref,
    far_ref,
    sel_ref,
    geom_ref,
    w_ref,
    dw_ref,
    mix_ref,
    read_ref,
    energy_ref,
    gown_ref,
    near_out,
    far_out,
    gpos_ref,
    far_scr,
    along_scr,
):
    atoms = feats_ref.shape[1]
    width = mix_ref.shape[1]
    slots = sel_ref.shape[1] // atoms
    rows = 2 * width
    low = lane_low(rows)
    odd = parity_odd(rows)
    near = near_ref[...]
    far = far_ref[...]
    upper = jnp.where(odd, far, near)
    lower = jnp.where(odd, near, far)
    g_lo = jnp.where(low, upper, roll64(lower))
    g_hi = jnp.where(low, roll64(upper), lower)
    feats = feats_ref[...]
    table = jnp.concatenate([feats, jnp.concatenate([g_lo, g_hi], axis=0)], axis=1)
    t_hi, t_lo = split_rows(table)
    tab = jnp.concatenate([t_hi, t_lo], axis=0)
    step = CHUNK * atoms
    m = jnp.zeros((width, atoms), F32)
    for j in range(slots // CHUNK):
        lanes = pl.ds(j * step, step)
        g = bdot(tab, sel_ref[:, lanes])
        f = g[: 4 * width] + g[4 * width :]
        far_scr[:, lanes] = f
        along = f[width : 2 * width] * tile8(geom_ref[0, :, lanes], width // 8)
        along = along + f[2 * width : 3 * width] * tile8(geom_ref[1, :, lanes], width // 8)
        along = along + f[3 * width :] * tile8(geom_ref[2, :, lanes], width // 8)
        along_scr[:, lanes] = along
        msg = w_ref[0:width, lanes] * f[:width] + w_ref[width : 2 * width, lanes] * along
        for k in range(CHUNK):
            m = m + msg[:, k * atoms : (k + 1) * atoms]
    scale = 1.0 / jnp.sqrt(F32(slots))
    s1 = feats[:width]
    pre = hdot_t(mix_ref[0], m * scale) + hdot_t(mix_ref[1], s1)
    sg = sigmoid(pre)
    s2 = pre * sg
    energy_ref[...] = hdot(read_ref[0:1], s1) + hdot(read_ref[1:2], s2)
    read = read_ref[...].T
    r_one = jnp.broadcast_to(read[:, 0:1], (width, atoms))
    r_two = jnp.broadcast_to(read[:, 1:2], (width, atoms))
    gpre = r_two * (sg + s2 * (1.0 - sg))
    gm = hdot(mix_ref[0], gpre) * scale
    gs_own = r_one + hdot(mix_ref[1], gpre)
    gm_rep = jnp.concatenate([gm] * CHUNK, axis=1)
    acc = jnp.zeros((8 * width + 16, 2 * atoms), F32)
    own_pos = [jnp.zeros((1, atoms), F32) for _ in range(3)]
    for j in range(slots // CHUNK):
        lanes = pl.ds(j * step, step)
        unit = [geom_ref[c, :, lanes] for c in range(3)]
        ga = w_ref[0:width, lanes] * gm_rep
        gb = w_ref[width : 2 * width, lanes] * gm_rep
        gv = [gb * tile8(unit[c], width // 8) for c in range(3)]
        drho = gm_rep * (
            dw_ref[0:width, lanes] * far_scr[0:width, lanes]
            + dw_ref[width : 2 * width, lanes] * along_scr[:, lanes]
        )
        du = [sum_rows(gb * far_scr[(c + 1) * width : (c + 2) * width, lanes]) for c in range(3)]
        gp = edge_gradient(
            [u[0:1] for u in unit], geom_ref[3, 0:1, lanes], sum_rows(drho), du
        )
        for k in range(CHUNK):
            for c in range(3):
                own_pos[c] = own_pos[c] + gp[c][:, k * atoms : (k + 1) * atoms]
        grads = jnp.concatenate([ga] + gv, axis=0)
        hi, lo = split_rows(grads)
        acc = acc + bdot_nt(
            jnp.concatenate([hi, lo, position_rows(gp)], axis=0), sel_ref[:, lanes]
        )
    grads = acc[: 4 * width] + acc[4 * width : 8 * width]
    own = grads[:, :atoms]
    gown_ref[0:width] = own[0:width] + gs_own
    gown_ref[width:] = own[width:]
    ghost = grads[:, atoms:]
    pack_halves_by_lane(ghost[: 2 * width], ghost[2 * width :], near_out, far_out)
    pos = acc[8 * width : 8 * width + 8] + acc[8 * width + 8 :]
    centre = jnp.concatenate(own_pos + [jnp.zeros((5, atoms), F32)], axis=0)
    gpos_ref[:, :atoms] = pos[:, :atoms] - centre
    gpos_ref[:, atoms:] = pos[:, atoms:]


def pack_halves_by_lane(lo_part, hi_part, near_out, far_out):
    rows = lo_part.shape[0]
    low = lane_low(rows)
    odd = parity_odd(rows)
    to_upper = jnp.where(low, lo_part, roll64(hi_part))
    to_lower = jnp.where(low, roll64(lo_part), hi_part)
    near_out[...] = jnp.where(odd, to_lower, to_upper)
    far_out[...] = jnp.where(odd, to_upper, to_lower)


def tangent_one_kernel(geom_ref, hfar_ref, win_ref, wmid_ref, wout_ref, out_ref):
    n = geom_ref.shape[2]
    width = hfar_ref.shape[0]
    step = CHUNK * 128
    for j in range(n // step):
        lanes = pl.ds(j * step, step)
        w, dw = radial_pair(
            win_ref[0], wmid_ref[0], wout_ref[0], geom_ref[4, :, lanes], geom_ref[5, :, lanes]
        )
        h = hfar_ref[:, lanes]
        out_ref[0:width, lanes] = dw[:width] * h
        out_ref[width : 2 * width, lanes] = dw[width:] * h
        out_ref[2 * width :, lanes] = w[width:] * h


def back_one_kernel(
    gown_ref,
    near_ref,
    far_ref,
    sel_ref,
    geom_ref,
    edge_ref,
    pre_ref,
    b_ref,
    mix_ref,
    vec_ref,
    gpos_in,
    gown_out,
    ghost_out,
):
    atoms = gown_ref.shape[1]
    width = mix_ref.shape[1]
    slots = sel_ref.shape[1] // atoms
    rows = 2 * width
    low = lane_low(rows)
    odd = parity_odd(rows)
    near = near_ref[...]
    far = far_ref[...]
    upper = jnp.where(odd, far, near)
    lower = jnp.where(odd, near, far)
    g_lo = gown_ref[0:rows] + jnp.where(low, lower, roll64(upper))
    g_hi = gown_ref[rows:] + jnp.where(low, roll64(lower), upper)
    scale = 1.0 / jnp.sqrt(F32(slots))
    pre = pre_ref[...]
    sg = sigmoid(pre)
    gpre = g_lo[:width] * (sg + pre * sg * (1.0 - sg))
    ga = hdot(mix_ref[0], gpre) * scale
    gq = hdot(mix_ref[2], gpre)
    gv = jnp.concatenate([g_lo[width:], g_hi[:width], g_hi[width:]], axis=1)
    gb_all = hdot(vec_ref[...], gv) + 2.0 * b_ref[...] * jnp.concatenate([gq] * 3, axis=1)
    gb = [gb_all[:, c * atoms : (c + 1) * atoms] * scale for c in range(3)]
    ga_rep = jnp.concatenate([ga] * CHUNK, axis=1)
    gb_rep = [jnp.concatenate([g] * CHUNK, axis=1) for g in gb]
    step = CHUNK * atoms
    acc = jnp.zeros((16, 2 * atoms), F32)
    own_pos = [jnp.zeros((1, atoms), F32) for _ in range(3)]
    for j in range(slots // CHUNK):
        lanes = pl.ds(j * step, step)
        unit = [geom_ref[c, :, lanes] for c in range(3)]
        gbu = gb_rep[0] * tile8(unit[0], width // 8)
        gbu = gbu + gb_rep[1] * tile8(unit[1], width // 8)
        gbu = gbu + gb_rep[2] * tile8(unit[2], width // 8)
        drho = edge_ref[0:width, lanes] * ga_rep + edge_ref[width : 2 * width, lanes] * gbu
        carried = edge_ref[2 * width :, lanes]
        du = [sum_rows(carried * gb_rep[c]) for c in range(3)]
        gp = edge_gradient(
            [u[0:1] for u in unit], geom_ref[3, 0:1, lanes], sum_rows(drho), du
        )
        for k in range(CHUNK):
            for c in range(3):
                own_pos[c] = own_pos[c] + gp[c][:, k * atoms : (k + 1) * atoms]
        acc = acc + bdot_nt(position_rows(gp), sel_ref[:, lanes])
    pos = acc[0:8] + acc[8:16] + gpos_in[...]
    centre = jnp.concatenate(own_pos + [jnp.zeros((5, atoms), F32)], axis=0)
    gown_out[...] = pos[:, :atoms] - centre
    ghost_out[...] = pos[:, atoms:]


def call(kernel, out_shapes, args, scratch=(), flops=0, transcendentals=0, space=pltpu.VMEM):
    if space is pltpu.HBM:
        args = [pltpu.with_memory_space_constraint(x, pltpu.HBM) for x in args]
    moved = sum(x.size * x.dtype.itemsize for x in list(args) + list(out_shapes))
    return pl.pallas_call(
        kernel,
        out_shape=out_shapes,
        in_specs=[pl.BlockSpec(memory_space=space)] * len(args),
        out_specs=[pl.BlockSpec(memory_space=pltpu.VMEM)] * len(out_shapes),
        scratch_shapes=list(scratch),
        cost_estimate=pl.CostEstimate(
            flops=flops, bytes_accessed=moved, transcendentals=transcendentals
        ),
        compiler_params=pltpu.CompilerParams(vmem_limit_bytes=48 * MIB),
    )(*args)


def shape(dims, dtype=F32):
    return jax.ShapeDtypeStruct(dims, dtype)


def body(
    positions,
    species,
    neighbours,
    counts,
    ghost_index,
    embed,
    radial_in,
    radial_mid,
    radial_out,
    mix_one,
    vec_mix,
    mix_two,
    readout,
):
    atoms = positions.shape[1]
    slots = neighbours.shape[0]
    edges = slots * atoms
    nbasis, hidden = radial_in.shape[1:]
    width = embed.shape[1]
    devices = lax.axis_size("space")
    near_route = [(i, i ^ 1) for i in range(devices)]
    far_route = [(i, ((i + 1) ^ 1) - 1) for i in range(1, devices - 1)]

    def swap_near(x):
        return lax.ppermute(x, "space", near_route)

    def swap_far(x):
        return lax.ppermute(x, "space", far_route)

    own = call(
        pack_kernel,
        [shape((4, atoms))],
        [positions, species[None]],
        scratch=[
            pltpu.VMEM((3, atoms), F32),
            pltpu.VMEM((1, atoms), jnp.int32),
            pltpu.SemaphoreType.DMA((2,)),
        ],
        space=pltpu.HBM,
    )[0]
    near = swap_near(own)
    far = swap_far(own)
    weights = [radial_in, radial_mid, radial_out]
    passed = [counts[None], embed, mix_one, vec_mix, mix_two, readout]
    moved = [neighbours, ghost_index] + weights + passed
    sel, win, wmid, wout, counts, embed, mix_one, vec_mix, mix_two, readout = call(
        prep_kernel,
        [
            shape((2 * atoms, edges), BF16),
            shape((2, hidden, 4 * nbasis), BF16),
            shape((2, hidden, 3 * hidden), BF16),
            shape((2, 2 * width, 3 * hidden), BF16),
        ]
        + [shape(x.shape, x.dtype) for x in passed],
        moved,
        scratch=[pltpu.VMEM(x.shape, x.dtype) for x in [neighbours, ghost_index] + weights]
        + [pltpu.SemaphoreType.DMA((len(moved),))],
        flops=10**8,
        space=pltpu.HBM,
    )
    feats, near_f, far_f, geom, pre, b_all, h_far = call(
        layer_one_kernel,
        [
            shape((4 * width, atoms)),
            shape((2 * width, atoms)),
            shape((2 * width, atoms)),
            shape((6, 8, edges)),
            shape((width, atoms)),
            shape((width, 3 * atoms)),
            shape((width, edges)),
        ],
        [own, near, far, sel, counts, embed, win, wmid, wout, mix_one, vec_mix],
        scratch=[pltpu.VMEM((72 + 2 * width, 2 * atoms), F32)],
        flops=10**9,
    )
    near_f = swap_near(near_f)
    far_f = swap_far(far_f)
    w, dw = call(
        radial_two_kernel,
        [shape((2 * width, edges)), shape((2 * width, edges))],
        [geom, win, wmid, wout],
        flops=2 * 10**9,
    )
    energy, g_own, near_g, far_g, gpos = call(
        layer_two_kernel,
        [
            shape((1, atoms)),
            shape((4 * width, atoms)),
            shape((2 * width, atoms)),
            shape((2 * width, atoms)),
            shape((8, 2 * atoms)),
        ],
        [feats, near_f, far_f, sel, geom, w, dw, mix_two, readout],
        scratch=[pltpu.VMEM((4 * width, edges), F32), pltpu.VMEM((width, edges), F32)],
        flops=10**9,
    )
    near_g = swap_near(near_g)
    far_g = swap_far(far_g)
    (edge,) = call(
        tangent_one_kernel,
        [shape((3 * width, edges))],
        [geom, h_far, win, wmid, wout],
        flops=2 * 10**9,
    )
    g_centre, ghost = call(
        back_one_kernel,
        [shape((8, atoms)), shape((8, atoms))],
        [g_own, near_g, far_g, sel, geom, edge, pre, b_all, mix_one, vec_mix, gpos],
        flops=10**9,
    )
    near_p = swap_near(ghost)
    far_p = swap_far(ghost)
    odd = lax.rem(lax.axis_index("space"), 2) == 1
    low = lax.broadcasted_iota(jnp.int32, (3, atoms), 1) < HALF
    come = jnp.where(low == odd, near_p[:3], far_p[:3])
    return (energy[0], -(g_centre[:3] + come))


def solution(mesh):
    placed = (
        P(None, "space"),
        P("space"),
        P(None, "space"),
        P("space"),
        P(None, "space"),
        P(),
        P(),
        P(),
        P(),
        P(),
        P(),
        P(),
        P(),
    )
    return jax.shard_map(
        body, mesh=mesh, in_specs=placed, out_specs=(P("space"), P(None, "space")), check_vma=False
    )
```

```python
import jax
import jax.numpy as jnp
from jax import lax
from jax.experimental import pallas as pl
from jax.experimental.pallas import tpu as pltpu
from jax.sharding import PartitionSpec as P

RADIUS = 5.0
SOFTEN = 0.25
F32 = jnp.float32
BF16 = jnp.bfloat16
HALF = 64
MIB = 1024 * 1024


def hdot(a, b, dims=(((1,), (0,)), ((), ()))):
    return lax.dot_general(
        a, b, dims, precision=lax.Precision.HIGHEST, preferred_element_type=F32
    )


def hdot_t(a, b):
    return hdot(a, b, (((0,), (0,)), ((), ())))


def bdot(a, b):
    return jnp.dot(a, b, preferred_element_type=F32)


def bdot_nt(a, b):
    return lax.dot_general(a, b, (((1,), (1,)), ((), ())), preferred_element_type=F32)


def high(x):
    return x.astype(BF16).astype(F32)


def split_rows(x):
    hi = x.astype(BF16)
    lo = (x - hi.astype(F32)).astype(BF16)
    return hi, lo


def stack3(x):
    hi, lo = split_rows(x)
    return jnp.concatenate([hi, lo, hi], axis=0)


def sigmoid(v):
    return 0.5 + 0.5 * jnp.tanh(0.5 * v)


def roll64(x):
    return pltpu.roll(x, HALF, 1)


def lane_low(rows):
    return lax.broadcasted_iota(jnp.int32, (rows, 128), 1) < HALF


def parity_odd(rows):
    odd = lax.rem(lax.axis_index("space"), 2)
    return jnp.full((rows, 128), odd, jnp.int32) > 0


def far_lanes(rows):
    return parity_odd(rows) == lane_low(rows)


def copy_in(moves, sems):
    copies = [
        pltpu.make_async_copy(src, dst, sems.at[i]) for i, (src, dst) in enumerate(moves)
    ]
    for c in copies:
        c.start()
    for c in copies:
        c.wait()


def pack_kernel(pos_hbm, kind_hbm, own_ref, pos_ref, kind_ref, sems):
    copy_in([(pos_hbm, pos_ref), (kind_hbm, kind_ref)], sems)
    own_ref[0:3, :] = pos_ref[...]
    own_ref[3:4, :] = (kind_ref[...] + 1).astype(F32)


def remap_kernel(nb_hbm, gi_hbm, counts_hbm, out_ref, nb_ref, gi_ref, counts_ref, hot_ref, sems):
    copy_in([(nb_hbm, nb_ref), (gi_hbm, gi_ref), (counts_hbm, counts_ref)], sems)
    slots, atoms = nb_ref.shape
    rows = lax.broadcasted_iota(jnp.int32, (atoms, atoms), 0) + atoms
    for k in range(slots):
        nb = jnp.broadcast_to(nb_ref[k : k + 1, :], (atoms, atoms))
        hot_ref[:, pl.ds(k * atoms, atoms)] = (rows == nb).astype(F32).astype(BF16)
    place = jnp.concatenate(
        [jnp.broadcast_to(gi_ref[i : i + 1, :], (16, HALF)).astype(F32) for i in range(2)], axis=1
    )
    ghost = bdot(place.astype(BF16), hot_ref[...])
    for k in range(slots):
        nb = nb_ref[k : k + 1, :]
        there = ghost[0:1, k * atoms : (k + 1) * atoms] + F32(atoms)
        out_ref[k : k + 1, :] = jnp.where(nb < atoms, nb.astype(F32), there)
    out_ref[slots : slots + 1, :] = counts_ref[...].astype(F32)
    out_ref[slots + 1 :, :] = jnp.zeros((out_ref.shape[0] - slots - 1, atoms), F32)


def build_selector(rows_f32, base, slots, sel_ref):
    atoms = rows_f32.shape[1]
    rows = lax.broadcasted_iota(jnp.int32, (2 * atoms, atoms), 0).astype(F32)
    for k in range(slots):
        nb = jnp.broadcast_to(rows_f32[base + k : base + k + 1, :], (2 * atoms, atoms))
        sel_ref[:, pl.ds(k * atoms, atoms)] = (rows == nb).astype(F32).astype(BF16)


def prep_kernel(
    rin_hbm,
    rmid_hbm,
    rout_hbm,
    embed_hbm,
    mix_one_hbm,
    vec_hbm,
    mix_two_hbm,
    read_hbm,
    edges_ref,
    sel_ref,
    win_ref,
    wmid_ref,
    wout_ref,
    embed_ref,
    mix_one_ref,
    vec_ref,
    mix_two_ref,
    read_ref,
    rin_ref,
    rmid_ref,
    rout_ref,
    sems,
):
    copy_in(
        [
            (rin_hbm, rin_ref),
            (rmid_hbm, rmid_ref),
            (rout_hbm, rout_ref),
            (embed_hbm, embed_ref),
            (mix_one_hbm, mix_one_ref),
            (vec_hbm, vec_ref),
            (mix_two_hbm, mix_two_ref),
            (read_hbm, read_ref),
        ],
        sems,
    )
    build_selector(edges_ref[...], 0, sel_ref.shape[1] // edges_ref.shape[1], sel_ref)
    for layer in range(2):
        w = rin_ref[layer]
        h = high(w)
        lo = w - h
        win_ref[layer] = jnp.concatenate([h, h, lo, lo], axis=0).T.astype(BF16)
        w = rmid_ref[layer]
        h = high(w)
        wmid_ref[layer] = jnp.concatenate([h, h, w - h], axis=0).T.astype(BF16)
        w = rout_ref[layer]
        h = high(w)
        wout_ref[layer] = jnp.concatenate([h, h, w - h], axis=0).T.astype(BF16)


def basis_rows(b):
    h = high(b)
    lo = b - h
    return jnp.concatenate([h, lo, h, lo], axis=0).astype(BF16)


def radial(win, wmid, wout, b):
    v1 = bdot(win, basis_rows(b))
    z1 = v1 * sigmoid(v1)
    v2 = bdot(wmid, stack3(z1))
    z2 = v2 * sigmoid(v2)
    return bdot(wout, stack3(z2))


def silu_pair(v, t):
    s = sigmoid(v)
    z = v * s
    return z, (s + z * (1.0 - s)) * t


def radial_pair(win, wmid, wout, b, db):
    z1, t1 = silu_pair(bdot(win, basis_rows(b)), bdot(win, basis_rows(db)))
    z2, t2 = silu_pair(bdot(wmid, stack3(z1)), bdot(wmid, stack3(t1)))
    return bdot(wout, stack3(z2)), bdot(wout, stack3(t2))


def tile8(x, times):
    return jnp.concatenate([x] * times, axis=0)


def spread_rows(row, rows):
    return jnp.broadcast_to(row, (rows, row.shape[1]))


def geometry(far, own, valid):
    vec = [f - o for f, o in zip(far, own)]
    r2 = vec[0] * vec[0] + vec[1] * vec[1] + vec[2] * vec[2] + SOFTEN
    inv = lax.rsqrt(r2)
    inv = inv * (1.5 - 0.5 * r2 * inv * inv)
    rho = r2 * inv
    unit = [v * inv for v in vec]
    x = jnp.minimum(rho * (1.0 / RADIUS), 1.0)
    y = 1.0 - x
    x2 = x * x
    env = y * y * y * (1.0 + x * (3.0 + x * (6.0 + x * (10.0 + x * 15.0))))
    denv = (-105.0 / RADIUS) * x2 * x2 * y * y
    f = RADIUS * inv * env * valid
    df = RADIUS * inv * (denv - env * inv) * valid
    n = (lax.broadcasted_iota(jnp.int32, rho.shape, 0) + 1).astype(F32)
    turns = n * x
    whole = jnp.floor(turns + 0.5)
    frac = (turns - whole) * jnp.pi
    parity = whole - 2.0 * jnp.floor(0.5 * whole)
    sign = 1.0 - 2.0 * parity
    q = frac * frac
    sin = frac * (
        1.0
        + q * (-1 / 6 + q * (1 / 120 + q * (-1 / 5040 + q * (1 / 362880 + q * (-1 / 39916800)))))
    )
    cos = 1.0 + q * (
        -1 / 2
        + q * (1 / 24 + q * (-1 / 720 + q * (1 / 40320 + q * (-1 / 3628800 + q * (1 / 479001600)))))
    )
    sin = sin * sign
    cos = cos * sign
    return unit, inv, sin * f, sin * df + (n * (jnp.pi / RADIUS)) * cos * f


def forward_one(
    domain,
    table,
    counts,
    sel,
    embed,
    win,
    wmid,
    wout,
    mix_ref,
    vec,
    tab_ref,
    htab_ref,
    geom_ref,
    basis_ref,
    pre_ref,
    b_ref,
):
    atoms = table.shape[1] // 2
    slots = sel.shape[1] // atoms
    species, width = embed.shape
    for c in range(3):
        p = jnp.broadcast_to(table[c : c + 1], (8, 2 * atoms))
        h = p.astype(BF16)
        rest = p - h.astype(F32)
        m = rest.astype(BF16)
        lo = (rest - m.astype(F32)).astype(BF16)
        part = jnp.concatenate([h.astype(F32), m.astype(F32), lo.astype(F32)], axis=0)
        tab_ref[domain, c * 24 : c * 24 + 24, :] = part
    kind = jnp.broadcast_to(table[3:4], (species, 2 * atoms))
    onehot = (
        kind == (lax.broadcasted_iota(jnp.int32, (species, 2 * atoms), 0) + 1).astype(F32)
    ).astype(F32)
    h0 = hdot_t(embed, onehot)
    h0_hi = high(h0)
    tab_ref[domain, 72 : 72 + width, :] = h0_hi
    tab_ref[domain, 72 + width : 72 + 2 * width, :] = h0 - h0_hi
    tab = tab_ref[domain].astype(BF16)
    htab_ref[domain] = tab_ref[domain, 72 : 72 + 2 * width, :].astype(BF16)
    own_rep = [
        jnp.concatenate([jnp.broadcast_to(table[c : c + 1, :atoms], (8, atoms))] * slots, axis=1)
        for c in range(3)
    ]
    counts = jnp.broadcast_to(counts, (8, atoms))
    g = bdot(tab, sel)
    far = [
        g[24 * c : 24 * c + 8] + g[24 * c + 8 : 24 * c + 16] + g[24 * c + 16 : 24 * c + 24]
        for c in range(3)
    ]
    h_far = g[72 : 72 + width] + g[72 + width : 72 + 2 * width]
    valid = jnp.concatenate([(counts > F32(k)).astype(F32) for k in range(slots)], axis=1)
    unit, inv, b, db = geometry(far, own_rep, valid)
    for i, x in enumerate(unit + [inv]):
        geom_ref[domain, i : i + 1] = x[0:1]
    basis_ref[domain, 0] = b
    basis_ref[domain, 1] = db
    w = radial(win, wmid, wout, b)
    wa = w[:width] * h_far
    wb = w[width:] * h_far
    a_sum = jnp.zeros((width, atoms), F32)
    b_sum = [jnp.zeros((width, atoms), F32) for _ in range(3)]
    for k in range(slots):
        s = slice(k * atoms, (k + 1) * atoms)
        a_sum = a_sum + wa[:, s]
        for c in range(3):
            b_sum[c] = b_sum[c] + wb[:, s] * tile8(unit[c][:, s], width // 8)
    scale = 1.0 / jnp.sqrt(F32(slots))
    a_sum = a_sum * scale
    b_all = jnp.concatenate([x * scale for x in b_sum], axis=1)
    sq = b_all * b_all
    q = sq[:, :atoms] + sq[:, atoms : 2 * atoms] + sq[:, 2 * atoms :]
    pre = hdot_t(mix_ref[0], a_sum) + hdot_t(mix_ref[1], h0[:, :atoms]) + hdot_t(mix_ref[2], q)
    pre_ref[domain] = pre
    b_ref[domain] = b_all
    s1 = pre * sigmoid(pre)
    v1 = hdot_t(vec, b_all)
    lo_part = jnp.concatenate([s1, v1[:, :atoms]], axis=0)
    hi_part = jnp.concatenate([v1[:, atoms : 2 * atoms], v1[:, 2 * atoms :]], axis=0)
    return lo_part, hi_part


def layer_one_kernel(
    own_ref,
    near_ref,
    edges_ref,
    far_ref,
    sel_ref,
    embed_ref,
    win_ref,
    wmid_ref,
    wout_ref,
    mix_ref,
    vec_ref,
    feats_ref,
    near_out,
    htab_ref,
    geom_ref,
    basis_ref,
    pre_ref,
    b_ref,
    sel_far_ref,
    tab_ref,
):
    atoms = own_ref.shape[1]
    slots = sel_ref.shape[1] // atoms
    width = embed_ref.shape[1]
    ours = far_lanes(4)
    own = own_ref[...]
    there = far_ref[...]
    build_selector(there, 8, slots, sel_far_ref)
    tables = [
        jnp.concatenate([own, jnp.where(ours, there[0:4], near_ref[...])], axis=1),
        jnp.concatenate([there[0:4], jnp.where(ours, there[4:8], own)], axis=1),
    ]
    counts = [edges_ref[slots : slots + 1, :], there[8 + slots : 9 + slots]]
    for domain in range(2):
        lo_part, hi_part = forward_one(
            domain,
            tables[domain],
            counts[domain],
            (sel_ref, sel_far_ref)[domain][...],
            embed_ref[...],
            win_ref[0],
            wmid_ref[0],
            wout_ref[0],
            mix_ref,
            vec_ref[...],
            tab_ref,
            htab_ref,
            geom_ref,
            basis_ref,
            pre_ref,
            b_ref,
        )
        feats_ref[domain, 0 : 2 * width] = lo_part
        feats_ref[domain, 2 * width :] = hi_part
        if domain == 0:
            low_lanes, high_lanes = packed(lo_part, hi_part)
            near_out[...] = jnp.where(parity_odd(2 * width), low_lanes, high_lanes)


def packed(lo_part, hi_part):
    low = lane_low(lo_part.shape[0])
    return (
        jnp.where(low, lo_part, roll64(hi_part)),
        jnp.where(low, roll64(lo_part), hi_part),
    )


def unpacked(tile, high_half):
    other = roll64(tile)
    return jnp.where(high_half, other, tile), jnp.where(high_half, tile, other)


def radial_two_kernel(basis_ref, win_ref, wmid_ref, wout_ref, w_ref, dw_ref):
    w, dw = radial_pair(win_ref[1], wmid_ref[1], wout_ref[1], basis_ref[0, 0], basis_ref[0, 1])
    w_ref[...] = w
    dw_ref[...] = dw


def edge_gradient(unit, inv, drho, du):
    dot = unit[0] * du[0] + unit[1] * du[1] + unit[2] * du[2]
    radial_part = drho - dot * inv
    return [unit[c] * radial_part + du[c] * inv for c in range(3)]


def sum_rows(x):
    return jnp.sum(x, axis=0, keepdims=True)


def position_rows(grads):
    g = jnp.concatenate([jnp.broadcast_to(x, (8, x.shape[1])) for x in grads], axis=0)
    x = jnp.concatenate([g[0:1], g[8:9], g[16:17], jnp.zeros((5, g.shape[1]), F32)], axis=0)
    h = high(x)
    return jnp.concatenate([h, x - h], axis=0).astype(BF16)


def layer_two_kernel(
    feats_ref,
    near_ref,
    sel_ref,
    geom_ref,
    w_ref,
    dw_ref,
    mix_ref,
    read_ref,
    energy_ref,
    gown_ref,
    gghost_ref,
    near_out,
    far_out,
    gpos_ref,
    gpos_ghost_ref,
    far_scr,
    along_scr,
):
    atoms = feats_ref.shape[2]
    width = mix_ref.shape[1]
    slots = sel_ref.shape[1] // atoms
    rows = 2 * width
    odd = parity_odd(rows)
    ours = far_lanes(rows)
    near_lo, near_hi = unpacked(near_ref[...], odd)
    g_lo = jnp.where(ours, feats_ref[1, 0:rows], near_lo)
    g_hi = jnp.where(ours, feats_ref[1, rows:], near_hi)
    feats = feats_ref[0]
    table = jnp.concatenate([feats, jnp.concatenate([g_lo, g_hi], axis=0)], axis=1)
    t_hi, t_lo = split_rows(table)
    g = bdot(jnp.concatenate([t_hi, t_lo], axis=0), sel_ref[...])
    f = g[: 4 * width] + g[4 * width :]
    far_scr[...] = f
    unit = [geom_ref[0, c : c + 1] for c in range(3)]
    along = f[width : 2 * width] * spread_rows(unit[0], width)
    along = along + f[2 * width : 3 * width] * spread_rows(unit[1], width)
    along = along + f[3 * width :] * spread_rows(unit[2], width)
    along_scr[...] = along
    msg = w_ref[0:width] * f[:width] + w_ref[width:] * along
    m = jnp.zeros((width, atoms), F32)
    for k in range(slots):
        m = m + msg[:, k * atoms : (k + 1) * atoms]
    scale = 1.0 / jnp.sqrt(F32(slots))
    s1 = feats[:width]
    pre = hdot_t(mix_ref[0], m * scale) + hdot_t(mix_ref[1], s1)
    sg = sigmoid(pre)
    s2 = pre * sg
    energy_ref[...] = hdot(read_ref[0:1], s1) + hdot(read_ref[1:2], s2)
    read = read_ref[...].T
    r_one = jnp.broadcast_to(read[:, 0:1], (width, atoms))
    r_two = jnp.broadcast_to(read[:, 1:2], (width, atoms))
    gpre = r_two * (sg + s2 * (1.0 - sg))
    gm = hdot(mix_ref[0], gpre) * scale
    gs_own = r_one + hdot(mix_ref[1], gpre)
    gm_rep = jnp.concatenate([gm] * slots, axis=1)
    ga = w_ref[0:width] * gm_rep
    gb = w_ref[width:] * gm_rep
    gv = [gb * spread_rows(unit[c], width) for c in range(3)]
    drho = gm_rep * (dw_ref[0:width] * far_scr[0:width] + dw_ref[width:] * along_scr[...])
    du = [sum_rows(gb * far_scr[(c + 1) * width : (c + 2) * width]) for c in range(3)]
    gp = edge_gradient(unit, geom_ref[0, 3:4], sum_rows(drho), du)
    hi, lo = split_rows(jnp.concatenate([ga] + gv, axis=0))
    acc = bdot_nt(jnp.concatenate([hi, lo, position_rows(gp)], axis=0), sel_ref[...])
    grads = acc[: 4 * width] + acc[4 * width : 8 * width]
    own = grads[:, :atoms]
    gown_ref[0:width] = own[0:width] + gs_own
    gown_ref[width:] = own[width:]
    ghost = grads[:, atoms:]
    gghost_ref[...] = ghost
    to_upper, to_lower = packed(ghost[:rows], ghost[rows:])
    near_out[...] = jnp.where(odd, to_lower, to_upper)
    far_out[...] = jnp.where(odd, to_upper, to_lower)
    pos = acc[8 * width : 8 * width + 8] + acc[8 * width + 8 :]
    gpos_ref[...] = pos[:, :atoms] - centre_rows(gp, slots, atoms)
    gpos_ghost_ref[...] = pos[:, atoms:]


def centre_rows(gp, slots, atoms):
    total = [jnp.zeros((1, atoms), F32) for _ in range(3)]
    for k in range(slots):
        for c in range(3):
            total[c] = total[c] + gp[c][:, k * atoms : (k + 1) * atoms]
    return jnp.concatenate(total + [jnp.zeros((5, atoms), F32)], axis=0)


def join_kernel(gown_ref, near_ref, far_ref, gpos_ghost_ref, out_ref):
    rows = near_ref.shape[0]
    odd = parity_odd(rows)
    ours = far_lanes(rows)
    zero = jnp.zeros(near_ref.shape, F32)
    lo, hi = unpacked(near_ref[...], jnp.logical_not(odd))
    out_ref[0:rows] = gown_ref[0:rows] + jnp.where(ours, lo, zero)
    out_ref[rows : 2 * rows] = gown_ref[rows:] + jnp.where(ours, hi, zero)
    out_ref[2 * rows : 3 * rows] = far_ref[...]
    out_ref[3 * rows :] = gpos_ghost_ref[...]


def tangent_one_kernel(
    basis_ref, htab_ref, sel_ref, there_ref, win_ref, wmid_ref, wout_ref, out_ref, sel_ghost_ref, sel_scr
):
    atoms = there_ref.shape[1]
    width = htab_ref.shape[1] // 2
    slots = sel_ref.shape[1] // atoms
    build_selector(there_ref[...], 8, slots, sel_scr)
    sel_ghost_ref[...] = sel_scr[atoms:]
    for domain in range(2):
        w, dw = radial_pair(
            win_ref[0], wmid_ref[0], wout_ref[0], basis_ref[domain, 0], basis_ref[domain, 1]
        )
        g = bdot(htab_ref[domain], (sel_ref, sel_scr)[domain][...])
        h = g[:width] + g[width:]
        out_ref[domain, 0:width] = dw[:width] * h
        out_ref[domain, width : 2 * width] = dw[width:] * h
        out_ref[domain, 2 * width :] = w[width:] * h


def backward_one(g_lo, g_hi, pre, b_all, mix_ref, vec, geom_ref, domain, edge_ref, slots):
    width, atoms = pre.shape
    scale = 1.0 / jnp.sqrt(F32(slots))
    sg = sigmoid(pre)
    gpre = g_lo[:width] * (sg + pre * sg * (1.0 - sg))
    ga = hdot(mix_ref[0], gpre) * scale
    gq = hdot(mix_ref[2], gpre)
    gv = jnp.concatenate([g_lo[width:], g_hi[:width], g_hi[width:]], axis=1)
    gb_all = hdot(vec, gv) + 2.0 * b_all * jnp.concatenate([gq] * 3, axis=1)
    gb = [gb_all[:, c * atoms : (c + 1) * atoms] * scale for c in range(3)]
    ga_rep = jnp.concatenate([ga] * slots, axis=1)
    gb_rep = [jnp.concatenate([g] * slots, axis=1) for g in gb]
    unit = [geom_ref[domain, c : c + 1] for c in range(3)]
    gbu = gb_rep[0] * spread_rows(unit[0], width)
    gbu = gbu + gb_rep[1] * spread_rows(unit[1], width)
    gbu = gbu + gb_rep[2] * spread_rows(unit[2], width)
    drho = edge_ref[domain, 0:width] * ga_rep + edge_ref[domain, width : 2 * width] * gbu
    carried = edge_ref[domain, 2 * width :]
    du = [sum_rows(carried * gb_rep[c]) for c in range(3)]
    return edge_gradient(unit, geom_ref[domain, 3:4], sum_rows(drho), du)


def back_one_kernel(
    sent_ref,
    far_ref,
    gghost_ref,
    sel_ref,
    sel_ghost_ref,
    geom_ref,
    edge_ref,
    pre_ref,
    b_ref,
    mix_ref,
    vec_ref,
    gpos_ref,
    gown_out,
    ghost_out,
):
    atoms = gpos_ref.shape[1]
    width = mix_ref.shape[1]
    slots = sel_ref.shape[1] // atoms
    rows = 2 * width
    odd = parity_odd(rows)
    ours = far_lanes(rows)
    zero = jnp.zeros((rows, atoms), F32)
    lo, hi = unpacked(far_ref[2 * rows : 3 * rows], odd)
    g_lo = sent_ref[0:rows] + jnp.where(ours, zero, lo)
    g_hi = sent_ref[rows : 2 * rows] + jnp.where(ours, zero, hi)
    vec = vec_ref[...]
    gp = backward_one(
        g_lo, g_hi, pre_ref[0], b_ref[0], mix_ref, vec, geom_ref, 0, edge_ref, slots
    )
    acc = bdot_nt(position_rows(gp), sel_ref[...])
    pos = acc[0:8] + acc[8:16]
    ghost_out[...] = pos[:, atoms:] + sent_ref[3 * rows :]
    f_lo = far_ref[0:rows] + jnp.where(ours, gghost_ref[0:rows], zero)
    f_hi = far_ref[rows : 2 * rows] + jnp.where(ours, gghost_ref[rows:], zero)
    gf = backward_one(
        f_lo, f_hi, pre_ref[1], b_ref[1], mix_ref, vec, geom_ref, 1, edge_ref, slots
    )
    acc = bdot_nt(position_rows(gf), sel_ghost_ref[...])
    there = acc[0:8] + acc[8:16] + far_ref[3 * rows :]
    there = jnp.where(far_lanes(8), jnp.zeros((8, atoms), F32), there)
    gown_out[...] = gpos_ref[...] + pos[:, :atoms] - centre_rows(gp, slots, atoms) + there


def call(kernel, out_shapes, args, scratch=(), flops=0, transcendentals=0, far_away=0):
    args = [
        pltpu.with_memory_space_constraint(x, pltpu.HBM) if i < far_away else x
        for i, x in enumerate(args)
    ]
    spaces = [pltpu.HBM] * far_away + [pltpu.VMEM] * (len(args) - far_away)
    moved = sum(x.size * x.dtype.itemsize for x in list(args) + list(out_shapes))
    return pl.pallas_call(
        kernel,
        out_shape=out_shapes,
        in_specs=[pl.BlockSpec(memory_space=space) for space in spaces],
        out_specs=[pl.BlockSpec(memory_space=pltpu.VMEM)] * len(out_shapes),
        scratch_shapes=list(scratch),
        cost_estimate=pl.CostEstimate(
            flops=flops, bytes_accessed=moved, transcendentals=transcendentals
        ),
        compiler_params=pltpu.CompilerParams(vmem_limit_bytes=36 * MIB),
    )(*args)


def shape(dims, dtype=F32):
    return jax.ShapeDtypeStruct(dims, dtype)


def body(
    positions,
    species,
    neighbours,
    counts,
    ghost_index,
    embed,
    radial_in,
    radial_mid,
    radial_out,
    mix_one,
    vec_mix,
    mix_two,
    readout,
):
    atoms = positions.shape[1]
    slots = neighbours.shape[0]
    edges = slots * atoms
    nbasis, hidden = radial_in.shape[1:]
    width = embed.shape[1]
    rows = 2 * width
    devices = lax.axis_size("space")
    near_route = [(i, i ^ 1) for i in range(devices)]
    far_route = [(i, ((i + 1) ^ 1) - 1) for i in range(1, devices - 1)]

    def swap_near(x):
        return lax.ppermute(x, "space", near_route)

    def swap_far(x):
        return lax.ppermute(x, "space", far_route)

    def scratch_of(args):
        return [pltpu.VMEM(x.shape, x.dtype) for x in args]

    (own,) = call(
        pack_kernel,
        [shape((4, atoms))],
        [positions, species[None]],
        scratch=scratch_of([positions, species[None]]) + [pltpu.SemaphoreType.DMA((2,))],
        far_away=2,
    )
    near = swap_near(own)
    lists = [neighbours, ghost_index, counts[None]]
    (edge_rows,) = call(
        remap_kernel,
        [shape((slots + 8, atoms))],
        lists,
        scratch=scratch_of(lists)
        + [pltpu.VMEM((atoms, edges), BF16), pltpu.SemaphoreType.DMA((3,))],
        flops=10**8,
        far_away=3,
    )
    there = swap_far(jnp.concatenate([own, near, edge_rows], axis=0))
    weights = [radial_in, radial_mid, radial_out]
    passed = [embed, mix_one, vec_mix, mix_two, readout]
    moved = weights + passed
    sel, win, wmid, wout, embed, mix_one, vec_mix, mix_two, readout = call(
        prep_kernel,
        [
            shape((2 * atoms, edges), BF16),
            shape((2, hidden, 4 * nbasis), BF16),
            shape((2, hidden, 3 * hidden), BF16),
            shape((2, 2 * width, 3 * hidden), BF16),
        ]
        + [shape(x.shape, x.dtype) for x in passed],
        moved + [edge_rows],
        scratch=scratch_of(weights) + [pltpu.SemaphoreType.DMA((len(moved),))],
        flops=10**8,
        far_away=len(moved),
    )
    feats, near_f, htab, geom, basis, pre, b_all = call(
        layer_one_kernel,
        [
            shape((2, 4 * width, atoms)),
            shape((rows, atoms)),
            shape((2, 2 * width, 2 * atoms), BF16),
            shape((2, 8, edges)),
            shape((2, 2, 8, edges)),
            shape((2, width, atoms)),
            shape((2, width, 3 * atoms)),
        ],
        [own, near, edge_rows, there, sel, embed, win, wmid, wout, mix_one, vec_mix],
        scratch=[
            pltpu.VMEM((2 * atoms, edges), BF16),
            pltpu.VMEM((2, 72 + 2 * width, 2 * atoms), F32),
        ],
        flops=2 * 10**9,
    )
    near_f = swap_near(near_f)
    w, dw = call(
        radial_two_kernel,
        [shape((2 * width, edges)), shape((2 * width, edges))],
        [basis, win, wmid, wout],
        flops=2 * 10**9,
    )
    energy, g_own, g_ghost, near_g, far_g, gpos, gpos_ghost = call(
        layer_two_kernel,
        [
            shape((1, atoms)),
            shape((4 * width, atoms)),
            shape((4 * width, atoms)),
            shape((rows, atoms)),
            shape((rows, atoms)),
            shape((8, atoms)),
            shape((8, atoms)),
        ],
        [feats, near_f, sel, geom, w, dw, mix_two, readout],
        scratch=[pltpu.VMEM((4 * width, edges), F32), pltpu.VMEM((width, edges), F32)],
        flops=10**9,
    )
    near_g = swap_near(near_g)

    (sent,) = call(
        join_kernel, [shape((3 * rows + 8, atoms))], [g_own, near_g, far_g, gpos_ghost]
    )
    come = swap_far(sent)
    edge, sel_ghost = call(
        tangent_one_kernel,
        [shape((2, 3 * width, edges)), shape((atoms, edges), BF16)],
        [basis, htab, sel, there, win, wmid, wout],
        scratch=[pltpu.VMEM((2 * atoms, edges), BF16)],
        flops=4 * 10**9,
    )
    centre, ghost = call(
        back_one_kernel,
        [shape((8, atoms)), shape((8, atoms))],
        [
            sent,
            come,
            g_ghost,
            sel,
            sel_ghost,
            geom,
            edge,
            pre,
            b_all,
            mix_one,
            vec_mix,
            gpos,
        ],
        flops=10**9,
    )
    near_p = swap_near(ghost)
    odd = lax.rem(lax.axis_index("space"), 2) == 1
    low = lax.broadcasted_iota(jnp.int32, (3, atoms), 1) < HALF
    back = jnp.where(low == odd, near_p[:3], 0.0)
    return (energy[0], -(centre[:3] + back))


def solution(mesh):
    placed = (
        P(None, "space"),
        P("space"),
        P(None, "space"),
        P("space"),
        P(None, "space"),
        P(),
        P(),
        P(),
        P(),
        P(),
        P(),
        P(),
        P(),
    )
    return jax.shard_map(
        body, mesh=mesh, in_specs=placed, out_specs=(P("space"), P(None, "space")), check_vma=False
    )
```

```python
import jax
import jax.numpy as jnp
from jax import lax
from jax.experimental import pallas as pl
from jax.experimental.pallas import tpu as pltpu
from jax.sharding import PartitionSpec as P

RADIUS = 5.0
SOFTEN = 0.25
F32 = jnp.float32
BF16 = jnp.bfloat16
HALF = 64
MIB = 1024 * 1024


def hdot(a, b, dims=(((1,), (0,)), ((), ()))):
    return lax.dot_general(
        a, b, dims, precision=lax.Precision.HIGHEST, preferred_element_type=F32
    )


def hdot_t(a, b):
    return hdot(a, b, (((0,), (0,)), ((), ())))


def bdot(a, b):
    return jnp.dot(a, b, preferred_element_type=F32)


def bdot_nt(a, b):
    return lax.dot_general(a, b, (((1,), (1,)), ((), ())), preferred_element_type=F32)


def high(x):
    return x.astype(BF16).astype(F32)


def split(x):
    hi = x.astype(BF16)
    return hi, (x - hi.astype(F32)).astype(BF16)


def stack3(x):
    hi, lo = split(x)
    return jnp.concatenate([hi, lo, hi], axis=0)


def slot(k):
    return slice(k * 128, (k + 1) * 128)


def sigmoid(v):
    return 0.5 + 0.5 * jnp.tanh(0.5 * v)


def roll64(x):
    return pltpu.roll(x, HALF, 1)


def lane_low(rows):
    return lax.broadcasted_iota(jnp.int32, (rows, 128), 1) < HALF


def parity_odd(rows):
    odd = lax.rem(lax.axis_index("space"), 2)
    return jnp.full((rows, 128), odd, jnp.int32) > 0


def far_lanes(rows):
    return parity_odd(rows) == lane_low(rows)


def copy_in(moves, sems):
    copies = [
        pltpu.make_async_copy(src, dst, sems.at[i]) for i, (src, dst) in enumerate(moves)
    ]
    for c in copies:
        c.start()
    for c in copies:
        c.wait()


def pack_kernel(
    pos_hbm, kind_hbm, nb_hbm, gi_hbm, counts_hbm, own_ref, nb_ref, gi_ref, counts_ref, pos_ref, kind_ref, sems
):
    copy_in(
        [
            (pos_hbm, pos_ref),
            (kind_hbm, kind_ref),
            (nb_hbm, nb_ref),
            (gi_hbm, gi_ref),
            (counts_hbm, counts_ref),
        ],
        sems,
    )
    own_ref[0:3, :] = pos_ref[...]
    own_ref[3:4, :] = (kind_ref[...] + 1).astype(F32)


def remap_kernel(nb_ref, gi_ref, counts_ref, out_ref, hot_ref):
    slots, atoms = nb_ref.shape
    rows = lax.broadcasted_iota(jnp.int32, (atoms, atoms), 0) + atoms
    for k in range(slots):
        nb = jnp.broadcast_to(nb_ref[k : k + 1, :], (atoms, atoms))
        hot_ref[:, slot(k)] = (rows == nb).astype(F32).astype(BF16)
    place = jnp.concatenate(
        [jnp.broadcast_to(gi_ref[i : i + 1, :], (16, HALF)).astype(F32) for i in range(2)], axis=1
    )
    ghost = bdot(place.astype(BF16), hot_ref[...])
    for k in range(slots):
        nb = nb_ref[k : k + 1, :]
        out_ref[k : k + 1, :] = jnp.where(
            nb < atoms, nb.astype(F32), ghost[0:1, slot(k)] + F32(atoms)
        )
    out_ref[slots : slots + 1, :] = counts_ref[...].astype(F32)
    out_ref[slots + 1 :, :] = jnp.zeros((out_ref.shape[0] - slots - 1, atoms), F32)


def build_selector(rows_f32, sel_ref):
    count, atoms = rows_f32.shape
    rows = lax.broadcasted_iota(jnp.int32, (2 * atoms, atoms), 0).astype(F32)
    for k in range(count):
        nb = jnp.broadcast_to(rows_f32[k : k + 1, :], (2 * atoms, atoms))
        sel_ref[:, slot(k)] = (rows == nb).astype(F32).astype(BF16)


def prep_kernel(
    rin_hbm,
    rmid_hbm,
    rout_hbm,
    embed_hbm,
    mix_one_hbm,
    vec_hbm,
    mix_two_hbm,
    read_hbm,
    edges_ref,
    sel_ref,
    win_ref,
    wmid_ref,
    wout_ref,
    embed_ref,
    mix_one_ref,
    vec_ref,
    mix_two_ref,
    read_ref,
    rin_ref,
    rmid_ref,
    rout_ref,
    sems,
):
    copy_in(
        [
            (rin_hbm, rin_ref),
            (rmid_hbm, rmid_ref),
            (rout_hbm, rout_ref),
            (embed_hbm, embed_ref),
            (mix_one_hbm, mix_one_ref),
            (vec_hbm, vec_ref),
            (mix_two_hbm, mix_two_ref),
            (read_hbm, read_ref),
        ],
        sems,
    )
    build_selector(edges_ref[0 : sel_ref.shape[1] // edges_ref.shape[1], :], sel_ref)
    for layer in range(2):
        w = rin_ref[layer]
        h = high(w)
        lo = w - h
        win_ref[layer] = jnp.concatenate([h, h, lo, lo], axis=0).T.astype(BF16)
        w = rmid_ref[layer]
        h = high(w)
        wmid_ref[layer] = jnp.concatenate([h, h, w - h], axis=0).T.astype(BF16)
        w = rout_ref[layer]
        h = high(w)
        wout_ref[layer] = jnp.concatenate([h, h, w - h], axis=0).T.astype(BF16)


def basis_rows(b):
    h = high(b)
    lo = b - h
    return jnp.concatenate([h, lo, h, lo], axis=0).astype(BF16)


def radial(win, wmid, wout, b):
    v1 = bdot(win, basis_rows(b))
    v2 = bdot(wmid, stack3(v1 * sigmoid(v1)))
    return bdot(wout, stack3(v2 * sigmoid(v2)))


def silu_pair(v, t):
    s = sigmoid(v)
    z = v * s
    return z, (s + z * (1.0 - s)) * t


def radial_pair(win, wmid, wout, b, db):
    z1, t1 = silu_pair(bdot(win, basis_rows(b)), bdot(win, basis_rows(db)))
    z2, t2 = silu_pair(bdot(wmid, stack3(z1)), bdot(wmid, stack3(t1)))
    return bdot(wout, stack3(z2)), bdot(wout, stack3(t2))


def spread_rows(row, rows):
    return jnp.broadcast_to(row, (rows, row.shape[1]))


def geometry(far, own, valid):
    vec = [f - o for f, o in zip(far, own)]
    r2 = vec[0] * vec[0] + vec[1] * vec[1] + vec[2] * vec[2] + SOFTEN
    inv = lax.rsqrt(r2)
    inv = inv * (1.5 - 0.5 * r2 * inv * inv)
    rho = r2 * inv
    unit = [v * inv for v in vec]
    x = jnp.minimum(rho * (1.0 / RADIUS), 1.0)
    y = 1.0 - x
    x2 = x * x
    env = y * y * y * (1.0 + x * (3.0 + x * (6.0 + x * (10.0 + x * 15.0))))
    denv = (-105.0 / RADIUS) * x2 * x2 * y * y
    f = RADIUS * inv * env * valid
    df = RADIUS * inv * (denv - env * inv) * valid
    n = (lax.broadcasted_iota(jnp.int32, rho.shape, 0) + 1).astype(F32)
    turns = n * x
    whole = jnp.floor(turns + 0.5)
    frac = (turns - whole) * jnp.pi
    parity = whole - 2.0 * jnp.floor(0.5 * whole)
    sign = 1.0 - 2.0 * parity
    q = frac * frac
    sin = frac * (
        1.0
        + q * (-1 / 6 + q * (1 / 120 + q * (-1 / 5040 + q * (1 / 362880 + q * (-1 / 39916800)))))
    )
    cos = 1.0 + q * (
        -1 / 2
        + q * (1 / 24 + q * (-1 / 720 + q * (1 / 40320 + q * (-1 / 3628800 + q * (1 / 479001600)))))
    )
    sin = sin * sign
    cos = cos * sign
    return unit, inv, sin * f, sin * df + (n * (jnp.pi / RADIUS)) * cos * f


def make_table(table, embed, tab_ref):
    species, width = embed.shape
    columns = table.shape[1]
    parts = []
    for c in range(3):
        p = jnp.broadcast_to(table[c : c + 1], (8, columns))
        h = high(p)
        m = high(p - h)
        parts += [h, m, p - h - m]
    kind = jnp.broadcast_to(table[3:4], (species, columns))
    onehot = (
        kind == (lax.broadcasted_iota(jnp.int32, (species, columns), 0) + 1).astype(F32)
    ).astype(F32)
    h0 = hdot_t(embed, onehot)
    h0_hi = high(h0)
    zero = jnp.zeros((8, columns), F32)
    tab_ref[...] = jnp.concatenate([h0_hi, h0 - h0_hi] + parts + [zero], axis=0).astype(BF16)
    return h0


def gathered(g, width):
    base = 2 * width
    far = [
        g[base + 24 * c : base + 24 * c + 8]
        + g[base + 24 * c + 8 : base + 24 * c + 16]
        + g[base + 24 * c + 16 : base + 24 * c + 24]
        for c in range(3)
    ]
    return far, g[:width] + g[width:base]


def edge_geometry(far, own, counts, tiles):
    centre = [jnp.concatenate([spread_rows(own[c : c + 1], 8)] * tiles, axis=1) for c in range(3)]
    valid = jnp.concatenate([(counts > F32(k)).astype(F32) for k in range(tiles)], axis=1)
    return geometry(far, centre, valid)


def messages(w, h, unit, width, tiles):
    atoms = 128
    wa = w[:width] * h
    wb = w[width:] * h
    a_sum = jnp.zeros((width, atoms), F32)
    b_sum = [jnp.zeros((width, atoms), F32) for _ in range(3)]
    for k in range(tiles):
        a_sum = a_sum + wa[:, slot(k)]
        for c in range(3):
            b_sum[c] = b_sum[c] + wb[:, slot(k)] * tile8(unit[c][:, slot(k)], width // 8)
    return a_sum, b_sum


def tile8(x, times):
    return jnp.concatenate([x] * times, axis=0)


def mixed_pre(a, b_all, h0_own, mix_ref):
    atoms = a.shape[1]
    sq = b_all * b_all
    q = sq[:, :atoms] + sq[:, atoms : 2 * atoms] + sq[:, 2 * atoms :]
    return hdot_t(mix_ref[0], a) + hdot_t(mix_ref[1], h0_own) + hdot_t(mix_ref[2], q)


def features(pre, b_all, vec):
    atoms = pre.shape[1]
    v1 = hdot_t(vec, b_all)
    return (
        jnp.concatenate([pre * sigmoid(pre), v1[:, :atoms]], axis=0),
        jnp.concatenate([v1[:, atoms : 2 * atoms], v1[:, 2 * atoms :]], axis=0),
    )


def doubled(x):
    rows = x.shape[0]
    low = lane_low(rows)
    other = roll64(x)
    return jnp.where(low == parity_odd(rows), x, other)


def layer_one_kernel(
    own_ref,
    near_ref,
    edges_ref,
    far_ref,
    sel_ref,
    embed_ref,
    win_ref,
    wmid_ref,
    wout_ref,
    mix_ref,
    vec_ref,
    feats_ref,
    far_feats_ref,
    near_out,
    htab_ref,
    ftab_ref,
    geom_ref,
    basis_ref,
    pre_ref,
    b_ref,
    sel_far_ref,
    tab_ref,
):
    atoms = own_ref.shape[1]
    slots = sel_ref.shape[1] // atoms
    tiles = slots // 2
    width = embed_ref.shape[1]
    embed = embed_ref[...]
    scale = 1.0 / jnp.sqrt(F32(slots))
    ours = far_lanes(4)
    own = own_ref[...]
    there = far_ref[...]
    low12 = lane_low(tiles)
    lists = there[8 : 8 + slots]
    first = lists[:tiles]
    second = lists[tiles:]
    odd12 = parity_odd(tiles)
    build_selector(
        jnp.where(
            low12,
            jnp.where(odd12, first, roll64(first)),
            jnp.where(odd12, roll64(second), second),
        ),
        sel_far_ref,
    )
    h0 = make_table(
        jnp.concatenate([own, jnp.where(ours, there[0:4], near_ref[...])], axis=1), embed, tab_ref
    )
    h0_far = make_table(
        jnp.concatenate([there[0:4], jnp.where(ours, there[4:8], own)], axis=1), embed, ftab_ref
    )
    htab_ref[...] = tab_ref[0 : 2 * width, :]
    g = bdot(tab_ref[...], sel_ref[...])
    gf = bdot(ftab_ref[...], sel_far_ref[...])

    far, h_far = gathered(g, width)
    counts = spread_rows(edges_ref[slots : slots + 1, :], 8)
    unit, inv, b, db = edge_geometry(far, own, counts, slots)
    for i, x in enumerate(unit + [inv]):
        geom_ref[i : i + 1, :] = x[0:1]
    basis_ref[0] = b
    basis_ref[1] = db
    far, far_h = gathered(gf, width)
    half = doubled(there)
    counts = spread_rows(half[8 + slots : 9 + slots], 8) - jnp.where(
        lane_low(8), F32(0), F32(tiles)
    )
    far_unit, _, far_b, _ = edge_geometry(far, half, counts, tiles)

    win, wmid, wout = win_ref[0], wmid_ref[0], wout_ref[0]
    w = radial(win, wmid, wout, b)
    wf = radial(win, wmid, wout, far_b)
    a, b = messages(w, h_far, unit, width, slots)
    b_all = jnp.concatenate(b, axis=1) * scale
    pre = mixed_pre(a * scale, b_all, h0[:, :atoms], mix_ref)
    pre_ref[...] = pre
    b_ref[...] = b_all
    vec = vec_ref[...]
    lo_part, hi_part = features(pre, b_all, vec)
    feats_ref[0 : 2 * width] = lo_part
    feats_ref[2 * width :] = hi_part
    low_lanes, high_lanes = packed(lo_part, hi_part)
    near_out[...] = jnp.where(parity_odd(2 * width), low_lanes, high_lanes)

    a, b = messages(wf, far_h, far_unit, width, tiles)
    a = (a + roll64(a)) * scale
    b_all = jnp.concatenate([x + roll64(x) for x in b], axis=1) * scale
    pre = mixed_pre(a, b_all, doubled(h0_far[:, :atoms]), mix_ref)
    lo_part, hi_part = features(pre, b_all, vec)
    far_feats_ref[0 : 2 * width] = lo_part
    far_feats_ref[2 * width :] = hi_part


def packed(lo_part, hi_part):
    low = lane_low(lo_part.shape[0])
    return (
        jnp.where(low, lo_part, roll64(hi_part)),
        jnp.where(low, roll64(lo_part), hi_part),
    )


def unpacked(tile, high_half):
    other = roll64(tile)
    return jnp.where(high_half, other, tile), jnp.where(high_half, tile, other)


def radial_two_kernel(basis_ref, win_ref, wmid_ref, wout_ref, w_ref, dw_ref):
    w, dw = radial_pair(win_ref[1], wmid_ref[1], wout_ref[1], basis_ref[0], basis_ref[1])
    w_ref[...] = w
    dw_ref[...] = dw


def edge_gradient(unit, inv, drho, du):
    dot = unit[0] * du[0] + unit[1] * du[1] + unit[2] * du[2]
    radial_part = drho - dot * inv
    return [unit[c] * radial_part + du[c] * inv for c in range(3)]


def sum_groups(x):
    total = x[0:8]
    for i in range(1, x.shape[0] // 8):
        total = total + x[8 * i : 8 * i + 8]
    return total


def put_positions(ref, base, grads):
    x = jnp.concatenate(list(grads), axis=0)
    hi, lo = split(x)
    ref[base : base + 24] = hi
    ref[base + 24 : base + 48] = lo


def rows8(x):
    sums = [jnp.sum(x[8 * c : 8 * c + 8], axis=0, keepdims=True) for c in range(3)]
    return jnp.concatenate(sums + [jnp.zeros((5, x.shape[1]), F32)], axis=0)


def centre_sum(grads, slots):
    x = jnp.concatenate(list(grads), axis=0)
    total = x[:, slot(0)]
    for k in range(1, slots):
        total = total + x[:, slot(k)]
    return total


def layer_two_kernel(
    feats_ref,
    far_feats_ref,
    near_ref,
    sel_ref,
    geom_ref,
    w_ref,
    dw_ref,
    mix_ref,
    read_ref,
    energy_ref,
    gown_ref,
    gghost_ref,
    near_out,
    far_out,
    gpos_ref,
    gpos_ghost_ref,
    grad_scr,
):
    atoms = feats_ref.shape[1]
    width = mix_ref.shape[1]
    slots = sel_ref.shape[1] // atoms
    rows = 2 * width
    odd = parity_odd(rows)
    ours = far_lanes(rows)
    near_lo, near_hi = unpacked(near_ref[...], odd)
    g_lo = jnp.where(ours, far_feats_ref[0:rows], near_lo)
    g_hi = jnp.where(ours, far_feats_ref[rows:], near_hi)
    feats = feats_ref[...]
    table = jnp.concatenate([feats, jnp.concatenate([g_lo, g_hi], axis=0)], axis=1)
    t_hi, t_lo = split(table)
    g = bdot(jnp.concatenate([t_hi, t_lo], axis=0), sel_ref[...])

    f = g[: 4 * width] + g[4 * width :]
    unit = [geom_ref[c : c + 1, :] for c in range(3)]
    along = f[width : 2 * width] * spread_rows(unit[0], width)
    along = along + f[2 * width : 3 * width] * spread_rows(unit[1], width)
    along = along + f[3 * width :] * spread_rows(unit[2], width)
    msg = w_ref[0:width] * f[:width] + w_ref[width:] * along
    m = jnp.zeros((width, atoms), F32)
    for k in range(slots):
        m = m + msg[:, slot(k)]
    scale = 1.0 / jnp.sqrt(F32(slots))
    s1 = feats[:width]
    pre = hdot_t(mix_ref[0], m * scale) + hdot_t(mix_ref[1], s1)
    sg = sigmoid(pre)
    s2 = pre * sg
    energy_ref[...] = hdot(read_ref[0:1], s1) + hdot(read_ref[1:2], s2)
    read = read_ref[...].T
    r_one = jnp.broadcast_to(read[:, 0:1], (width, atoms))
    r_two = jnp.broadcast_to(read[:, 1:2], (width, atoms))
    gpre = r_two * (sg + s2 * (1.0 - sg))
    gm = hdot(mix_ref[0], gpre) * scale
    gs_own = r_one + hdot(mix_ref[1], gpre)
    gm_rep = jnp.concatenate([gm] * slots, axis=1)
    ga = w_ref[0:width] * gm_rep
    gb = w_ref[width:] * gm_rep
    for i, x in enumerate([ga] + [gb * spread_rows(u, width) for u in unit]):
        hi, lo = split(x)
        grad_scr[i * width : (i + 1) * width] = hi
        grad_scr[(4 + i) * width : (5 + i) * width] = lo
    drho = gm_rep * (dw_ref[0:width] * f[:width] + dw_ref[width:] * along)
    du = [sum_groups(gb * f[(c + 1) * width : (c + 2) * width]) for c in range(3)]
    gp = edge_gradient(
        [spread_rows(u, 8) for u in unit],
        spread_rows(geom_ref[3:4, :], 8),
        sum_groups(drho),
        du,
    )
    put_positions(grad_scr, 8 * width, gp)
    centre = centre_sum(gp, slots)
    acc = bdot_nt(grad_scr[...], sel_ref[...])
    grads = acc[: 4 * width] + acc[4 * width : 8 * width]
    own = grads[:, :atoms]
    gown_ref[0:width] = own[0:width] + gs_own
    gown_ref[width:] = own[width:]
    ghost = grads[:, atoms:]
    gghost_ref[...] = ghost
    to_upper, to_lower = packed(ghost[:rows], ghost[rows:])
    near_out[...] = jnp.where(odd, to_lower, to_upper)
    far_out[...] = jnp.where(odd, to_upper, to_lower)
    pos = acc[8 * width : 8 * width + 24] + acc[8 * width + 24 :]
    gpos_ref[...] = rows8(pos[:, :atoms] - centre)
    gpos_ghost_ref[...] = rows8(pos[:, atoms:])


def join_kernel(gown_ref, near_ref, far_ref, gpos_ghost_ref, out_ref):
    rows = near_ref.shape[0]
    odd = parity_odd(rows)
    ours = far_lanes(rows)
    zero = jnp.zeros(near_ref.shape, F32)
    lo, hi = unpacked(near_ref[...], jnp.logical_not(odd))
    out_ref[0:rows] = gown_ref[0:rows] + jnp.where(ours, lo, zero)
    out_ref[rows : 2 * rows] = gown_ref[rows:] + jnp.where(ours, hi, zero)
    out_ref[2 * rows : 3 * rows] = far_ref[...]
    out_ref[3 * rows :] = gpos_ghost_ref[...]


def tangent_one_kernel(
    basis_ref,
    htab_ref,
    ftab_ref,
    sel_ref,
    there_ref,
    win_ref,
    wmid_ref,
    wout_ref,
    mix_ref,
    embed_ref,
    edge_ref,
    sel_ghost_ref,
    geom_ref,
    pre_ref,
    b_ref,
    sel_scr,
):
    atoms = there_ref.shape[1]
    width = htab_ref.shape[0] // 2
    slots = sel_ref.shape[1] // atoms
    win, wmid, wout = win_ref[0], wmid_ref[0], wout_ref[0]

    def store(domain, w, dw, h):
        edge_ref[domain, 0:width] = dw[:width] * h
        edge_ref[domain, width : 2 * width] = dw[width:] * h
        edge_ref[domain, 2 * width :] = w[width:] * h

    w, dw = radial_pair(win, wmid, wout, basis_ref[0], basis_ref[1])
    g = bdot(htab_ref[...], sel_ref[...])
    store(0, w, dw, g[:width] + g[width:])

    there = there_ref[...]
    build_selector(there[8 : 8 + slots], sel_scr)
    sel_ghost_ref[...] = sel_scr[atoms:]
    far, h = gathered(bdot(ftab_ref[...], sel_scr[...]), width)
    counts = spread_rows(there[8 + slots : 9 + slots], 8)
    unit, inv, b, db = edge_geometry(far, there, counts, slots)
    for i, x in enumerate(unit + [inv]):
        geom_ref[i : i + 1, :] = x[0:1]
    w, dw = radial_pair(win, wmid, wout, b, db)
    store(1, w, dw, h)
    a, b = messages(w, h, unit, width, slots)
    scale = 1.0 / jnp.sqrt(F32(slots))
    b_all = jnp.concatenate(b, axis=1) * scale
    species = embed_ref.shape[0]
    kind = jnp.broadcast_to(there[3:4], (species, atoms))
    onehot = (
        kind == (lax.broadcasted_iota(jnp.int32, (species, atoms), 0) + 1).astype(F32)
    ).astype(F32)
    pre_ref[...] = mixed_pre(a * scale, b_all, hdot_t(embed_ref[...], onehot), mix_ref)
    b_ref[...] = b_all


def back_one_kernel(
    sent_ref,
    far_ref,
    gghost_ref,
    sel_ref,
    sel_ghost_ref,
    geom_ref,
    far_geom_ref,
    edge_ref,
    pre_ref,
    far_pre_ref,
    b_ref,
    far_b_ref,
    mix_ref,
    vec_ref,
    gpos_ref,
    gown_out,
    ghost_out,
    pos_scr,
    far_pos_scr,
):
    atoms = gpos_ref.shape[1]
    width = mix_ref.shape[1]
    slots = sel_ref.shape[1] // atoms
    rows = 2 * width
    odd = parity_odd(rows)
    ours = far_lanes(rows)
    zero = jnp.zeros((rows, atoms), F32)
    scale = 1.0 / jnp.sqrt(F32(slots))
    lo, hi = unpacked(far_ref[2 * rows : 3 * rows], odd)
    g_lo = sent_ref[0:rows] + jnp.where(ours, zero, lo)
    g_hi = sent_ref[rows : 2 * rows] + jnp.where(ours, zero, hi)
    f_lo = far_ref[0:rows] + jnp.where(ours, gghost_ref[0:rows], zero)
    f_hi = far_ref[rows : 2 * rows] + jnp.where(ours, gghost_ref[rows:], zero)
    pre = jnp.concatenate([pre_ref[...], far_pre_ref[...]], axis=1)
    sg = sigmoid(pre)
    gpre = jnp.concatenate([g_lo[:width], f_lo[:width]], axis=1) * (sg + pre * sg * (1.0 - sg))
    ga = hdot(mix_ref[0], gpre) * scale
    gq = hdot(mix_ref[2], gpre) * (2.0 * scale)
    gv = jnp.concatenate(
        [g_lo[width:], g_hi[:width], g_hi[width:], f_lo[width:], f_hi[:width], f_hi[width:]],
        axis=1,
    )
    gb_all = hdot(vec_ref[...], gv) * scale
    b_of = [b_ref, far_b_ref]
    geom_of = [geom_ref, far_geom_ref]
    scr_of = [pos_scr, far_pos_scr]
    for domain in range(2):
        ga_d = ga[:, slot(domain)]
        gq_d = gq[:, slot(domain)]
        gb = [
            gb_all[:, slot(3 * domain + c)] + b_of[domain][:, slot(c)] * gq_d for c in range(3)
        ]
        geom = geom_of[domain]
        total = jnp.zeros((24, atoms), F32)
        for k in range(slots):
            unit = [spread_rows(geom[c : c + 1, slot(k)], 8) for c in range(3)]
            u = [tile8(x, width // 8) for x in unit]
            gbu = gb[0] * u[0] + gb[1] * u[1] + gb[2] * u[2]
            drho = (
                edge_ref[domain, 0:width, slot(k)] * ga_d
                + edge_ref[domain, width : 2 * width, slot(k)] * gbu
            )
            carried = edge_ref[domain, 2 * width :, slot(k)]
            du = [sum_groups(carried * gb[c]) for c in range(3)]
            gp = edge_gradient(unit, spread_rows(geom[3:4, slot(k)], 8), sum_groups(drho), du)
            x = jnp.concatenate(gp, axis=0)
            if domain == 0:
                total = total + x
            hi, lo = split(x)
            scr_of[domain][0:24, slot(k)] = hi
            scr_of[domain][24:48, slot(k)] = lo
        if domain == 0:
            centre = total
    acc = bdot_nt(pos_scr[...], sel_ref[...])
    pos = acc[0:24] + acc[24:48]
    ghost_out[...] = rows8(pos[:, atoms:]) + sent_ref[3 * rows :]
    acc = bdot_nt(far_pos_scr[...], sel_ghost_ref[...])
    there = rows8(acc[0:24] + acc[24:48]) + far_ref[3 * rows :]
    there = jnp.where(far_lanes(8), jnp.zeros((8, atoms), F32), there)
    gown_out[...] = gpos_ref[...] + rows8(pos[:, :atoms] - centre) + there


def call(kernel, out_shapes, args, scratch=(), flops=0, transcendentals=0, far_away=0):
    args = [
        pltpu.with_memory_space_constraint(x, pltpu.HBM) if i < far_away else x
        for i, x in enumerate(args)
    ]
    spaces = [pltpu.HBM] * far_away + [pltpu.VMEM] * (len(args) - far_away)
    moved = sum(x.size * x.dtype.itemsize for x in list(args) + list(out_shapes))
    return pl.pallas_call(
        kernel,
        out_shape=out_shapes,
        in_specs=[pl.BlockSpec(memory_space=space) for space in spaces],
        out_specs=[pl.BlockSpec(memory_space=pltpu.VMEM)] * len(out_shapes),
        scratch_shapes=list(scratch),
        cost_estimate=pl.CostEstimate(
            flops=flops, bytes_accessed=moved, transcendentals=transcendentals
        ),
        compiler_params=pltpu.CompilerParams(vmem_limit_bytes=36 * MIB),
    )(*args)


def shape(dims, dtype=F32):
    return jax.ShapeDtypeStruct(dims, dtype)


def body(
    positions,
    species,
    neighbours,
    counts,
    ghost_index,
    embed,
    radial_in,
    radial_mid,
    radial_out,
    mix_one,
    vec_mix,
    mix_two,
    readout,
):
    atoms = positions.shape[1]
    slots = neighbours.shape[0]
    edges = slots * atoms
    nbasis, hidden = radial_in.shape[1:]
    width = embed.shape[1]
    rows = 2 * width
    devices = lax.axis_size("space")
    near_route = [(i, i ^ 1) for i in range(devices)]
    far_route = [(i, ((i + 1) ^ 1) - 1) for i in range(1, devices - 1)]

    def swap_near(x):
        return lax.ppermute(x, "space", near_route)

    def swap_far(x):
        return lax.ppermute(x, "space", far_route)

    def scratch_of(args):
        return [pltpu.VMEM(x.shape, x.dtype) for x in args]

    def shapes_of(args):
        return [shape(x.shape, x.dtype) for x in args]

    atom_rows = [positions, species[None]]
    lists = [neighbours, ghost_index, counts[None]]
    own, *lists = call(
        pack_kernel,
        [shape((4, atoms))] + shapes_of(lists),
        atom_rows + lists,
        scratch=scratch_of(atom_rows) + [pltpu.SemaphoreType.DMA((5,))],
        far_away=5,
    )
    near = swap_near(own)
    (edge_rows,) = call(
        remap_kernel,
        [shape((slots + 8, atoms))],
        lists,
        scratch=[pltpu.VMEM((atoms, edges), BF16)],
        flops=10**8,
    )
    there = swap_far(jnp.concatenate([own, near, edge_rows], axis=0))
    weights = [radial_in, radial_mid, radial_out]
    passed = [embed, mix_one, vec_mix, mix_two, readout]
    moved = weights + passed
    sel, win, wmid, wout, embed, mix_one, vec_mix, mix_two, readout = call(
        prep_kernel,
        [
            shape((2 * atoms, edges), BF16),
            shape((2, hidden, 4 * nbasis), BF16),
            shape((2, hidden, 3 * hidden), BF16),
            shape((2, 2 * width, 3 * hidden), BF16),
        ]
        + shapes_of(passed),
        moved + [edge_rows],
        scratch=scratch_of(weights) + [pltpu.SemaphoreType.DMA((len(moved),))],
        flops=10**8,
        far_away=len(moved),
    )
    table_rows = 2 * width + 80
    feats, far_feats, near_f, htab, ftab, geom, basis, pre, b_all = call(
        layer_one_kernel,
        [
            shape((4 * width, atoms)),
            shape((4 * width, atoms)),
            shape((rows, atoms)),
            shape((2 * width, 2 * atoms), BF16),
            shape((table_rows, 2 * atoms), BF16),
            shape((8, edges)),
            shape((2, nbasis, edges)),
            shape((width, atoms)),
            shape((width, 3 * atoms)),
        ],
        [own, near, edge_rows, there, sel, embed, win, wmid, wout, mix_one, vec_mix],
        scratch=[
            pltpu.VMEM((2 * atoms, edges // 2), BF16),
            pltpu.VMEM((table_rows, 2 * atoms), BF16),
        ],
        flops=2 * 10**9,
    )
    near_f = swap_near(near_f)
    w, dw = call(
        radial_two_kernel,
        [shape((2 * width, edges)), shape((2 * width, edges))],
        [basis, win, wmid, wout],
        flops=2 * 10**9,
    )
    energy, g_own, g_ghost, near_g, far_g, gpos, gpos_ghost = call(
        layer_two_kernel,
        [
            shape((1, atoms)),
            shape((4 * width, atoms)),
            shape((4 * width, atoms)),
            shape((rows, atoms)),
            shape((rows, atoms)),
            shape((8, atoms)),
            shape((8, atoms)),
        ],
        [feats, far_feats, near_f, sel, geom, w, dw, mix_two, readout],
        scratch=[pltpu.VMEM((8 * width + 48, edges), BF16)],
        flops=10**9,
    )
    near_g = swap_near(near_g)
    (sent,) = call(
        join_kernel, [shape((3 * rows + 8, atoms))], [g_own, near_g, far_g, gpos_ghost]
    )
    come = swap_far(sent)
    edge, sel_ghost, far_geom, far_pre, far_b = call(
        tangent_one_kernel,
        [
            shape((2, 3 * width, edges)),
            shape((atoms, edges), BF16),
            shape((8, edges)),
            shape((width, atoms)),
            shape((width, 3 * atoms)),
        ],
        [basis, htab, ftab, sel, there, win, wmid, wout, mix_one, embed],
        scratch=[pltpu.VMEM((2 * atoms, edges), BF16)],
        flops=4 * 10**9,
    )
    centre, ghost = call(
        back_one_kernel,
        [shape((8, atoms)), shape((8, atoms))],
        [
            sent,
            come,
            g_ghost,
            sel,
            sel_ghost,
            geom,
            far_geom,
            edge,
            pre,
            far_pre,
            b_all,
            far_b,
            mix_one,
            vec_mix,
            gpos,
        ],
        scratch=[pltpu.VMEM((48, edges), BF16), pltpu.VMEM((48, edges), BF16)],
        flops=10**9,
    )
    near_p = swap_near(ghost)
    odd = lax.rem(lax.axis_index("space"), 2) == 1
    low = lax.broadcasted_iota(jnp.int32, (3, atoms), 1) < HALF
    back = jnp.where(low == odd, near_p[:3], 0.0)
    return (energy[0], -(centre[:3] + back))


def solution(mesh):
    placed = (
        P(None, "space"),
        P("space"),
        P(None, "space"),
        P("space"),
        P(None, "space"),
        P(),
        P(),
        P(),
        P(),
        P(),
        P(),
        P(),
        P(),
    )
    return jax.shard_map(
        body, mesh=mesh, in_specs=placed, out_specs=(P("space"), P(None, "space")), check_vma=False
    )
```

```python
import jax
import jax.numpy as jnp
from jax import lax
from jax.experimental import pallas as pl
from jax.experimental.pallas import tpu as pltpu
from jax.sharding import PartitionSpec as P

RADIUS = 5.0
SOFTEN = 0.25
F32 = jnp.float32
BF16 = jnp.bfloat16
HALF = 64
MIB = 1024 * 1024


def hdot(a, b, dims=(((1,), (0,)), ((), ()))):
    return lax.dot_general(
        a, b, dims, precision=lax.Precision.HIGHEST, preferred_element_type=F32
    )


def hdot_t(a, b):
    return hdot(a, b, (((0,), (0,)), ((), ())))


def bdot(a, b):
    return jnp.dot(a, b, preferred_element_type=F32)


def bdot_nt(a, b):
    return lax.dot_general(a, b, (((1,), (1,)), ((), ())), preferred_element_type=F32)


def high(x):
    return x.astype(BF16).astype(F32)


def split(x):
    hi = x.astype(BF16)
    return hi, (x - hi.astype(F32)).astype(BF16)


def stack3(x):
    hi, lo = split(x)
    return jnp.concatenate([hi, lo, hi], axis=0)


def slot(k):
    return slice(k * 128, (k + 1) * 128)


def sigmoid(v):
    return 0.5 + 0.5 * jnp.tanh(0.5 * v)


def roll64(x):
    return pltpu.roll(x, HALF, 1)


def lane_low(rows):
    return lax.broadcasted_iota(jnp.int32, (rows, 128), 1) < HALF


def parity_odd(rows):
    odd = lax.rem(lax.axis_index("space"), 2)
    return jnp.full((rows, 128), odd, jnp.int32) > 0


def far_lanes(rows):
    return parity_odd(rows) == lane_low(rows)


def copy_in(moves, sems):
    copies = [
        pltpu.make_async_copy(src, dst, sems.at[i]) for i, (src, dst) in enumerate(moves)
    ]
    for c in copies:
        c.start()
    for c in copies:
        c.wait()


def put_lists(nb_ref, gi_ref, counts_ref, out_ref, hot_ref):
    slots, atoms = nb_ref.shape
    rows = lax.broadcasted_iota(jnp.int32, (atoms, atoms), 0) + atoms
    for k in range(slots):
        nb = jnp.broadcast_to(nb_ref[k : k + 1, :], (atoms, atoms))
        hot_ref[:, slot(k)] = (rows == nb).astype(F32).astype(BF16)
    place = jnp.concatenate(
        [jnp.broadcast_to(gi_ref[i : i + 1, :], (16, HALF)).astype(F32) for i in range(2)], axis=1
    )
    ghost = bdot(place.astype(BF16), hot_ref[...])
    for k in range(slots):
        nb = nb_ref[k : k + 1, :]
        out_ref[k : k + 1, :] = jnp.where(
            nb < atoms, nb.astype(F32), ghost[0:1, slot(k)] + F32(atoms)
        )
    out_ref[slots : slots + 1, :] = counts_ref[...].astype(F32)
    out_ref[slots + 1 :, :] = jnp.zeros((out_ref.shape[0] - slots - 1, atoms), F32)


def build_selector(rows_f32, sel_ref):
    count, atoms = rows_f32.shape
    rows = lax.broadcasted_iota(jnp.int32, (2 * atoms, atoms), 0).astype(F32)
    for k in range(count):
        nb = jnp.broadcast_to(rows_f32[k : k + 1, :], (2 * atoms, atoms))
        sel_ref[:, slot(k)] = (rows == nb).astype(F32).astype(BF16)


def prep_kernel(
    pos_hbm,
    kind_hbm,
    nb_hbm,
    gi_hbm,
    counts_hbm,
    rin_hbm,
    rmid_hbm,
    rout_hbm,
    embed_hbm,
    mix_one_hbm,
    vec_hbm,
    mix_two_hbm,
    read_hbm,
    own_ref,
    edges_ref,
    sel_ref,
    win_ref,
    wmid_ref,
    wout_ref,
    embed_ref,
    mix_one_ref,
    vec_ref,
    mix_two_ref,
    read_ref,
    pos_ref,
    kind_ref,
    nb_ref,
    gi_ref,
    counts_ref,
    rin_ref,
    rmid_ref,
    rout_ref,
    hot_ref,
    sems,
):
    copy_in(
        [
            (pos_hbm, pos_ref),
            (kind_hbm, kind_ref),
            (nb_hbm, nb_ref),
            (gi_hbm, gi_ref),
            (counts_hbm, counts_ref),
            (rin_hbm, rin_ref),
            (rmid_hbm, rmid_ref),
            (rout_hbm, rout_ref),
            (embed_hbm, embed_ref),
            (mix_one_hbm, mix_one_ref),
            (vec_hbm, vec_ref),
            (mix_two_hbm, mix_two_ref),
            (read_hbm, read_ref),
        ],
        sems,
    )
    own_ref[0:3, :] = pos_ref[...]
    own_ref[3:4, :] = (kind_ref[...] + 1).astype(F32)
    put_lists(nb_ref, gi_ref, counts_ref, edges_ref, hot_ref)
    build_selector(edges_ref[0 : nb_ref.shape[0], :], sel_ref)
    for layer in range(2):
        w = rin_ref[layer]
        h = high(w)
        lo = w - h
        win_ref[layer] = jnp.concatenate([h, h, lo, lo], axis=0).T.astype(BF16)
        w = rmid_ref[layer]
        h = high(w)
        wmid_ref[layer] = jnp.concatenate([h, h, w - h], axis=0).T.astype(BF16)
        w = rout_ref[layer]
        h = high(w)
        wout_ref[layer] = jnp.concatenate([h, h, w - h], axis=0).T.astype(BF16)


def basis_rows(b):
    h = high(b)
    lo = b - h
    return jnp.concatenate([h, lo, h, lo], axis=0).astype(BF16)


def radial(win, wmid, wout, b):
    v1 = bdot(win, basis_rows(b))
    v2 = bdot(wmid, stack3(v1 * sigmoid(v1)))
    return bdot(wout, stack3(v2 * sigmoid(v2)))


def silu_pair(v, t):
    s = sigmoid(v)
    z = v * s
    return z, (s + z * (1.0 - s)) * t


def radial_pair(win, wmid, wout, b, db):
    z1, t1 = silu_pair(bdot(win, basis_rows(b)), bdot(win, basis_rows(db)))
    z2, t2 = silu_pair(bdot(wmid, stack3(z1)), bdot(wmid, stack3(t1)))
    return bdot(wout, stack3(z2)), bdot(wout, stack3(t2))


def spread_rows(row, rows):
    return jnp.broadcast_to(row, (rows, row.shape[1]))


def geometry(far, own, valid):
    vec = [f - o for f, o in zip(far, own)]
    r2 = vec[0] * vec[0] + vec[1] * vec[1] + vec[2] * vec[2] + SOFTEN
    inv = lax.rsqrt(r2)
    inv = inv * (1.5 - 0.5 * r2 * inv * inv)
    rho = r2 * inv
    unit = [v * inv for v in vec]
    x = jnp.minimum(rho * (1.0 / RADIUS), 1.0)
    y = 1.0 - x
    x2 = x * x
    env = y * y * y * (1.0 + x * (3.0 + x * (6.0 + x * (10.0 + x * 15.0))))
    denv = (-105.0 / RADIUS) * x2 * x2 * y * y
    f = RADIUS * inv * env * valid
    df = RADIUS * inv * (denv - env * inv) * valid
    n = (lax.broadcasted_iota(jnp.int32, rho.shape, 0) + 1).astype(F32)
    turns = n * x
    whole = jnp.floor(turns + 0.5)
    frac = (turns - whole) * jnp.pi
    parity = whole - 2.0 * jnp.floor(0.5 * whole)
    sign = 1.0 - 2.0 * parity
    q = frac * frac
    sin = frac * (
        1.0
        + q * (-1 / 6 + q * (1 / 120 + q * (-1 / 5040 + q * (1 / 362880 + q * (-1 / 39916800)))))
    )
    cos = 1.0 + q * (
        -1 / 2
        + q * (1 / 24 + q * (-1 / 720 + q * (1 / 40320 + q * (-1 / 3628800 + q * (1 / 479001600)))))
    )
    sin = sin * sign
    cos = cos * sign
    return unit, inv, sin * f, sin * df + (n * (jnp.pi / RADIUS)) * cos * f


def make_table(table, embed, tab_ref):
    species, width = embed.shape
    columns = table.shape[1]
    parts = []
    for c in range(3):
        p = jnp.broadcast_to(table[c : c + 1], (8, columns))
        h = high(p)
        m = high(p - h)
        parts += [h, m, p - h - m]
    kind = jnp.broadcast_to(table[3:4], (species, columns))
    onehot = (
        kind == (lax.broadcasted_iota(jnp.int32, (species, columns), 0) + 1).astype(F32)
    ).astype(F32)
    h0 = hdot_t(embed, onehot)
    h0_hi = high(h0)
    zero = jnp.zeros((8, columns), F32)
    tab_ref[...] = jnp.concatenate([h0_hi, h0 - h0_hi] + parts + [zero], axis=0).astype(BF16)
    return h0


def gathered(g, width):
    base = 2 * width
    far = [
        g[base + 24 * c : base + 24 * c + 8]
        + g[base + 24 * c + 8 : base + 24 * c + 16]
        + g[base + 24 * c + 16 : base + 24 * c + 24]
        for c in range(3)
    ]
    return far, g[:width] + g[width:base]


def edge_geometry(far, own, counts, tiles):
    centre = [jnp.concatenate([spread_rows(own[c : c + 1], 8)] * tiles, axis=1) for c in range(3)]
    valid = jnp.concatenate([(counts > F32(k)).astype(F32) for k in range(tiles)], axis=1)
    return geometry(far, centre, valid)


def messages(w, h, unit, width, tiles):
    atoms = 128
    wa = w[:width] * h
    wb = w[width:] * h
    a_sum = jnp.zeros((width, atoms), F32)
    b_sum = [jnp.zeros((width, atoms), F32) for _ in range(3)]
    for k in range(tiles):
        a_sum = a_sum + wa[:, slot(k)]
        for c in range(3):
            b_sum[c] = b_sum[c] + wb[:, slot(k)] * tile8(unit[c][:, slot(k)], width // 8)
    return a_sum, b_sum


def tile8(x, times):
    return jnp.concatenate([x] * times, axis=0)


def mixed_pre(a, b_all, h0_own, mix_ref):
    atoms = a.shape[1]
    sq = b_all * b_all
    q = sq[:, :atoms] + sq[:, atoms : 2 * atoms] + sq[:, 2 * atoms :]
    return hdot_t(mix_ref[0], a) + hdot_t(mix_ref[1], h0_own) + hdot_t(mix_ref[2], q)


def features(pre, b_all, vec):
    atoms = pre.shape[1]
    v1 = hdot_t(vec, b_all)
    return (
        jnp.concatenate([pre * sigmoid(pre), v1[:, :atoms]], axis=0),
        jnp.concatenate([v1[:, atoms : 2 * atoms], v1[:, 2 * atoms :]], axis=0),
    )


def doubled(x):
    rows = x.shape[0]
    low = lane_low(rows)
    other = roll64(x)
    return jnp.where(low == parity_odd(rows), x, other)


def layer_one_kernel(
    sent_ref,
    come_ref,
    sel_ref,
    embed_ref,
    win_ref,
    wmid_ref,
    wout_ref,
    mix_ref,
    vec_ref,
    feats_ref,
    far_feats_ref,
    near_out,
    htab_ref,
    ftab_ref,
    geom_ref,
    basis_ref,
    pre_ref,
    b_ref,
    there_ref,
    sel_far_ref,
    tab_ref,
):
    atoms = sent_ref.shape[1]
    slots = sel_ref.shape[1] // atoms
    tiles = slots // 2
    width = embed_ref.shape[1]
    embed = embed_ref[...]
    scale = 1.0 / jnp.sqrt(F32(slots))
    ours = far_lanes(4)
    own = sent_ref[0:4]
    near = sent_ref[4:8]
    me = jnp.full(sent_ref.shape, lax.axis_index("space"), jnp.int32)
    has = jnp.logical_and(me > 0, me < lax.axis_size("space") - 1)
    there = jnp.where(parity_odd(sent_ref.shape[0]), come_ref[1], come_ref[0])
    there = jnp.where(has, there, jnp.zeros(sent_ref.shape, F32))
    there_ref[...] = there
    low12 = lane_low(tiles)
    lists = there[8 : 8 + slots]
    first = lists[:tiles]
    second = lists[tiles:]
    odd12 = parity_odd(tiles)
    build_selector(
        jnp.where(
            low12,
            jnp.where(odd12, first, roll64(first)),
            jnp.where(odd12, roll64(second), second),
        ),
        sel_far_ref,
    )
    h0 = make_table(
        jnp.concatenate([own, jnp.where(ours, there[0:4], near)], axis=1), embed, tab_ref
    )
    h0_far = make_table(
        jnp.concatenate([there[0:4], jnp.where(ours, there[4:8], own)], axis=1), embed, ftab_ref
    )
    htab_ref[...] = tab_ref[0 : 2 * width, :]
    g = bdot(tab_ref[...], sel_ref[...])
    gf = bdot(ftab_ref[...], sel_far_ref[...])

    far, h_far = gathered(g, width)
    counts = spread_rows(sent_ref[8 + slots : 9 + slots, :], 8)
    unit, inv, b, db = edge_geometry(far, own, counts, slots)
    for i, x in enumerate(unit + [inv]):
        geom_ref[i : i + 1, :] = x[0:1]
    basis_ref[0] = b
    basis_ref[1] = db
    far, far_h = gathered(gf, width)
    half = doubled(there)
    counts = spread_rows(half[8 + slots : 9 + slots], 8) - jnp.where(
        lane_low(8), F32(0), F32(tiles)
    )
    far_unit, _, far_b, _ = edge_geometry(far, half, counts, tiles)

    win, wmid, wout = win_ref[0], wmid_ref[0], wout_ref[0]
    w = radial(win, wmid, wout, b)
    wf = radial(win, wmid, wout, far_b)
    a, b = messages(w, h_far, unit, width, slots)
    b_all = jnp.concatenate(b, axis=1) * scale
    pre = mixed_pre(a * scale, b_all, h0[:, :atoms], mix_ref)
    pre_ref[...] = pre
    b_ref[...] = b_all
    vec = vec_ref[...]
    lo_part, hi_part = features(pre, b_all, vec)
    feats_ref[0 : 2 * width] = lo_part
    feats_ref[2 * width :] = hi_part
    low_lanes, high_lanes = packed(lo_part, hi_part)
    near_out[...] = jnp.where(parity_odd(2 * width), low_lanes, high_lanes)

    a, b = messages(wf, far_h, far_unit, width, tiles)
    a = (a + roll64(a)) * scale
    b_all = jnp.concatenate([x + roll64(x) for x in b], axis=1) * scale
    pre = mixed_pre(a, b_all, doubled(h0_far[:, :atoms]), mix_ref)
    lo_part, hi_part = features(pre, b_all, vec)
    far_feats_ref[0 : 2 * width] = lo_part
    far_feats_ref[2 * width :] = hi_part


def packed(lo_part, hi_part):
    low = lane_low(lo_part.shape[0])
    return (
        jnp.where(low, lo_part, roll64(hi_part)),
        jnp.where(low, roll64(lo_part), hi_part),
    )


def unpacked(tile, high_half):
    other = roll64(tile)
    return jnp.where(high_half, other, tile), jnp.where(high_half, tile, other)


def radial_two_kernel(basis_ref, win_ref, wmid_ref, wout_ref, w_ref, dw_ref):
    w, dw = radial_pair(win_ref[1], wmid_ref[1], wout_ref[1], basis_ref[0], basis_ref[1])
    w_ref[...] = w
    dw_ref[...] = dw


def edge_gradient(unit, inv, drho, du):
    dot = unit[0] * du[0] + unit[1] * du[1] + unit[2] * du[2]
    radial_part = drho - dot * inv
    return [unit[c] * radial_part + du[c] * inv for c in range(3)]


def sum_groups(x):
    total = x[0:8]
    for i in range(1, x.shape[0] // 8):
        total = total + x[8 * i : 8 * i + 8]
    return total


def put_positions(ref, base, grads):
    x = jnp.concatenate(list(grads), axis=0)
    hi, lo = split(x)
    ref[base : base + 24] = hi
    ref[base + 24 : base + 48] = lo


def rows8(x):
    sums = [jnp.sum(x[8 * c : 8 * c + 8], axis=0, keepdims=True) for c in range(3)]
    return jnp.concatenate(sums + [jnp.zeros((5, x.shape[1]), F32)], axis=0)


def centre_sum(grads, slots):
    x = jnp.concatenate(list(grads), axis=0)
    total = x[:, slot(0)]
    for k in range(1, slots):
        total = total + x[:, slot(k)]
    return total


def layer_two_kernel(
    feats_ref,
    far_feats_ref,
    near_ref,
    sel_ref,
    geom_ref,
    w_ref,
    dw_ref,
    mix_ref,
    read_ref,
    energy_ref,
    gown_ref,
    gghost_ref,
    near_out,
    far_out,
    gpos_ref,
    gpos_ghost_ref,
    grad_scr,
):
    atoms = feats_ref.shape[1]
    width = mix_ref.shape[1]
    slots = sel_ref.shape[1] // atoms
    rows = 2 * width
    odd = parity_odd(rows)
    ours = far_lanes(rows)
    near_lo, near_hi = unpacked(near_ref[...], odd)
    g_lo = jnp.where(ours, far_feats_ref[0:rows], near_lo)
    g_hi = jnp.where(ours, far_feats_ref[rows:], near_hi)
    feats = feats_ref[...]
    table = jnp.concatenate([feats, jnp.concatenate([g_lo, g_hi], axis=0)], axis=1)
    t_hi, t_lo = split(table)
    g = bdot(jnp.concatenate([t_hi, t_lo], axis=0), sel_ref[...])

    f = g[: 4 * width] + g[4 * width :]
    unit = [geom_ref[c : c + 1, :] for c in range(3)]
    along = f[width : 2 * width] * spread_rows(unit[0], width)
    along = along + f[2 * width : 3 * width] * spread_rows(unit[1], width)
    along = along + f[3 * width :] * spread_rows(unit[2], width)
    msg = w_ref[0:width] * f[:width] + w_ref[width:] * along
    m = jnp.zeros((width, atoms), F32)
    for k in range(slots):
        m = m + msg[:, slot(k)]
    scale = 1.0 / jnp.sqrt(F32(slots))
    s1 = feats[:width]
    pre = hdot_t(mix_ref[0], m * scale) + hdot_t(mix_ref[1], s1)
    sg = sigmoid(pre)
    s2 = pre * sg
    energy_ref[...] = hdot(read_ref[0:1], s1) + hdot(read_ref[1:2], s2)
    read = read_ref[...].T
    r_one = jnp.broadcast_to(read[:, 0:1], (width, atoms))
    r_two = jnp.broadcast_to(read[:, 1:2], (width, atoms))
    gpre = r_two * (sg + s2 * (1.0 - sg))
    gm = hdot(mix_ref[0], gpre) * scale
    gs_own = r_one + hdot(mix_ref[1], gpre)
    gm_rep = jnp.concatenate([gm] * slots, axis=1)
    ga = w_ref[0:width] * gm_rep
    gb = w_ref[width:] * gm_rep
    for i, x in enumerate([ga] + [gb * spread_rows(u, width) for u in unit]):
        hi, lo = split(x)
        grad_scr[i * width : (i + 1) * width] = hi
        grad_scr[(4 + i) * width : (5 + i) * width] = lo
    drho = gm_rep * (dw_ref[0:width] * f[:width] + dw_ref[width:] * along)
    du = [sum_groups(gb * f[(c + 1) * width : (c + 2) * width]) for c in range(3)]
    gp = edge_gradient(
        [spread_rows(u, 8) for u in unit],
        spread_rows(geom_ref[3:4, :], 8),
        sum_groups(drho),
        du,
    )
    put_positions(grad_scr, 8 * width, gp)
    centre = centre_sum(gp, slots)
    acc = bdot_nt(grad_scr[...], sel_ref[...])
    grads = acc[: 4 * width] + acc[4 * width : 8 * width]
    own = grads[:, :atoms]
    gown_ref[0:width] = own[0:width] + gs_own
    gown_ref[width:] = own[width:]
    ghost = grads[:, atoms:]
    gghost_ref[...] = ghost
    to_upper, to_lower = packed(ghost[:rows], ghost[rows:])
    near_out[...] = jnp.where(odd, to_lower, to_upper)
    far_out[...] = jnp.where(odd, to_upper, to_lower)
    pos = acc[8 * width : 8 * width + 24] + acc[8 * width + 24 :]
    gpos_ref[...] = rows8(pos[:, :atoms] - centre)
    gpos_ghost_ref[...] = rows8(pos[:, atoms:])


def join_kernel(gown_ref, near_ref, far_ref, gpos_ghost_ref, out_ref):
    rows = near_ref.shape[0]
    odd = parity_odd(rows)
    ours = far_lanes(rows)
    zero = jnp.zeros(near_ref.shape, F32)
    lo, hi = unpacked(near_ref[...], jnp.logical_not(odd))
    out_ref[0:rows] = gown_ref[0:rows] + jnp.where(ours, lo, zero)
    out_ref[rows : 2 * rows] = gown_ref[rows:] + jnp.where(ours, hi, zero)
    out_ref[2 * rows : 3 * rows] = far_ref[...]
    out_ref[3 * rows :] = gpos_ghost_ref[...]


def tangent_one_kernel(
    basis_ref,
    htab_ref,
    ftab_ref,
    sel_ref,
    there_ref,
    win_ref,
    wmid_ref,
    wout_ref,
    mix_ref,
    embed_ref,
    edge_ref,
    sel_ghost_ref,
    geom_ref,
    pre_ref,
    b_ref,
    sel_scr,
):
    atoms = there_ref.shape[1]
    width = htab_ref.shape[0] // 2
    slots = sel_ref.shape[1] // atoms
    win, wmid, wout = win_ref[0], wmid_ref[0], wout_ref[0]

    def store(domain, w, dw, h):
        edge_ref[domain, 0:width] = dw[:width] * h
        edge_ref[domain, width : 2 * width] = dw[width:] * h
        edge_ref[domain, 2 * width :] = w[width:] * h

    w, dw = radial_pair(win, wmid, wout, basis_ref[0], basis_ref[1])
    g = bdot(htab_ref[...], sel_ref[...])
    store(0, w, dw, g[:width] + g[width:])

    there = there_ref[...]
    build_selector(there[8 : 8 + slots], sel_scr)
    sel_ghost_ref[...] = sel_scr[atoms:]
    far, h = gathered(bdot(ftab_ref[...], sel_scr[...]), width)
    counts = spread_rows(there[8 + slots : 9 + slots], 8)
    unit, inv, b, db = edge_geometry(far, there, counts, slots)
    for i, x in enumerate(unit + [inv]):
        geom_ref[i : i + 1, :] = x[0:1]
    w, dw = radial_pair(win, wmid, wout, b, db)
    store(1, w, dw, h)
    a, b = messages(w, h, unit, width, slots)
    scale = 1.0 / jnp.sqrt(F32(slots))
    b_all = jnp.concatenate(b, axis=1) * scale
    species = embed_ref.shape[0]
    kind = jnp.broadcast_to(there[3:4], (species, atoms))
    onehot = (
        kind == (lax.broadcasted_iota(jnp.int32, (species, atoms), 0) + 1).astype(F32)
    ).astype(F32)
    pre_ref[...] = mixed_pre(a * scale, b_all, hdot_t(embed_ref[...], onehot), mix_ref)
    b_ref[...] = b_all


def back_one_kernel(
    sent_ref,
    far_ref,
    gghost_ref,
    sel_ref,
    sel_ghost_ref,
    geom_ref,
    far_geom_ref,
    edge_ref,
    pre_ref,
    far_pre_ref,
    b_ref,
    far_b_ref,
    mix_ref,
    vec_ref,
    gpos_ref,
    gown_out,
    ghost_out,
    pos_scr,
    far_pos_scr,
):
    atoms = gpos_ref.shape[1]
    width = mix_ref.shape[1]
    slots = sel_ref.shape[1] // atoms
    rows = 2 * width
    odd = parity_odd(rows)
    ours = far_lanes(rows)
    zero = jnp.zeros((rows, atoms), F32)
    scale = 1.0 / jnp.sqrt(F32(slots))
    lo, hi = unpacked(far_ref[2 * rows : 3 * rows], odd)
    g_lo = sent_ref[0:rows] + jnp.where(ours, zero, lo)
    g_hi = sent_ref[rows : 2 * rows] + jnp.where(ours, zero, hi)
    f_lo = far_ref[0:rows] + jnp.where(ours, gghost_ref[0:rows], zero)
    f_hi = far_ref[rows : 2 * rows] + jnp.where(ours, gghost_ref[rows:], zero)
    pre = jnp.concatenate([pre_ref[...], far_pre_ref[...]], axis=1)
    sg = sigmoid(pre)
    gpre = jnp.concatenate([g_lo[:width], f_lo[:width]], axis=1) * (sg + pre * sg * (1.0 - sg))
    ga = hdot(mix_ref[0], gpre) * scale
    gq = hdot(mix_ref[2], gpre) * (2.0 * scale)
    gv = jnp.concatenate(
        [g_lo[width:], g_hi[:width], g_hi[width:], f_lo[width:], f_hi[:width], f_hi[width:]],
        axis=1,
    )
    gb_all = hdot(vec_ref[...], gv) * scale
    b_of = [b_ref, far_b_ref]
    geom_of = [geom_ref, far_geom_ref]
    scr_of = [pos_scr, far_pos_scr]
    for domain in range(2):
        ga_d = ga[:, slot(domain)]
        gq_d = gq[:, slot(domain)]
        gb = [
            gb_all[:, slot(3 * domain + c)] + b_of[domain][:, slot(c)] * gq_d for c in range(3)
        ]
        geom = geom_of[domain]
        total = jnp.zeros((24, atoms), F32)
        for k in range(slots):
            unit = [spread_rows(geom[c : c + 1, slot(k)], 8) for c in range(3)]
            u = [tile8(x, width // 8) for x in unit]
            gbu = gb[0] * u[0] + gb[1] * u[1] + gb[2] * u[2]
            drho = (
                edge_ref[domain, 0:width, slot(k)] * ga_d
                + edge_ref[domain, width : 2 * width, slot(k)] * gbu
            )
            carried = edge_ref[domain, 2 * width :, slot(k)]
            du = [sum_groups(carried * gb[c]) for c in range(3)]
            gp = edge_gradient(unit, spread_rows(geom[3:4, slot(k)], 8), sum_groups(drho), du)
            x = jnp.concatenate(gp, axis=0)
            if domain == 0:
                total = total + x
            hi, lo = split(x)
            scr_of[domain][0:24, slot(k)] = hi
            scr_of[domain][24:48, slot(k)] = lo
        if domain == 0:
            centre = total
    acc = bdot_nt(pos_scr[...], sel_ref[...])
    pos = acc[0:24] + acc[24:48]
    ghost_out[...] = rows8(pos[:, atoms:]) + sent_ref[3 * rows :]
    acc = bdot_nt(far_pos_scr[...], sel_ghost_ref[...])
    there = rows8(acc[0:24] + acc[24:48]) + far_ref[3 * rows :]
    there = jnp.where(far_lanes(8), jnp.zeros((8, atoms), F32), there)
    gown_out[...] = gpos_ref[...] + rows8(pos[:, :atoms] - centre) + there


def call(kernel, out_shapes, args, scratch=(), flops=0, transcendentals=0, far_away=0):
    args = [
        pltpu.with_memory_space_constraint(x, pltpu.HBM) if i < far_away else x
        for i, x in enumerate(args)
    ]
    spaces = [pltpu.HBM] * far_away + [pltpu.VMEM] * (len(args) - far_away)
    moved = sum(x.size * x.dtype.itemsize for x in list(args) + list(out_shapes))
    return pl.pallas_call(
        kernel,
        out_shape=out_shapes,
        in_specs=[pl.BlockSpec(memory_space=space) for space in spaces],
        out_specs=[pl.BlockSpec(memory_space=pltpu.VMEM)] * len(out_shapes),
        scratch_shapes=list(scratch),
        cost_estimate=pl.CostEstimate(
            flops=flops, bytes_accessed=moved, transcendentals=transcendentals
        ),
        compiler_params=pltpu.CompilerParams(vmem_limit_bytes=36 * MIB),
    )(*args)


def shape(dims, dtype=F32):
    return jax.ShapeDtypeStruct(dims, dtype)


def body(
    positions,
    species,
    neighbours,
    counts,
    ghost_index,
    embed,
    radial_in,
    radial_mid,
    radial_out,
    mix_one,
    vec_mix,
    mix_two,
    readout,
):
    atoms = positions.shape[1]
    slots = neighbours.shape[0]
    edges = slots * atoms
    nbasis, hidden = radial_in.shape[1:]
    width = embed.shape[1]
    rows = 2 * width
    devices = lax.axis_size("space")
    near_route = [(i, i ^ 1) for i in range(devices)]
    far_route = [(i, ((i + 1) ^ 1) - 1) for i in range(1, devices - 1)]

    def swap_near(x):
        return lax.ppermute(x, "space", near_route)

    def swap_far(x):
        return lax.ppermute(x, "space", far_route)

    def scratch_of(args):
        return [pltpu.VMEM(x.shape, x.dtype) for x in args]

    def shapes_of(args):
        return [shape(x.shape, x.dtype) for x in args]

    near_pos = swap_near(positions)
    near_kind = swap_near(species)
    local = [positions, species[None], neighbours, ghost_index, counts[None]]
    weights = [radial_in, radial_mid, radial_out]
    passed = [embed, mix_one, vec_mix, mix_two, readout]
    moved = local + weights + passed
    own, edge_rows, sel, win, wmid, wout, embed, mix_one, vec_mix, mix_two, readout = call(
        prep_kernel,
        [
            shape((4, atoms)),
            shape((slots + 8, atoms)),
            shape((2 * atoms, edges), BF16),
            shape((2, hidden, 4 * nbasis), BF16),
            shape((2, hidden, 3 * hidden), BF16),
            shape((2, 2 * width, 3 * hidden), BF16),
        ]
        + shapes_of(passed),
        moved,
        scratch=scratch_of(local + weights)
        + [pltpu.VMEM((atoms, edges), BF16), pltpu.SemaphoreType.DMA((len(moved),))],
        flops=10**8,
        far_away=len(moved),
    )
    near_rows = [near_pos, (near_kind + 1).astype(F32)[None]]
    sent = jnp.concatenate([own] + near_rows + [edge_rows], axis=0)
    pairs = [[i, (i + 1) % devices] for i in range(1, devices, 2)]
    come = lax.all_gather(sent, "space", axis_index_groups=pairs)
    table_rows = 2 * width + 80
    feats, far_feats, near_f, htab, ftab, geom, basis, pre, b_all, there = call(
        layer_one_kernel,
        [
            shape((4 * width, atoms)),
            shape((4 * width, atoms)),
            shape((rows, atoms)),
            shape((2 * width, 2 * atoms), BF16),
            shape((table_rows, 2 * atoms), BF16),
            shape((8, edges)),
            shape((2, nbasis, edges)),
            shape((width, atoms)),
            shape((width, 3 * atoms)),
            shape((slots + 16, atoms)),
        ],
        [sent, come, sel, embed, win, wmid, wout, mix_one, vec_mix],
        scratch=[
            pltpu.VMEM((2 * atoms, edges // 2), BF16),
            pltpu.VMEM((table_rows, 2 * atoms), BF16),
        ],
        flops=2 * 10**9,
    )
    near_f = swap_near(near_f)
    w, dw = call(
        radial_two_kernel,
        [shape((2 * width, edges)), shape((2 * width, edges))],
        [basis, win, wmid, wout],
        flops=2 * 10**9,
    )
    energy, g_own, g_ghost, near_g, far_g, gpos, gpos_ghost = call(
        layer_two_kernel,
        [
            shape((1, atoms)),
            shape((4 * width, atoms)),
            shape((4 * width, atoms)),
            shape((rows, atoms)),
            shape((rows, atoms)),
            shape((8, atoms)),
            shape((8, atoms)),
        ],
        [feats, far_feats, near_f, sel, geom, w, dw, mix_two, readout],
        scratch=[pltpu.VMEM((8 * width + 48, edges), BF16)],
        flops=10**9,
    )
    near_g = swap_near(near_g)
    (sent,) = call(
        join_kernel, [shape((3 * rows + 8, atoms))], [g_own, near_g, far_g, gpos_ghost]
    )
    come = swap_far(sent)
    edge, sel_ghost, far_geom, far_pre, far_b = call(
        tangent_one_kernel,
        [
            shape((2, 3 * width, edges)),
            shape((atoms, edges), BF16),
            shape((8, edges)),
            shape((width, atoms)),
            shape((width, 3 * atoms)),
        ],
        [basis, htab, ftab, sel, there, win, wmid, wout, mix_one, embed],
        scratch=[pltpu.VMEM((2 * atoms, edges), BF16)],
        flops=4 * 10**9,
    )
    centre, ghost = call(
        back_one_kernel,
        [shape((8, atoms)), shape((8, atoms))],
        [
            sent,
            come,
            g_ghost,
            sel,
            sel_ghost,
            geom,
            far_geom,
            edge,
            pre,
            far_pre,
            b_all,
            far_b,
            mix_one,
            vec_mix,
            gpos,
        ],
        scratch=[pltpu.VMEM((48, edges), BF16), pltpu.VMEM((48, edges), BF16)],
        flops=10**9,
    )
    near_p = swap_near(ghost)
    odd = lax.rem(lax.axis_index("space"), 2) == 1
    low = lax.broadcasted_iota(jnp.int32, (3, atoms), 1) < HALF
    back = jnp.where(low == odd, near_p[:3], 0.0)
    return (energy[0], -(centre[:3] + back))


def solution(mesh):
    placed = (
        P(None, "space"),
        P("space"),
        P(None, "space"),
        P("space"),
        P(None, "space"),
        P(),
        P(),
        P(),
        P(),
        P(),
        P(),
        P(),
        P(),
    )
    return jax.shard_map(
        body, mesh=mesh, in_specs=placed, out_specs=(P("space"), P(None, "space")), check_vma=False
    )
```

```python
import jax
import jax.numpy as jnp
from jax import lax
from jax.experimental import pallas as pl
from jax.experimental.pallas import tpu as pltpu
from jax.sharding import PartitionSpec as P

RADIUS = 5.0
SOFTEN = 0.25
F32 = jnp.float32
BF16 = jnp.bfloat16
HALF = 64
MIB = 1024 * 1024


def hdot(a, b, dims=(((1,), (0,)), ((), ()))):
    return lax.dot_general(
        a, b, dims, precision=lax.Precision.HIGHEST, preferred_element_type=F32
    )


def hdot_t(a, b):
    return hdot(a, b, (((0,), (0,)), ((), ())))


def bdot(a, b):
    return jnp.dot(a, b, preferred_element_type=F32)


def bdot_nt(a, b):
    return lax.dot_general(a, b, (((1,), (1,)), ((), ())), preferred_element_type=F32)


def high(x):
    return x.astype(BF16).astype(F32)


def split(x):
    hi = x.astype(BF16)
    return hi, (x - hi.astype(F32)).astype(BF16)


def stack3(x):
    hi, lo = split(x)
    return jnp.concatenate([hi, lo, hi], axis=0)


def slot(k):
    return slice(k * 128, (k + 1) * 128)


def sigmoid(v):
    return 0.5 + 0.5 * jnp.tanh(0.5 * v)


def roll64(x):
    return pltpu.roll(x, HALF, 1)


def lane_low(rows):
    return lax.broadcasted_iota(jnp.int32, (rows, 128), 1) < HALF


def parity_odd(rows):
    odd = lax.rem(lax.axis_index("space"), 2)
    return jnp.full((rows, 128), odd, jnp.int32) > 0


def far_lanes(rows):
    return parity_odd(rows) == lane_low(rows)


def copy_in(moves, sems):
    copies = [
        pltpu.make_async_copy(src, dst, sems.at[i]) for i, (src, dst) in enumerate(moves)
    ]
    for c in copies:
        c.start()
    for c in copies:
        c.wait()


def put_lists(nb_ref, gi_ref, counts_ref, out_ref, hot_ref):
    slots, atoms = nb_ref.shape
    rows = (lax.broadcasted_iota(jnp.int32, (atoms, atoms), 0) + atoms).astype(F32).astype(BF16)
    one = jnp.ones((atoms, atoms), BF16)
    zero = jnp.zeros((atoms, atoms), BF16)
    for k in range(slots):
        nb = jnp.broadcast_to(nb_ref[k : k + 1, :].astype(F32), (16, atoms)).astype(BF16)
        nb = jnp.concatenate([nb] * (atoms // 16), axis=0)
        hot_ref[:, slot(k)] = jnp.where(rows == nb, one, zero)
    place = jnp.concatenate(
        [jnp.broadcast_to(gi_ref[i : i + 1, :], (16, HALF)).astype(F32) for i in range(2)], axis=1
    )
    ghost = bdot(place.astype(BF16), hot_ref[...])
    for k in range(slots):
        nb = nb_ref[k : k + 1, :]
        out_ref[k : k + 1, :] = jnp.where(
            nb < atoms, nb.astype(F32), ghost[0:1, slot(k)] + F32(atoms)
        )
    out_ref[slots : slots + 1, :] = counts_ref[...].astype(F32)
    out_ref[slots + 1 :, :] = jnp.zeros((out_ref.shape[0] - slots - 1, atoms), F32)


def build_selector(rows_f32, sel_ref):
    count, atoms = rows_f32.shape
    rows = lax.broadcasted_iota(jnp.int32, (2 * atoms, atoms), 0).astype(F32).astype(BF16)
    one = jnp.ones((2 * atoms, atoms), BF16)
    zero = jnp.zeros((2 * atoms, atoms), BF16)
    for k in range(count):
        nb = jnp.broadcast_to(rows_f32[k : k + 1, :], (16, atoms)).astype(BF16)
        nb = jnp.concatenate([nb] * (atoms // 8), axis=0)
        sel_ref[:, slot(k)] = jnp.where(rows == nb, one, zero)


def prep_kernel(
    pos_hbm,
    kind_hbm,
    nb_hbm,
    gi_hbm,
    counts_hbm,
    rin_hbm,
    rmid_hbm,
    rout_hbm,
    embed_hbm,
    mix_one_hbm,
    vec_hbm,
    mix_two_hbm,
    read_hbm,
    own_ref,
    edges_ref,
    sel_ref,
    win_ref,
    wmid_ref,
    wout_ref,
    embed_ref,
    mix_one_ref,
    vec_ref,
    mix_two_ref,
    read_ref,
    pos_ref,
    kind_ref,
    nb_ref,
    gi_ref,
    counts_ref,
    rin_ref,
    rmid_ref,
    rout_ref,
    hot_ref,
    sems,
):
    copy_in(
        [
            (pos_hbm, pos_ref),
            (kind_hbm, kind_ref),
            (nb_hbm, nb_ref),
            (gi_hbm, gi_ref),
            (counts_hbm, counts_ref),
            (rin_hbm, rin_ref),
            (rmid_hbm, rmid_ref),
            (rout_hbm, rout_ref),
            (embed_hbm, embed_ref),
            (mix_one_hbm, mix_one_ref),
            (vec_hbm, vec_ref),
            (mix_two_hbm, mix_two_ref),
            (read_hbm, read_ref),
        ],
        sems,
    )
    own_ref[0:3, :] = pos_ref[...]
    own_ref[3:4, :] = (kind_ref[...] + 1).astype(F32)
    put_lists(nb_ref, gi_ref, counts_ref, edges_ref, hot_ref)
    build_selector(edges_ref[0 : nb_ref.shape[0], :], sel_ref)
    for layer in range(2):
        w = rin_ref[layer]
        h = high(w)
        lo = w - h
        win_ref[layer] = jnp.concatenate([h, h, lo, lo], axis=0).T.astype(BF16)
        w = rmid_ref[layer]
        h = high(w)
        wmid_ref[layer] = jnp.concatenate([h, h, w - h], axis=0).T.astype(BF16)
        w = rout_ref[layer]
        h = high(w)
        wout_ref[layer] = jnp.concatenate([h, h, w - h], axis=0).T.astype(BF16)


def basis_rows(b):
    h = high(b)
    lo = b - h
    return jnp.concatenate([h, lo, h, lo], axis=0).astype(BF16)


def radial(win, wmid, wout, b):
    v1 = bdot(win, basis_rows(b))
    v2 = bdot(wmid, stack3(v1 * sigmoid(v1)))
    return bdot(wout, stack3(v2 * sigmoid(v2)))


def silu_pair(v, t):
    s = sigmoid(v)
    z = v * s
    return z, (s + z * (1.0 - s)) * t


def radial_pair(win, wmid, wout, b, db):
    z1, t1 = silu_pair(bdot(win, basis_rows(b)), bdot(win, basis_rows(db)))
    z2, t2 = silu_pair(bdot(wmid, stack3(z1)), bdot(wmid, stack3(t1)))
    return bdot(wout, stack3(z2)), bdot(wout, stack3(t2))


def spread_rows(row, rows):
    return jnp.broadcast_to(row, (rows, row.shape[1]))


def geometry(far, own, valid):
    vec = [f - o for f, o in zip(far, own)]
    r2 = vec[0] * vec[0] + vec[1] * vec[1] + vec[2] * vec[2] + SOFTEN
    inv = lax.rsqrt(r2)
    inv = inv * (1.5 - 0.5 * r2 * inv * inv)
    rho = r2 * inv
    unit = [v * inv for v in vec]
    x = jnp.minimum(rho * (1.0 / RADIUS), 1.0)
    y = 1.0 - x
    x2 = x * x
    env = y * y * y * (1.0 + x * (3.0 + x * (6.0 + x * (10.0 + x * 15.0))))
    denv = (-105.0 / RADIUS) * x2 * x2 * y * y
    f = RADIUS * inv * env * valid
    df = RADIUS * inv * (denv - env * inv) * valid
    n = (lax.broadcasted_iota(jnp.int32, rho.shape, 0) + 1).astype(F32)
    turns = n * x
    whole = jnp.floor(turns + 0.5)
    frac = (turns - whole) * jnp.pi
    parity = whole - 2.0 * jnp.floor(0.5 * whole)
    sign = 1.0 - 2.0 * parity
    q = frac * frac
    sin = frac * (
        1.0
        + q * (-1 / 6 + q * (1 / 120 + q * (-1 / 5040 + q * (1 / 362880 + q * (-1 / 39916800)))))
    )
    cos = 1.0 + q * (
        -1 / 2
        + q * (1 / 24 + q * (-1 / 720 + q * (1 / 40320 + q * (-1 / 3628800 + q * (1 / 479001600)))))
    )
    sin = sin * sign
    cos = cos * sign
    return unit, inv, sin * f, sin * df + (n * (jnp.pi / RADIUS)) * cos * f


def kinds(row, species):
    n = row.shape[1]
    numbers = (lax.broadcasted_iota(jnp.int32, (8, n), 0) + 1).astype(F32)
    return jnp.logical_and(spread_rows(row, 8) == numbers, numbers <= F32(species)).astype(F32)


def make_table(table, species, tab_ref):
    parts = []
    for c in range(3):
        p = table[c : c + 1]
        h = high(p)
        m = high(p - h)
        parts += [h, m, p - h - m]
    pad = jnp.zeros((7, table.shape[1]), F32)
    rows = parts + [pad, kinds(table[3:4], species), pad, pad[0:1]]
    tab_ref[...] = jnp.concatenate(rows, axis=0).astype(BF16)


def embed_rows(embed):
    species, width = embed.shape
    e = jnp.concatenate([embed, jnp.zeros((8 - species, width), F32)], axis=0)
    h = high(e)
    return jnp.concatenate([h, e - h], axis=0).T.astype(BF16)


def far_kinds(g, emb):
    hot = g[16:24]
    return bdot(emb, jnp.concatenate([hot, hot], axis=0).astype(BF16))


def far_positions(g):
    return [
        spread_rows(g[3 * c : 3 * c + 1], 8)
        + spread_rows(g[3 * c + 1 : 3 * c + 2], 8)
        + spread_rows(g[3 * c + 2 : 3 * c + 3], 8)
        for c in range(3)
    ]


def edge_geometry(far, own, counts, tiles):
    centre = [jnp.concatenate([spread_rows(own[c : c + 1], 8)] * tiles, axis=1) for c in range(3)]
    valid = jnp.concatenate([(counts > F32(k)).astype(F32) for k in range(tiles)], axis=1)
    return geometry(far, centre, valid)


def messages(w, h, unit, width, tiles):
    atoms = 128
    wa = w[:width] * h
    wb = w[width:] * h
    a_sum = jnp.zeros((width, atoms), F32)
    b_sum = [jnp.zeros((width, atoms), F32) for _ in range(3)]
    for k in range(tiles):
        a_sum = a_sum + wa[:, slot(k)]
        for c in range(3):
            b_sum[c] = b_sum[c] + wb[:, slot(k)] * tile8(unit[c][:, slot(k)], width // 8)
    return a_sum, b_sum


def tile8(x, times):
    return jnp.concatenate([x] * times, axis=0)


def mixed_pre(a, b_all, h0_own, mix_ref):
    atoms = a.shape[1]
    sq = b_all * b_all
    q = sq[:, :atoms] + sq[:, atoms : 2 * atoms] + sq[:, 2 * atoms :]
    return hdot_t(mix_ref[0], a) + hdot_t(mix_ref[1], h0_own) + hdot_t(mix_ref[2], q)


def features(pre, b_all, vec):
    atoms = pre.shape[1]
    v1 = hdot_t(vec, b_all)
    return (
        jnp.concatenate([pre * sigmoid(pre), v1[:, :atoms]], axis=0),
        jnp.concatenate([v1[:, atoms : 2 * atoms], v1[:, 2 * atoms :]], axis=0),
    )


def doubled(x):
    rows = x.shape[0]
    low = lane_low(rows)
    other = roll64(x)
    return jnp.where(low == parity_odd(rows), x, other)


def layer_one_kernel(
    sent_ref,
    come_ref,
    sel_ref,
    embed_ref,
    win_ref,
    wmid_ref,
    wout_ref,
    mix_ref,
    vec_ref,
    feats_ref,
    far_feats_ref,
    near_out,
    tab_ref,
    ftab_ref,
    emb_ref,
    geom_ref,
    basis_ref,
    pre_ref,
    b_ref,
    there_ref,
    sel_far_ref,
):
    atoms = sent_ref.shape[1]
    slots = sel_ref.shape[1] // atoms
    tiles = slots // 2
    width = embed_ref.shape[1]
    embed = embed_ref[...]
    scale = 1.0 / jnp.sqrt(F32(slots))
    ours = far_lanes(4)
    own = sent_ref[0:4]
    near = sent_ref[4:8]
    me = jnp.full(sent_ref.shape, lax.axis_index("space"), jnp.int32)
    has = jnp.logical_and(me > 0, me < lax.axis_size("space") - 1)
    there = jnp.where(parity_odd(sent_ref.shape[0]), come_ref[1], come_ref[0])
    there = jnp.where(has, there, jnp.zeros(sent_ref.shape, F32))
    there_ref[...] = there
    low12 = lane_low(tiles)
    lists = there[8 : 8 + slots]
    first = lists[:tiles]
    second = lists[tiles:]
    odd12 = parity_odd(tiles)
    build_selector(
        jnp.where(
            low12,
            jnp.where(odd12, first, roll64(first)),
            jnp.where(odd12, roll64(second), second),
        ),
        sel_far_ref,
    )
    species = embed.shape[0]
    make_table(
        jnp.concatenate([own, jnp.where(ours, there[0:4], near)], axis=1), species, tab_ref
    )
    make_table(
        jnp.concatenate([there[0:4], jnp.where(ours, there[4:8], own)], axis=1), species, ftab_ref
    )
    emb = embed_rows(embed)
    emb_ref[...] = emb
    h0 = hdot_t(embed, kinds(own[3:4], species)[:species])
    h0_far = hdot_t(embed, kinds(doubled(there[0:8])[3:4], species)[:species])
    g = bdot(tab_ref[...], sel_ref[...])
    gf = bdot(ftab_ref[...], sel_far_ref[...])

    edges = slots * atoms
    half = doubled(there)
    far = [jnp.concatenate(x, axis=1) for x in zip(far_positions(g), far_positions(gf))]
    centre = [
        jnp.concatenate(
            [spread_rows(own[c : c + 1], 8)] * slots + [spread_rows(half[c : c + 1], 8)] * tiles,
            axis=1,
        )
        for c in range(3)
    ]
    counts = spread_rows(sent_ref[8 + slots : 9 + slots, :], 8)
    far_counts = spread_rows(half[8 + slots : 9 + slots], 8) - jnp.where(
        lane_low(8), F32(0), F32(tiles)
    )
    valid = jnp.concatenate(
        [(counts > F32(k)).astype(F32) for k in range(slots)]
        + [(far_counts > F32(k)).astype(F32) for k in range(tiles)],
        axis=1,
    )
    unit, inv, b, db = geometry(far, centre, valid)
    for i, x in enumerate(unit + [inv]):
        geom_ref[i : i + 1, :] = x[0:1, :edges]
    basis_ref[0] = b[:, :edges]
    basis_ref[1] = db[:, :edges]
    hot = jnp.concatenate([g[16:24], gf[16:24]], axis=1)
    h = bdot(emb, jnp.concatenate([hot, hot], axis=0).astype(BF16))
    w = radial(win_ref[0], wmid_ref[0], wout_ref[0], b)
    wa = w[:width] * h
    wb = w[width:] * h

    def summed(first, count):
        sums = [jnp.zeros((width, atoms), F32) for _ in range(4)]
        for k in range(first, first + count):
            x = wb[:, slot(k)]
            sums[0] = sums[0] + wa[:, slot(k)]
            for c in range(3):
                sums[c + 1] = sums[c + 1] + x * tile8(unit[c][:, slot(k)], width // 8)
        return sums

    ours_sum = summed(0, slots)
    theirs = [x + roll64(x) for x in summed(slots, tiles)]
    both = [jnp.concatenate([x, y], axis=1) * scale for x, y in zip(ours_sum, theirs)]
    q = both[1] * both[1] + both[2] * both[2] + both[3] * both[3]
    pre = (
        hdot_t(mix_ref[0], both[0])
        + hdot_t(mix_ref[1], jnp.concatenate([h0, h0_far], axis=1))
        + hdot_t(mix_ref[2], q)
    )
    pre_ref[...] = pre[:, :atoms]
    for c in range(3):
        b_ref[:, slot(c)] = both[c + 1][:, :atoms]
    s1 = pre * sigmoid(pre)
    v1 = hdot_t(vec_ref[...], jnp.concatenate(both[1:], axis=1))
    for domain, ref in ((0, feats_ref), (1, far_feats_ref)):
        ref[0:width] = s1[:, slot(domain)]
        for c in range(3):
            ref[(c + 1) * width : (c + 2) * width] = v1[:, slot(2 * c + domain)]
    low_lanes, high_lanes = packed(feats_ref[0 : 2 * width], feats_ref[2 * width :])
    near_out[...] = jnp.where(parity_odd(2 * width), low_lanes, high_lanes)


def packed(lo_part, hi_part):
    low = lane_low(lo_part.shape[0])
    return (
        jnp.where(low, lo_part, roll64(hi_part)),
        jnp.where(low, roll64(lo_part), hi_part),
    )


def unpacked(tile, high_half):
    other = roll64(tile)
    return jnp.where(high_half, other, tile), jnp.where(high_half, tile, other)


def radial_two_kernel(basis_ref, win_ref, wmid_ref, wout_ref, w_ref, dw_ref):
    w, dw = radial_pair(win_ref[1], wmid_ref[1], wout_ref[1], basis_ref[0], basis_ref[1])
    w_ref[...] = w
    dw_ref[...] = dw


def edge_gradient(unit, inv, drho, du):
    dot = unit[0] * du[0] + unit[1] * du[1] + unit[2] * du[2]
    radial_part = drho - dot * inv
    return [unit[c] * radial_part + du[c] * inv for c in range(3)]


def sum_groups(x):
    total = x[0:8]
    for i in range(1, x.shape[0] // 8):
        total = total + x[8 * i : 8 * i + 8]
    return total


def put_positions(ref, base, grads):
    x = jnp.concatenate(list(grads), axis=0)
    hi, lo = split(x)
    ref[base : base + 24] = hi
    ref[base + 24 : base + 48] = lo


def rows8(x):
    sums = [jnp.sum(x[8 * c : 8 * c + 8], axis=0, keepdims=True) for c in range(3)]
    return jnp.concatenate(sums + [jnp.zeros((5, x.shape[1]), F32)], axis=0)


def centre_sum(grads, slots):
    x = jnp.concatenate(list(grads), axis=0)
    total = x[:, slot(0)]
    for k in range(1, slots):
        total = total + x[:, slot(k)]
    return total


def layer_two_kernel(
    feats_ref,
    far_feats_ref,
    near_ref,
    sel_ref,
    geom_ref,
    w_ref,
    dw_ref,
    mix_ref,
    read_ref,
    energy_ref,
    gown_ref,
    gghost_ref,
    near_out,
    far_out,
    gpos_ref,
    gpos_ghost_ref,
    grad_scr,
):
    atoms = feats_ref.shape[1]
    width = mix_ref.shape[1]
    slots = sel_ref.shape[1] // atoms
    rows = 2 * width
    odd = parity_odd(rows)
    ours = far_lanes(rows)
    near_lo, near_hi = unpacked(near_ref[...], odd)
    g_lo = jnp.where(ours, far_feats_ref[0:rows], near_lo)
    g_hi = jnp.where(ours, far_feats_ref[rows:], near_hi)
    feats = feats_ref[...]
    table = jnp.concatenate([feats, jnp.concatenate([g_lo, g_hi], axis=0)], axis=1)
    t_hi, t_lo = split(table)
    g = bdot(jnp.concatenate([t_hi, t_lo], axis=0), sel_ref[...])

    f = g[: 4 * width] + g[4 * width :]
    unit = [geom_ref[c : c + 1, :] for c in range(3)]
    along = f[width : 2 * width] * spread_rows(unit[0], width)
    along = along + f[2 * width : 3 * width] * spread_rows(unit[1], width)
    along = along + f[3 * width :] * spread_rows(unit[2], width)
    msg = w_ref[0:width] * f[:width] + w_ref[width:] * along
    m = jnp.zeros((width, atoms), F32)
    for k in range(slots):
        m = m + msg[:, slot(k)]
    scale = 1.0 / jnp.sqrt(F32(slots))
    s1 = feats[:width]
    pre = hdot_t(mix_ref[0], m * scale) + hdot_t(mix_ref[1], s1)
    sg = sigmoid(pre)
    s2 = pre * sg
    energy_ref[...] = hdot(read_ref[0:1], s1) + hdot(read_ref[1:2], s2)
    read = read_ref[...].T
    r_one = jnp.broadcast_to(read[:, 0:1], (width, atoms))
    r_two = jnp.broadcast_to(read[:, 1:2], (width, atoms))
    gpre = r_two * (sg + s2 * (1.0 - sg))
    gm = hdot(mix_ref[0], gpre) * scale
    gs_own = r_one + hdot(mix_ref[1], gpre)
    gm_rep = jnp.concatenate([gm] * slots, axis=1)
    ga = w_ref[0:width] * gm_rep
    gb = w_ref[width:] * gm_rep
    for i, x in enumerate([ga] + [gb * spread_rows(u, width) for u in unit]):
        hi, lo = split(x)
        grad_scr[i * width : (i + 1) * width] = hi
        grad_scr[(4 + i) * width : (5 + i) * width] = lo
    drho = gm_rep * (dw_ref[0:width] * f[:width] + dw_ref[width:] * along)
    du = [sum_groups(gb * f[(c + 1) * width : (c + 2) * width]) for c in range(3)]
    gp = edge_gradient(
        [spread_rows(u, 8) for u in unit],
        spread_rows(geom_ref[3:4, :], 8),
        sum_groups(drho),
        du,
    )
    put_positions(grad_scr, 8 * width, gp)
    centre = centre_sum(gp, slots)
    acc = bdot_nt(grad_scr[...], sel_ref[...])
    grads = acc[: 4 * width] + acc[4 * width : 8 * width]
    own = grads[:, :atoms]
    gown_ref[0:width] = own[0:width] + gs_own
    gown_ref[width:] = own[width:]
    ghost = grads[:, atoms:]
    gghost_ref[...] = ghost
    to_upper, to_lower = packed(ghost[:rows], ghost[rows:])
    near_out[...] = jnp.where(odd, to_lower, to_upper)
    far_out[...] = jnp.where(odd, to_upper, to_lower)
    pos = acc[8 * width : 8 * width + 24] + acc[8 * width + 24 :]
    gpos_ref[...] = rows8(pos[:, :atoms] - centre)
    gpos_ghost_ref[...] = rows8(pos[:, atoms:])


def join_kernel(gown_ref, near_ref, far_ref, gpos_ghost_ref, out_ref):
    rows = near_ref.shape[0]
    odd = parity_odd(rows)
    ours = far_lanes(rows)
    zero = jnp.zeros(near_ref.shape, F32)
    lo, hi = unpacked(near_ref[...], jnp.logical_not(odd))
    out_ref[0:rows] = gown_ref[0:rows] + jnp.where(ours, lo, zero)
    out_ref[rows : 2 * rows] = gown_ref[rows:] + jnp.where(ours, hi, zero)
    out_ref[2 * rows : 3 * rows] = far_ref[...]
    out_ref[3 * rows :] = gpos_ghost_ref[...]


def tangent_one_kernel(
    basis_ref,
    tab_ref,
    ftab_ref,
    emb_ref,
    sel_ref,
    there_ref,
    win_ref,
    wmid_ref,
    wout_ref,
    mix_ref,
    embed_ref,
    edge_ref,
    sel_ghost_ref,
    geom_ref,
    pre_ref,
    b_ref,
    sel_scr,
):
    atoms = there_ref.shape[1]
    width = emb_ref.shape[0]
    emb = emb_ref[...]
    slots = sel_ref.shape[1] // atoms
    win, wmid, wout = win_ref[0], wmid_ref[0], wout_ref[0]

    def store(domain, w, dw, h):
        edge_ref[domain, 0:width] = dw[:width] * h
        edge_ref[domain, width : 2 * width] = dw[width:] * h
        edge_ref[domain, 2 * width :] = w[width:] * h

    w, dw = radial_pair(win, wmid, wout, basis_ref[0], basis_ref[1])
    store(0, w, dw, far_kinds(bdot(tab_ref[...], sel_ref[...]), emb))

    there = there_ref[...]
    build_selector(there[8 : 8 + slots], sel_scr)
    sel_ghost_ref[...] = sel_scr[atoms:]
    g = bdot(ftab_ref[...], sel_scr[...])
    far, h = far_positions(g), far_kinds(g, emb)
    counts = spread_rows(there[8 + slots : 9 + slots], 8)
    unit, inv, b, db = edge_geometry(far, there, counts, slots)
    for i, x in enumerate(unit + [inv]):
        geom_ref[i : i + 1, :] = x[0:1]
    w, dw = radial_pair(win, wmid, wout, b, db)
    store(1, w, dw, h)
    a, b = messages(w, h, unit, width, slots)
    scale = 1.0 / jnp.sqrt(F32(slots))
    b_all = jnp.concatenate(b, axis=1) * scale
    species = embed_ref.shape[0]
    onehot = kinds(there[3:4], species)[:species]
    pre_ref[...] = mixed_pre(a * scale, b_all, hdot_t(embed_ref[...], onehot), mix_ref)
    b_ref[...] = b_all


def back_one_kernel(
    sent_ref,
    far_ref,
    gghost_ref,
    sel_ref,
    sel_ghost_ref,
    geom_ref,
    far_geom_ref,
    edge_ref,
    pre_ref,
    far_pre_ref,
    b_ref,
    far_b_ref,
    mix_ref,
    vec_ref,
    gpos_ref,
    gown_out,
    ghost_out,
    pos_scr,
    far_pos_scr,
):
    atoms = gpos_ref.shape[1]
    width = mix_ref.shape[1]
    slots = sel_ref.shape[1] // atoms
    rows = 2 * width
    odd = parity_odd(rows)
    ours = far_lanes(rows)
    zero = jnp.zeros((rows, atoms), F32)
    scale = 1.0 / jnp.sqrt(F32(slots))
    lo, hi = unpacked(far_ref[2 * rows : 3 * rows], odd)
    g_lo = sent_ref[0:rows] + jnp.where(ours, zero, lo)
    g_hi = sent_ref[rows : 2 * rows] + jnp.where(ours, zero, hi)
    f_lo = far_ref[0:rows] + jnp.where(ours, gghost_ref[0:rows], zero)
    f_hi = far_ref[rows : 2 * rows] + jnp.where(ours, gghost_ref[rows:], zero)
    pre = jnp.concatenate([pre_ref[...], far_pre_ref[...]], axis=1)
    sg = sigmoid(pre)
    gpre = jnp.concatenate([g_lo[:width], f_lo[:width]], axis=1) * (sg + pre * sg * (1.0 - sg))
    ga = hdot(mix_ref[0], gpre) * scale
    gq = hdot(mix_ref[2], gpre) * (2.0 * scale)
    gv = jnp.concatenate(
        [g_lo[width:], g_hi[:width], g_hi[width:], f_lo[width:], f_hi[:width], f_hi[width:]],
        axis=1,
    )
    gb_all = hdot(vec_ref[...], gv) * scale
    b_of = [b_ref, far_b_ref]
    geom_of = [geom_ref, far_geom_ref]
    scr_of = [pos_scr, far_pos_scr]
    for domain in range(2):
        ga_d = ga[:, slot(domain)]
        gq_d = gq[:, slot(domain)]
        gb = [
            gb_all[:, slot(3 * domain + c)] + b_of[domain][:, slot(c)] * gq_d for c in range(3)
        ]
        geom = geom_of[domain]
        total = jnp.zeros((24, atoms), F32)
        for k in range(slots):
            unit = [spread_rows(geom[c : c + 1, slot(k)], 8) for c in range(3)]
            u = [tile8(x, width // 8) for x in unit]
            gbu = gb[0] * u[0] + gb[1] * u[1] + gb[2] * u[2]
            drho = (
                edge_ref[domain, 0:width, slot(k)] * ga_d
                + edge_ref[domain, width : 2 * width, slot(k)] * gbu
            )
            carried = edge_ref[domain, 2 * width :, slot(k)]
            du = [sum_groups(carried * gb[c]) for c in range(3)]
            gp = edge_gradient(unit, spread_rows(geom[3:4, slot(k)], 8), sum_groups(drho), du)
            x = jnp.concatenate(gp, axis=0)
            if domain == 0:
                total = total + x
            hi, lo = split(x)
            scr_of[domain][0:24, slot(k)] = hi
            scr_of[domain][24:48, slot(k)] = lo
        if domain == 0:
            centre = total
    acc = bdot_nt(pos_scr[...], sel_ref[...])
    pos = acc[0:24] + acc[24:48]
    ghost_out[...] = rows8(pos[:, atoms:]) + sent_ref[3 * rows :]
    acc = bdot_nt(far_pos_scr[...], sel_ghost_ref[...])
    there = rows8(acc[0:24] + acc[24:48]) + far_ref[3 * rows :]
    there = jnp.where(far_lanes(8), jnp.zeros((8, atoms), F32), there)
    gown_out[...] = gpos_ref[...] + rows8(pos[:, :atoms] - centre) + there


def call(kernel, out_shapes, args, scratch=(), flops=0, transcendentals=0, far_away=0):
    args = [
        pltpu.with_memory_space_constraint(x, pltpu.HBM) if i < far_away else x
        for i, x in enumerate(args)
    ]
    spaces = [pltpu.HBM] * far_away + [pltpu.VMEM] * (len(args) - far_away)
    moved = sum(x.size * x.dtype.itemsize for x in list(args) + list(out_shapes))
    return pl.pallas_call(
        kernel,
        out_shape=out_shapes,
        in_specs=[pl.BlockSpec(memory_space=space) for space in spaces],
        out_specs=[pl.BlockSpec(memory_space=pltpu.VMEM)] * len(out_shapes),
        scratch_shapes=list(scratch),
        cost_estimate=pl.CostEstimate(
            flops=flops, bytes_accessed=moved, transcendentals=transcendentals
        ),
        compiler_params=pltpu.CompilerParams(vmem_limit_bytes=36 * MIB),
    )(*args)


def shape(dims, dtype=F32):
    return jax.ShapeDtypeStruct(dims, dtype)


def body(
    positions,
    species,
    neighbours,
    counts,
    ghost_index,
    embed,
    radial_in,
    radial_mid,
    radial_out,
    mix_one,
    vec_mix,
    mix_two,
    readout,
):
    atoms = positions.shape[1]
    slots = neighbours.shape[0]
    edges = slots * atoms
    nbasis, hidden = radial_in.shape[1:]
    width = embed.shape[1]
    rows = 2 * width
    devices = lax.axis_size("space")
    near_route = [(i, i ^ 1) for i in range(devices)]
    far_route = [(i, ((i + 1) ^ 1) - 1) for i in range(1, devices - 1)]

    def swap_near(x):
        return lax.ppermute(x, "space", near_route)

    def swap_far(x):
        return lax.ppermute(x, "space", far_route)

    def scratch_of(args):
        return [pltpu.VMEM(x.shape, x.dtype) for x in args]

    def shapes_of(args):
        return [shape(x.shape, x.dtype) for x in args]

    near_pos = swap_near(positions)
    near_kind = swap_near(species)
    local = [positions, species[None], neighbours, ghost_index, counts[None]]
    weights = [radial_in, radial_mid, radial_out]
    passed = [embed, mix_one, vec_mix, mix_two, readout]
    moved = local + weights + passed
    own, edge_rows, sel, win, wmid, wout, embed, mix_one, vec_mix, mix_two, readout = call(
        prep_kernel,
        [
            shape((4, atoms)),
            shape((slots + 8, atoms)),
            shape((2 * atoms, edges), BF16),
            shape((2, hidden, 4 * nbasis), BF16),
            shape((2, hidden, 3 * hidden), BF16),
            shape((2, 2 * width, 3 * hidden), BF16),
        ]
        + shapes_of(passed),
        moved,
        scratch=scratch_of(local + weights)
        + [pltpu.VMEM((atoms, edges), BF16), pltpu.SemaphoreType.DMA((len(moved),))],
        flops=10**8,
        far_away=len(moved),
    )
    near_rows = [near_pos, (near_kind + 1).astype(F32)[None]]
    sent = jnp.concatenate([own] + near_rows + [edge_rows], axis=0)
    pairs = [[i, (i + 1) % devices] for i in range(1, devices, 2)]
    come = lax.all_gather(sent, "space", axis_index_groups=pairs)
    feats, far_feats, near_f, tab, ftab, emb, geom, basis, pre, b_all, there = call(
        layer_one_kernel,
        [
            shape((4 * width, atoms)),
            shape((4 * width, atoms)),
            shape((rows, atoms)),
            shape((32, 2 * atoms), BF16),
            shape((32, 2 * atoms), BF16),
            shape((width, 16), BF16),
            shape((8, edges)),
            shape((2, nbasis, edges)),
            shape((width, atoms)),
            shape((width, 3 * atoms)),
            shape((slots + 16, atoms)),
        ],
        [sent, come, sel, embed, win, wmid, wout, mix_one, vec_mix],
        scratch=[pltpu.VMEM((2 * atoms, edges // 2), BF16)],
        flops=2 * 10**9,
    )
    near_f = swap_near(near_f)
    w, dw = call(
        radial_two_kernel,
        [shape((2 * width, edges)), shape((2 * width, edges))],
        [basis, win, wmid, wout],
        flops=2 * 10**9,
    )
    energy, g_own, g_ghost, near_g, far_g, gpos, gpos_ghost = call(
        layer_two_kernel,
        [
            shape((1, atoms)),
            shape((4 * width, atoms)),
            shape((4 * width, atoms)),
            shape((rows, atoms)),
            shape((rows, atoms)),
            shape((8, atoms)),
            shape((8, atoms)),
        ],
        [feats, far_feats, near_f, sel, geom, w, dw, mix_two, readout],
        scratch=[pltpu.VMEM((8 * width + 48, edges), BF16)],
        flops=10**9,
    )
    near_g = swap_near(near_g)
    (sent,) = call(
        join_kernel, [shape((3 * rows + 8, atoms))], [g_own, near_g, far_g, gpos_ghost]
    )
    come = swap_far(sent)
    edge, sel_ghost, far_geom, far_pre, far_b = call(
        tangent_one_kernel,
        [
            shape((2, 3 * width, edges)),
            shape((atoms, edges), BF16),
            shape((8, edges)),
            shape((width, atoms)),
            shape((width, 3 * atoms)),
        ],
        [basis, tab, ftab, emb, sel, there, win, wmid, wout, mix_one, embed],
        scratch=[pltpu.VMEM((2 * atoms, edges), BF16)],
        flops=4 * 10**9,
    )
    centre, ghost = call(
        back_one_kernel,
        [shape((8, atoms)), shape((8, atoms))],
        [
            sent,
            come,
            g_ghost,
            sel,
            sel_ghost,
            geom,
            far_geom,
            edge,
            pre,
            far_pre,
            b_all,
            far_b,
            mix_one,
            vec_mix,
            gpos,
        ],
        scratch=[pltpu.VMEM((48, edges), BF16), pltpu.VMEM((48, edges), BF16)],
        flops=10**9,
    )
    near_p = swap_near(ghost)
    odd = lax.rem(lax.axis_index("space"), 2) == 1
    low = lax.broadcasted_iota(jnp.int32, (3, atoms), 1) < HALF
    back = jnp.where(low == odd, near_p[:3], 0.0)
    return (energy[0], -(centre[:3] + back))


def solution(mesh):
    placed = (
        P(None, "space"),
        P("space"),
        P(None, "space"),
        P("space"),
        P(None, "space"),
        P(),
        P(),
        P(),
        P(),
        P(),
        P(),
        P(),
        P(),
    )
    return jax.shard_map(
        body, mesh=mesh, in_specs=placed, out_specs=(P("space"), P(None, "space")), check_vma=False
    )
```

```python
import jax
import jax.numpy as jnp
from jax import lax
from jax.experimental import pallas as pl
from jax.experimental.pallas import tpu as pltpu
from jax.sharding import PartitionSpec as P

RADIUS = 5.0
SOFTEN = 0.25
F32 = jnp.float32
BF16 = jnp.bfloat16
HALF = 64
MIB = 1024 * 1024


def hdot(a, b, dims=(((1,), (0,)), ((), ()))):
    return lax.dot_general(
        a, b, dims, precision=lax.Precision.HIGHEST, preferred_element_type=F32
    )


def hdot_t(a, b):
    return hdot(a, b, (((0,), (0,)), ((), ())))


def bdot(a, b):
    return jnp.dot(a, b, preferred_element_type=F32)


def bdot_nt(a, b):
    return lax.dot_general(a, b, (((1,), (1,)), ((), ())), preferred_element_type=F32)


def high(x):
    return x.astype(BF16).astype(F32)


def split(x):
    hi = x.astype(BF16)
    return hi, (x - hi.astype(F32)).astype(BF16)


def stack3(x):
    hi, lo = split(x)
    return jnp.concatenate([hi, lo, hi], axis=0)


def slot(k):
    return slice(k * 128, (k + 1) * 128)


def sigmoid(v):
    return 0.5 + 0.5 * jnp.tanh(0.5 * v)


def roll64(x):
    return pltpu.roll(x, HALF, 1)


def lane_low(rows):
    return lax.broadcasted_iota(jnp.int32, (rows, 128), 1) < HALF


def parity_odd(rows):
    odd = lax.rem(lax.axis_index("space"), 2)
    return jnp.full((rows, 128), odd, jnp.int32) > 0


def far_lanes(rows):
    return parity_odd(rows) == lane_low(rows)


def copy_in(moves, sems):
    copies = [
        pltpu.make_async_copy(src, dst, sems.at[i]) for i, (src, dst) in enumerate(moves)
    ]
    for c in copies:
        c.start()
    for c in copies:
        c.wait()


def put_lists(nb_ref, gi_ref, counts_ref, out_ref, hot_ref):
    slots, atoms = nb_ref.shape
    rows = (lax.broadcasted_iota(jnp.int32, (atoms, atoms), 0) + atoms).astype(F32).astype(BF16)
    one = jnp.ones((atoms, atoms), BF16)
    zero = jnp.zeros((atoms, atoms), BF16)
    for k in range(slots):
        nb = jnp.broadcast_to(nb_ref[k : k + 1, :].astype(F32), (16, atoms)).astype(BF16)
        nb = jnp.concatenate([nb] * (atoms // 16), axis=0)
        hot_ref[:, slot(k)] = jnp.where(rows == nb, one, zero)
    place = jnp.concatenate(
        [jnp.broadcast_to(gi_ref[i : i + 1, :], (16, HALF)).astype(F32) for i in range(2)], axis=1
    )
    ghost = bdot(place.astype(BF16), hot_ref[...])
    for k in range(slots):
        nb = nb_ref[k : k + 1, :]
        out_ref[k : k + 1, :] = jnp.where(
            nb < atoms, nb.astype(F32), ghost[0:1, slot(k)] + F32(atoms)
        )
    out_ref[slots : slots + 1, :] = counts_ref[...].astype(F32)
    out_ref[slots + 1 :, :] = jnp.zeros((out_ref.shape[0] - slots - 1, atoms), F32)


def build_selector(rows_f32, sel_ref):
    count, atoms = rows_f32.shape
    rows = lax.broadcasted_iota(jnp.int32, (2 * atoms, atoms), 0).astype(F32).astype(BF16)
    one = jnp.ones((2 * atoms, atoms), BF16)
    zero = jnp.zeros((2 * atoms, atoms), BF16)
    for k in range(count):
        nb = jnp.broadcast_to(rows_f32[k : k + 1, :], (16, atoms)).astype(BF16)
        nb = jnp.concatenate([nb] * (atoms // 8), axis=0)
        sel_ref[:, slot(k)] = jnp.where(rows == nb, one, zero)


def prep_kernel(
    pos_hbm,
    kind_hbm,
    nb_hbm,
    gi_hbm,
    counts_hbm,
    rin_hbm,
    rmid_hbm,
    rout_hbm,
    embed_hbm,
    mix_one_hbm,
    vec_hbm,
    mix_two_hbm,
    read_hbm,
    own_ref,
    edges_ref,
    sel_ref,
    win_ref,
    wmid_ref,
    wout_ref,
    embed_ref,
    mix_one_ref,
    vec_ref,
    mix_two_ref,
    read_ref,
    pos_ref,
    kind_ref,
    nb_ref,
    gi_ref,
    counts_ref,
    rin_ref,
    rmid_ref,
    rout_ref,
    hot_ref,
    sems,
):
    copy_in(
        [
            (pos_hbm, pos_ref),
            (kind_hbm, kind_ref),
            (nb_hbm, nb_ref),
            (gi_hbm, gi_ref),
            (counts_hbm, counts_ref),
            (rin_hbm, rin_ref),
            (rmid_hbm, rmid_ref),
            (rout_hbm, rout_ref),
            (embed_hbm, embed_ref),
            (mix_one_hbm, mix_one_ref),
            (vec_hbm, vec_ref),
            (mix_two_hbm, mix_two_ref),
            (read_hbm, read_ref),
        ],
        sems,
    )
    own_ref[0:3, :] = pos_ref[...]
    own_ref[3:4, :] = (kind_ref[...] + 1).astype(F32)
    put_lists(nb_ref, gi_ref, counts_ref, edges_ref, hot_ref)
    build_selector(edges_ref[0 : nb_ref.shape[0], :], sel_ref)
    for layer in range(2):
        w = rin_ref[layer]
        h = high(w)
        lo = w - h
        win_ref[layer] = jnp.concatenate([h, h, lo, lo], axis=0).T.astype(BF16)
        w = rmid_ref[layer]
        h = high(w)
        wmid_ref[layer] = jnp.concatenate([h, h, w - h], axis=0).T.astype(BF16)
        w = rout_ref[layer]
        h = high(w)
        wout_ref[layer] = jnp.concatenate([h, h, w - h], axis=0).T.astype(BF16)


def basis_rows(b):
    h = high(b)
    lo = b - h
    return jnp.concatenate([h, lo, h, lo], axis=0).astype(BF16)


def radial(win, wmid, wout, b):
    v1 = bdot(win, basis_rows(b))
    v2 = bdot(wmid, stack3(v1 * sigmoid(v1)))
    return bdot(wout, stack3(v2 * sigmoid(v2)))


def silu_pair(v, t):
    s = sigmoid(v)
    z = v * s
    return z, (s + z * (1.0 - s)) * t


def radial_pair(win, wmid, wout, b, db):
    z1, t1 = silu_pair(bdot(win, basis_rows(b)), bdot(win, basis_rows(db)))
    z2, t2 = silu_pair(bdot(wmid, stack3(z1)), bdot(wmid, stack3(t1)))
    return bdot(wout, stack3(z2)), bdot(wout, stack3(t2))


def spread_rows(row, rows):
    return jnp.broadcast_to(row, (rows, row.shape[1]))


def geometry(far, own, valid):
    vec = [f - o for f, o in zip(far, own)]
    r2 = vec[0] * vec[0] + vec[1] * vec[1] + vec[2] * vec[2] + SOFTEN
    inv = lax.rsqrt(r2)
    inv = inv * (1.5 - 0.5 * r2 * inv * inv)
    rho = r2 * inv
    unit = [v * inv for v in vec]
    x = jnp.minimum(rho * (1.0 / RADIUS), 1.0)
    y = 1.0 - x
    x2 = x * x
    env = y * y * y * (1.0 + x * (3.0 + x * (6.0 + x * (10.0 + x * 15.0))))
    denv = (-105.0 / RADIUS) * x2 * x2 * y * y
    f = RADIUS * inv * env * valid
    df = RADIUS * inv * (denv - env * inv) * valid
    n = (lax.broadcasted_iota(jnp.int32, rho.shape, 0) + 1).astype(F32)
    turns = n * x
    whole = jnp.floor(turns + 0.5)
    frac = (turns - whole) * jnp.pi
    parity = whole - 2.0 * jnp.floor(0.5 * whole)
    sign = 1.0 - 2.0 * parity
    q = frac * frac
    sin = frac * (
        1.0
        + q * (-1 / 6 + q * (1 / 120 + q * (-1 / 5040 + q * (1 / 362880 + q * (-1 / 39916800)))))
    )
    cos = 1.0 + q * (
        -1 / 2
        + q * (1 / 24 + q * (-1 / 720 + q * (1 / 40320 + q * (-1 / 3628800 + q * (1 / 479001600)))))
    )
    sin = sin * sign
    cos = cos * sign
    return unit, inv, sin * f, sin * df + (n * (jnp.pi / RADIUS)) * cos * f


def kinds(row, species):
    n = row.shape[1]
    numbers = (lax.broadcasted_iota(jnp.int32, (8, n), 0) + 1).astype(F32)
    return jnp.logical_and(spread_rows(row, 8) == numbers, numbers <= F32(species)).astype(F32)


def make_table(table, species, tab_ref):
    parts = []
    for c in range(3):
        p = table[c : c + 1]
        h = high(p)
        m = high(p - h)
        parts += [h, m, p - h - m]
    pad = jnp.zeros((7, table.shape[1]), F32)
    rows = parts + [pad, kinds(table[3:4], species), pad, pad[0:1]]
    tab_ref[...] = jnp.concatenate(rows, axis=0).astype(BF16)


def embed_rows(embed):
    species, width = embed.shape
    e = jnp.concatenate([embed, jnp.zeros((8 - species, width), F32)], axis=0)
    h = high(e)
    return jnp.concatenate([h, e - h], axis=0).T.astype(BF16)


def far_kinds(g, emb):
    hot = g[16:24]
    return bdot(emb, jnp.concatenate([hot, hot], axis=0).astype(BF16))


def far_positions(g):
    return [
        spread_rows(g[3 * c : 3 * c + 1], 8)
        + spread_rows(g[3 * c + 1 : 3 * c + 2], 8)
        + spread_rows(g[3 * c + 2 : 3 * c + 3], 8)
        for c in range(3)
    ]


def edge_geometry(far, own, counts, tiles):
    centre = [jnp.concatenate([spread_rows(own[c : c + 1], 8)] * tiles, axis=1) for c in range(3)]
    valid = jnp.concatenate([(counts > F32(k)).astype(F32) for k in range(tiles)], axis=1)
    return geometry(far, centre, valid)


def messages(w, h, unit, width, tiles):
    atoms = 128
    wa = w[:width] * h
    wb = w[width:] * h
    a_sum = jnp.zeros((width, atoms), F32)
    b_sum = [jnp.zeros((width, atoms), F32) for _ in range(3)]
    for k in range(tiles):
        a_sum = a_sum + wa[:, slot(k)]
        for c in range(3):
            b_sum[c] = b_sum[c] + wb[:, slot(k)] * tile8(unit[c][:, slot(k)], width // 8)
    return a_sum, b_sum


def tile8(x, times):
    return jnp.concatenate([x] * times, axis=0)


def mixed_pre(a, b_all, h0_own, mix_ref):
    atoms = a.shape[1]
    sq = b_all * b_all
    q = sq[:, :atoms] + sq[:, atoms : 2 * atoms] + sq[:, 2 * atoms :]
    return hdot_t(mix_ref[0], a) + hdot_t(mix_ref[1], h0_own) + hdot_t(mix_ref[2], q)


def features(pre, b_all, vec):
    atoms = pre.shape[1]
    v1 = hdot_t(vec, b_all)
    return (
        jnp.concatenate([pre * sigmoid(pre), v1[:, :atoms]], axis=0),
        jnp.concatenate([v1[:, atoms : 2 * atoms], v1[:, 2 * atoms :]], axis=0),
    )


def doubled(x):
    rows = x.shape[0]
    low = lane_low(rows)
    other = roll64(x)
    return jnp.where(low == parity_odd(rows), x, other)


def layer_one_kernel(
    sent_ref,
    come_ref,
    sel_ref,
    embed_ref,
    win_ref,
    wmid_ref,
    wout_ref,
    mix_ref,
    vec_ref,
    feats_ref,
    far_feats_ref,
    near_out,
    tab_ref,
    ftab_ref,
    emb_ref,
    geom_ref,
    basis_ref,
    pre_ref,
    b_ref,
    there_ref,
    sel_far_ref,
):
    atoms = sent_ref.shape[1]
    slots = sel_ref.shape[1] // atoms
    tiles = slots // 2
    width = embed_ref.shape[1]
    embed = embed_ref[...]
    scale = 1.0 / jnp.sqrt(F32(slots))
    ours = far_lanes(4)
    own = sent_ref[0:4]
    near = sent_ref[4:8]
    me = jnp.full(sent_ref.shape, lax.axis_index("space"), jnp.int32)
    has = jnp.logical_and(me > 0, me < lax.axis_size("space") - 1)
    there = jnp.where(parity_odd(sent_ref.shape[0]), come_ref[1], come_ref[0])
    there = jnp.where(has, there, jnp.zeros(sent_ref.shape, F32))
    there_ref[...] = there
    low12 = lane_low(tiles)
    lists = there[8 : 8 + slots]
    first = lists[:tiles]
    second = lists[tiles:]
    odd12 = parity_odd(tiles)
    build_selector(
        jnp.where(
            low12,
            jnp.where(odd12, first, roll64(first)),
            jnp.where(odd12, roll64(second), second),
        ),
        sel_far_ref,
    )
    species = embed.shape[0]
    make_table(
        jnp.concatenate([own, jnp.where(ours, there[0:4], near)], axis=1), species, tab_ref
    )
    make_table(
        jnp.concatenate([there[0:4], jnp.where(ours, there[4:8], own)], axis=1), species, ftab_ref
    )
    emb = embed_rows(embed)
    emb_ref[...] = emb
    h0 = hdot_t(embed, kinds(own[3:4], species)[:species])
    h0_far = hdot_t(embed, kinds(doubled(there[0:8])[3:4], species)[:species])
    g = bdot(tab_ref[...], sel_ref[...])
    gf = bdot(ftab_ref[...], sel_far_ref[...])

    edges = slots * atoms
    half = doubled(there)
    far = [jnp.concatenate(x, axis=1) for x in zip(far_positions(g), far_positions(gf))]
    centre = [
        jnp.concatenate(
            [spread_rows(own[c : c + 1], 8)] * slots + [spread_rows(half[c : c + 1], 8)] * tiles,
            axis=1,
        )
        for c in range(3)
    ]
    counts = spread_rows(sent_ref[8 + slots : 9 + slots, :], 8)
    far_counts = spread_rows(half[8 + slots : 9 + slots], 8) - jnp.where(
        lane_low(8), F32(0), F32(tiles)
    )
    valid = jnp.concatenate(
        [(counts > F32(k)).astype(F32) for k in range(slots)]
        + [(far_counts > F32(k)).astype(F32) for k in range(tiles)],
        axis=1,
    )
    unit, inv, b, db = geometry(far, centre, valid)
    for i, x in enumerate(unit + [inv]):
        geom_ref[i : i + 1, :] = x[0:1, :edges]
    basis_ref[0] = b[:, :edges]
    basis_ref[1] = db[:, :edges]
    hot = jnp.concatenate([g[16:24], gf[16:24]], axis=1)
    h = bdot(emb, jnp.concatenate([hot, hot], axis=0).astype(BF16))
    w = radial(win_ref[0], wmid_ref[0], wout_ref[0], b)
    wa = w[:width] * h
    wb = w[width:] * h

    def summed(first, count):
        sums = [jnp.zeros((width, atoms), F32) for _ in range(4)]
        for k in range(first, first + count):
            x = wb[:, slot(k)]
            sums[0] = sums[0] + wa[:, slot(k)]
            for c in range(3):
                sums[c + 1] = sums[c + 1] + x * tile8(unit[c][:, slot(k)], width // 8)
        return sums

    ours_sum = summed(0, slots)
    theirs = [x + roll64(x) for x in summed(slots, tiles)]
    both = [jnp.concatenate([x, y], axis=1) * scale for x, y in zip(ours_sum, theirs)]
    q = both[1] * both[1] + both[2] * both[2] + both[3] * both[3]
    pre = (
        hdot_t(mix_ref[0], both[0])
        + hdot_t(mix_ref[1], jnp.concatenate([h0, h0_far], axis=1))
        + hdot_t(mix_ref[2], q)
    )
    pre_ref[...] = pre[:, :atoms]
    for c in range(3):
        b_ref[:, slot(c)] = both[c + 1][:, :atoms]
    s1 = pre * sigmoid(pre)
    v1 = hdot_t(vec_ref[...], jnp.concatenate(both[1:], axis=1))
    for domain, ref in ((0, feats_ref), (1, far_feats_ref)):
        ref[0:width] = s1[:, slot(domain)]
        for c in range(3):
            ref[(c + 1) * width : (c + 2) * width] = v1[:, slot(2 * c + domain)]
    low_lanes, high_lanes = packed(feats_ref[0 : 2 * width], feats_ref[2 * width :])
    near_out[...] = jnp.where(parity_odd(2 * width), low_lanes, high_lanes)


def packed(lo_part, hi_part):
    low = lane_low(lo_part.shape[0])
    return (
        jnp.where(low, lo_part, roll64(hi_part)),
        jnp.where(low, roll64(lo_part), hi_part),
    )


def unpacked(tile, high_half):
    other = roll64(tile)
    return jnp.where(high_half, other, tile), jnp.where(high_half, tile, other)


def radial_two_kernel(basis_ref, win_ref, wmid_ref, wout_ref, w_ref, dw_ref):
    w, dw = radial_pair(win_ref[1], wmid_ref[1], wout_ref[1], basis_ref[0], basis_ref[1])
    w_ref[...] = w
    dw_ref[...] = dw


def edge_gradient(unit, inv, drho, du):
    dot = unit[0] * du[0] + unit[1] * du[1] + unit[2] * du[2]
    radial_part = drho - dot * inv
    return [unit[c] * radial_part + du[c] * inv for c in range(3)]


def sum_groups(x):
    total = x[0:8]
    for i in range(1, x.shape[0] // 8):
        total = total + x[8 * i : 8 * i + 8]
    return total


def both_parts(grads):
    x = jnp.concatenate(list(grads), axis=0)
    h = high(x)
    return jnp.concatenate([h, x - h], axis=0).astype(BF16)


def put_positions(ref, base, grads):
    ref[base : base + 48] = both_parts(grads)


def rows8(x):
    sums = [jnp.sum(x[8 * c : 8 * c + 8], axis=0, keepdims=True) for c in range(3)]
    return jnp.concatenate(sums + [jnp.zeros((5, x.shape[1]), F32)], axis=0)


def centre_sum(grads, slots):
    x = jnp.concatenate(list(grads), axis=0)
    total = x[:, slot(0)]
    for k in range(1, slots):
        total = total + x[:, slot(k)]
    return total


def layer_two_kernel(
    feats_ref,
    far_feats_ref,
    near_ref,
    sel_ref,
    geom_ref,
    w_ref,
    dw_ref,
    mix_ref,
    read_ref,
    energy_ref,
    gown_ref,
    gghost_ref,
    near_out,
    far_out,
    gpos_ref,
    gpos_ghost_ref,
    grad_scr,
):
    atoms = feats_ref.shape[1]
    width = mix_ref.shape[1]
    slots = sel_ref.shape[1] // atoms
    rows = 2 * width
    odd = parity_odd(rows)
    ours = far_lanes(rows)
    near_lo, near_hi = unpacked(near_ref[...], odd)
    g_lo = jnp.where(ours, far_feats_ref[0:rows], near_lo)
    g_hi = jnp.where(ours, far_feats_ref[rows:], near_hi)
    feats = feats_ref[...]
    table = jnp.concatenate([feats, jnp.concatenate([g_lo, g_hi], axis=0)], axis=1)
    t_hi, t_lo = split(table)
    g = bdot(jnp.concatenate([t_hi, t_lo], axis=0), sel_ref[...])

    f = g[: 4 * width] + g[4 * width :]
    unit = [geom_ref[c : c + 1, :] for c in range(3)]
    along = f[width : 2 * width] * spread_rows(unit[0], width)
    along = along + f[2 * width : 3 * width] * spread_rows(unit[1], width)
    along = along + f[3 * width :] * spread_rows(unit[2], width)
    msg = w_ref[0:width] * f[:width] + w_ref[width:] * along
    m = jnp.zeros((width, atoms), F32)
    for k in range(slots):
        m = m + msg[:, slot(k)]
    scale = 1.0 / jnp.sqrt(F32(slots))
    s1 = feats[:width]
    pre = hdot_t(mix_ref[0], m * scale) + hdot_t(mix_ref[1], s1)
    sg = sigmoid(pre)
    s2 = pre * sg
    energy_ref[...] = hdot(read_ref[0:1], s1) + hdot(read_ref[1:2], s2)
    read = read_ref[...].T
    r_one = jnp.broadcast_to(read[:, 0:1], (width, atoms))
    r_two = jnp.broadcast_to(read[:, 1:2], (width, atoms))
    gpre = r_two * (sg + s2 * (1.0 - sg))
    gm = hdot(mix_ref[0], gpre) * scale
    gs_own = r_one + hdot(mix_ref[1], gpre)
    gm_rep = jnp.concatenate([gm] * slots, axis=1)
    ga = w_ref[0:width] * gm_rep
    gb = w_ref[width:] * gm_rep
    for i, x in enumerate([ga] + [gb * spread_rows(u, width) for u in unit]):
        hi, lo = split(x)
        grad_scr[i * width : (i + 1) * width] = hi
        grad_scr[(4 + i) * width : (5 + i) * width] = lo
    drho = gm_rep * (dw_ref[0:width] * f[:width] + dw_ref[width:] * along)
    du = [sum_groups(gb * f[(c + 1) * width : (c + 2) * width]) for c in range(3)]
    gp = edge_gradient(
        [spread_rows(u, 8) for u in unit],
        spread_rows(geom_ref[3:4, :], 8),
        sum_groups(drho),
        du,
    )
    put_positions(grad_scr, 8 * width, gp)
    centre = centre_sum(gp, slots)
    acc = bdot_nt(grad_scr[...], sel_ref[...])
    grads = acc[: 4 * width] + acc[4 * width : 8 * width]
    own = grads[:, :atoms]
    gown_ref[0:width] = own[0:width] + gs_own
    gown_ref[width:] = own[width:]
    ghost = grads[:, atoms:]
    gghost_ref[...] = ghost
    to_upper, to_lower = packed(ghost[:rows], ghost[rows:])
    near_out[...] = jnp.where(odd, to_lower, to_upper)
    far_out[...] = jnp.where(odd, to_upper, to_lower)
    pos = acc[8 * width : 8 * width + 24] + acc[8 * width + 24 :]
    gpos_ref[...] = rows8(pos[:, :atoms] - centre)
    gpos_ghost_ref[...] = rows8(pos[:, atoms:])


def join_kernel(gown_ref, near_ref, far_ref, gpos_ghost_ref, out_ref):
    rows = near_ref.shape[0]
    odd = parity_odd(rows)
    ours = far_lanes(rows)
    zero = jnp.zeros(near_ref.shape, F32)
    lo, hi = unpacked(near_ref[...], jnp.logical_not(odd))
    out_ref[0:rows] = gown_ref[0:rows] + jnp.where(ours, lo, zero)
    out_ref[rows : 2 * rows] = gown_ref[rows:] + jnp.where(ours, hi, zero)
    out_ref[2 * rows : 3 * rows] = far_ref[...]
    out_ref[3 * rows :] = gpos_ghost_ref[...]


def tangent_one_kernel(
    basis_ref,
    tab_ref,
    ftab_ref,
    emb_ref,
    sel_ref,
    there_ref,
    win_ref,
    wmid_ref,
    wout_ref,
    mix_ref,
    embed_ref,
    edge_ref,
    sel_ghost_ref,
    geom_ref,
    pre_ref,
    b_ref,
    sel_scr,
):
    atoms = there_ref.shape[1]
    width = emb_ref.shape[0]
    emb = emb_ref[...]
    slots = sel_ref.shape[1] // atoms
    win, wmid, wout = win_ref[0], wmid_ref[0], wout_ref[0]

    def store(domain, w, dw, h):
        edge_ref[domain, 0:width] = dw[:width] * h
        edge_ref[domain, width : 2 * width] = dw[width:] * h
        edge_ref[domain, 2 * width :] = w[width:] * h

    w, dw = radial_pair(win, wmid, wout, basis_ref[0], basis_ref[1])
    store(0, w, dw, far_kinds(bdot(tab_ref[...], sel_ref[...]), emb))

    there = there_ref[...]
    build_selector(there[8 : 8 + slots], sel_scr)
    sel_ghost_ref[...] = sel_scr[atoms:]
    g = bdot(ftab_ref[...], sel_scr[...])
    far, h = far_positions(g), far_kinds(g, emb)
    counts = spread_rows(there[8 + slots : 9 + slots], 8)
    unit, inv, b, db = edge_geometry(far, there, counts, slots)
    for i, x in enumerate(unit + [inv]):
        geom_ref[i : i + 1, :] = x[0:1]
    w, dw = radial_pair(win, wmid, wout, b, db)
    store(1, w, dw, h)
    a, b = messages(w, h, unit, width, slots)
    scale = 1.0 / jnp.sqrt(F32(slots))
    b_all = jnp.concatenate(b, axis=1) * scale
    species = embed_ref.shape[0]
    onehot = kinds(there[3:4], species)[:species]
    pre_ref[...] = mixed_pre(a * scale, b_all, hdot_t(embed_ref[...], onehot), mix_ref)
    b_ref[...] = b_all


def back_one_kernel(
    sent_ref,
    far_ref,
    gghost_ref,
    sel_ref,
    sel_ghost_ref,
    geom_ref,
    far_geom_ref,
    edge_ref,
    pre_ref,
    far_pre_ref,
    b_ref,
    far_b_ref,
    mix_ref,
    vec_ref,
    gpos_ref,
    gown_out,
    ghost_out,
    pos_scr,
    far_pos_scr,
):
    atoms = gpos_ref.shape[1]
    width = mix_ref.shape[1]
    slots = sel_ref.shape[1] // atoms
    rows = 2 * width
    odd = parity_odd(rows)
    ours = far_lanes(rows)
    zero = jnp.zeros((rows, atoms), F32)
    scale = 1.0 / jnp.sqrt(F32(slots))
    lo, hi = unpacked(far_ref[2 * rows : 3 * rows], odd)
    g_lo = sent_ref[0:rows] + jnp.where(ours, zero, lo)
    g_hi = sent_ref[rows : 2 * rows] + jnp.where(ours, zero, hi)
    f_lo = far_ref[0:rows] + jnp.where(ours, gghost_ref[0:rows], zero)
    f_hi = far_ref[rows : 2 * rows] + jnp.where(ours, gghost_ref[rows:], zero)
    pre = jnp.concatenate([pre_ref[...], far_pre_ref[...]], axis=1)
    sg = sigmoid(pre)
    gpre = jnp.concatenate([g_lo[:width], f_lo[:width]], axis=1) * (sg + pre * sg * (1.0 - sg))
    ga = hdot(mix_ref[0], gpre) * scale
    gq = hdot(mix_ref[2], gpre) * (2.0 * scale)
    gv = jnp.concatenate(
        [g_lo[width:], g_hi[:width], g_hi[width:], f_lo[width:], f_hi[:width], f_hi[width:]],
        axis=1,
    )
    gb_all = hdot(vec_ref[...], gv) * scale
    b_of = [b_ref, far_b_ref]
    geom_of = [geom_ref, far_geom_ref]
    scr_of = [pos_scr, far_pos_scr]
    for domain in range(2):
        ga_d = ga[:, slot(domain)]
        gq_d = gq[:, slot(domain)]
        gb = [
            gb_all[:, slot(3 * domain + c)] + b_of[domain][:, slot(c)] * gq_d for c in range(3)
        ]
        geom = geom_of[domain]
        total = jnp.zeros((24, atoms), F32)
        for k in range(slots):
            unit = [spread_rows(geom[c : c + 1, slot(k)], 8) for c in range(3)]
            u = [tile8(x, width // 8) for x in unit]
            gbu = gb[0] * u[0] + gb[1] * u[1] + gb[2] * u[2]
            drho = (
                edge_ref[domain, 0:width, slot(k)] * ga_d
                + edge_ref[domain, width : 2 * width, slot(k)] * gbu
            )
            carried = edge_ref[domain, 2 * width :, slot(k)]
            du = [sum_groups(carried * gb[c]) for c in range(3)]
            gp = edge_gradient(unit, spread_rows(geom[3:4, slot(k)], 8), sum_groups(drho), du)
            if domain == 0:
                total = total + jnp.concatenate(gp, axis=0)
            scr_of[domain][:, slot(k)] = both_parts(gp)
        if domain == 0:
            centre = total
    acc = bdot_nt(pos_scr[...], sel_ref[...])
    pos = acc[0:24] + acc[24:48]
    ghost_out[...] = rows8(pos[:, atoms:]) + sent_ref[3 * rows :]
    acc = bdot_nt(far_pos_scr[...], sel_ghost_ref[...])
    there = rows8(acc[0:24] + acc[24:48]) + far_ref[3 * rows :]
    there = jnp.where(far_lanes(8), jnp.zeros((8, atoms), F32), there)
    gown_out[...] = gpos_ref[...] + rows8(pos[:, :atoms] - centre) + there


def call(kernel, out_shapes, args, scratch=(), flops=0, transcendentals=0, far_away=0):
    args = [
        pltpu.with_memory_space_constraint(x, pltpu.HBM) if i < far_away else x
        for i, x in enumerate(args)
    ]
    spaces = [pltpu.HBM] * far_away + [pltpu.VMEM] * (len(args) - far_away)
    moved = sum(x.size * x.dtype.itemsize for x in list(args) + list(out_shapes))
    return pl.pallas_call(
        kernel,
        out_shape=out_shapes,
        in_specs=[pl.BlockSpec(memory_space=space) for space in spaces],
        out_specs=[pl.BlockSpec(memory_space=pltpu.VMEM)] * len(out_shapes),
        scratch_shapes=list(scratch),
        cost_estimate=pl.CostEstimate(
            flops=flops, bytes_accessed=moved, transcendentals=transcendentals
        ),
        compiler_params=pltpu.CompilerParams(vmem_limit_bytes=36 * MIB),
    )(*args)


def shape(dims, dtype=F32):
    return jax.ShapeDtypeStruct(dims, dtype)


def body(
    positions,
    species,
    neighbours,
    counts,
    ghost_index,
    embed,
    radial_in,
    radial_mid,
    radial_out,
    mix_one,
    vec_mix,
    mix_two,
    readout,
):
    atoms = positions.shape[1]
    slots = neighbours.shape[0]
    edges = slots * atoms
    nbasis, hidden = radial_in.shape[1:]
    width = embed.shape[1]
    rows = 2 * width
    devices = lax.axis_size("space")
    near_route = [(i, i ^ 1) for i in range(devices)]
    far_route = [(i, ((i + 1) ^ 1) - 1) for i in range(1, devices - 1)]

    def swap_near(x):
        return lax.ppermute(x, "space", near_route)

    def swap_far(x):
        return lax.ppermute(x, "space", far_route)

    def scratch_of(args):
        return [pltpu.VMEM(x.shape, x.dtype) for x in args]

    def shapes_of(args):
        return [shape(x.shape, x.dtype) for x in args]

    near_pos = swap_near(positions)
    near_kind = swap_near(species)
    local = [positions, species[None], neighbours, ghost_index, counts[None]]
    weights = [radial_in, radial_mid, radial_out]
    passed = [embed, mix_one, vec_mix, mix_two, readout]
    moved = local + weights + passed
    own, edge_rows, sel, win, wmid, wout, embed, mix_one, vec_mix, mix_two, readout = call(
        prep_kernel,
        [
            shape((4, atoms)),
            shape((slots + 8, atoms)),
            shape((2 * atoms, edges), BF16),
            shape((2, hidden, 4 * nbasis), BF16),
            shape((2, hidden, 3 * hidden), BF16),
            shape((2, 2 * width, 3 * hidden), BF16),
        ]
        + shapes_of(passed),
        moved,
        scratch=scratch_of(local + weights)
        + [pltpu.VMEM((atoms, edges), BF16), pltpu.SemaphoreType.DMA((len(moved),))],
        flops=10**8,
        far_away=len(moved),
    )
    near_rows = [near_pos, (near_kind + 1).astype(F32)[None]]
    sent = jnp.concatenate([own] + near_rows + [edge_rows], axis=0)
    pairs = [[i, (i + 1) % devices] for i in range(1, devices, 2)]
    come = lax.all_gather(sent, "space", axis_index_groups=pairs)
    feats, far_feats, near_f, tab, ftab, emb, geom, basis, pre, b_all, there = call(
        layer_one_kernel,
        [
            shape((4 * width, atoms)),
            shape((4 * width, atoms)),
            shape((rows, atoms)),
            shape((32, 2 * atoms), BF16),
            shape((32, 2 * atoms), BF16),
            shape((width, 16), BF16),
            shape((8, edges)),
            shape((2, nbasis, edges)),
            shape((width, atoms)),
            shape((width, 3 * atoms)),
            shape((slots + 16, atoms)),
        ],
        [sent, come, sel, embed, win, wmid, wout, mix_one, vec_mix],
        scratch=[pltpu.VMEM((2 * atoms, edges // 2), BF16)],
        flops=2 * 10**9,
    )
    near_f = swap_near(near_f)
    w, dw = call(
        radial_two_kernel,
        [shape((2 * width, edges)), shape((2 * width, edges))],
        [basis, win, wmid, wout],
        flops=2 * 10**9,
    )
    energy, g_own, g_ghost, near_g, far_g, gpos, gpos_ghost = call(
        layer_two_kernel,
        [
            shape((1, atoms)),
            shape((4 * width, atoms)),
            shape((4 * width, atoms)),
            shape((rows, atoms)),
            shape((rows, atoms)),
            shape((8, atoms)),
            shape((8, atoms)),
        ],
        [feats, far_feats, near_f, sel, geom, w, dw, mix_two, readout],
        scratch=[pltpu.VMEM((8 * width + 48, edges), BF16)],
        flops=10**9,
    )
    near_g = swap_near(near_g)
    (sent,) = call(
        join_kernel, [shape((3 * rows + 8, atoms))], [g_own, near_g, far_g, gpos_ghost]
    )
    come = swap_far(sent)
    edge, sel_ghost, far_geom, far_pre, far_b = call(
        tangent_one_kernel,
        [
            shape((2, 3 * width, edges)),
            shape((atoms, edges), BF16),
            shape((8, edges)),
            shape((width, atoms)),
            shape((width, 3 * atoms)),
        ],
        [basis, tab, ftab, emb, sel, there, win, wmid, wout, mix_one, embed],
        scratch=[pltpu.VMEM((2 * atoms, edges), BF16)],
        flops=4 * 10**9,
    )
    centre, ghost = call(
        back_one_kernel,
        [shape((8, atoms)), shape((8, atoms))],
        [
            sent,
            come,
            g_ghost,
            sel,
            sel_ghost,
            geom,
            far_geom,
            edge,
            pre,
            far_pre,
            b_all,
            far_b,
            mix_one,
            vec_mix,
            gpos,
        ],
        scratch=[pltpu.VMEM((48, edges), BF16), pltpu.VMEM((48, edges), BF16)],
        flops=10**9,
    )
    near_p = swap_near(ghost)
    odd = lax.rem(lax.axis_index("space"), 2) == 1
    low = lax.broadcasted_iota(jnp.int32, (3, atoms), 1) < HALF
    back = jnp.where(low == odd, near_p[:3], 0.0)
    return (energy[0], -(centre[:3] + back))


def solution(mesh):
    placed = (
        P(None, "space"),
        P("space"),
        P(None, "space"),
        P("space"),
        P(None, "space"),
        P(),
        P(),
        P(),
        P(),
        P(),
        P(),
        P(),
        P(),
    )
    return jax.shard_map(
        body, mesh=mesh, in_specs=placed, out_specs=(P("space"), P(None, "space")), check_vma=False
    )
```

```python
import jax
import jax.numpy as jnp
from jax import lax
from jax.experimental import pallas as pl
from jax.experimental.pallas import tpu as pltpu
from jax.sharding import PartitionSpec as P

RADIUS = 5.0
SOFTEN = 0.25
F32 = jnp.float32
BF16 = jnp.bfloat16
HALF = 64
MIB = 1024 * 1024


def hdot(a, b, dims=(((1,), (0,)), ((), ()))):
    return lax.dot_general(
        a, b, dims, precision=lax.Precision.HIGHEST, preferred_element_type=F32
    )


def hdot_t(a, b):
    return hdot(a, b, (((0,), (0,)), ((), ())))


def bdot(a, b):
    return jnp.dot(a, b, preferred_element_type=F32)


def bdot_nt(a, b):
    return lax.dot_general(a, b, (((1,), (1,)), ((), ())), preferred_element_type=F32)


def high(x):
    return x.astype(BF16).astype(F32)


def split(x):
    hi = x.astype(BF16)
    return hi, (x - hi.astype(F32)).astype(BF16)


def stack3(x):
    hi, lo = split(x)
    return jnp.concatenate([hi, lo, hi], axis=0)


def slot(k):
    return slice(k * 128, (k + 1) * 128)


def sigmoid(v):
    return 0.5 + 0.5 * jnp.tanh(0.5 * v)


def roll64(x):
    return pltpu.roll(x, HALF, 1)


def lane_low(rows):
    return lax.broadcasted_iota(jnp.int32, (rows, 128), 1) < HALF


def parity_odd(rows):
    odd = lax.rem(lax.axis_index("space"), 2)
    return jnp.full((rows, 128), odd, jnp.int32) > 0


def far_lanes(rows):
    return parity_odd(rows) == lane_low(rows)


def copy_in(moves, sems):
    copies = [
        pltpu.make_async_copy(src, dst, sems.at[i]) for i, (src, dst) in enumerate(moves)
    ]
    for c in copies:
        c.start()
    for c in copies:
        c.wait()


def put_lists(nb_ref, gi_ref, counts_ref, out_ref, hot_ref):
    slots, atoms = nb_ref.shape
    rows = (lax.broadcasted_iota(jnp.int32, (atoms, atoms), 0) + atoms).astype(F32).astype(BF16)
    one = jnp.ones((atoms, atoms), BF16)
    zero = jnp.zeros((atoms, atoms), BF16)
    for k in range(slots):
        nb = jnp.broadcast_to(nb_ref[k : k + 1, :].astype(F32), (16, atoms)).astype(BF16)
        nb = jnp.concatenate([nb] * (atoms // 16), axis=0)
        hot_ref[:, slot(k)] = jnp.where(rows == nb, one, zero)
    place = jnp.concatenate(
        [jnp.broadcast_to(gi_ref[i : i + 1, :], (16, HALF)).astype(F32) for i in range(2)], axis=1
    )
    ghost = bdot(place.astype(BF16), hot_ref[...])
    for k in range(slots):
        nb = nb_ref[k : k + 1, :]
        out_ref[k : k + 1, :] = jnp.where(
            nb < atoms, nb.astype(F32), ghost[0:1, slot(k)] + F32(atoms)
        )
    out_ref[slots : slots + 1, :] = counts_ref[...].astype(F32)
    out_ref[slots + 1 :, :] = jnp.zeros((out_ref.shape[0] - slots - 1, atoms), F32)


def build_selector(rows_f32, sel_ref):
    count, atoms = rows_f32.shape
    rows = lax.broadcasted_iota(jnp.int32, (2 * atoms, atoms), 0).astype(F32).astype(BF16)
    one = jnp.ones((2 * atoms, atoms), BF16)
    zero = jnp.zeros((2 * atoms, atoms), BF16)
    for k in range(count):
        nb = jnp.broadcast_to(rows_f32[k : k + 1, :], (16, atoms)).astype(BF16)
        nb = jnp.concatenate([nb] * (atoms // 8), axis=0)
        sel_ref[:, slot(k)] = jnp.where(rows == nb, one, zero)


def prep_kernel(
    pos_hbm,
    kind_hbm,
    nb_hbm,
    gi_hbm,
    counts_hbm,
    rin_hbm,
    rmid_hbm,
    rout_hbm,
    embed_hbm,
    mix_one_hbm,
    vec_hbm,
    mix_two_hbm,
    read_hbm,
    own_ref,
    edges_ref,
    sel_ref,
    win_ref,
    wmid_ref,
    wout_ref,
    embed_ref,
    mix_one_ref,
    vec_ref,
    mix_two_ref,
    read_ref,
    pos_ref,
    kind_ref,
    nb_ref,
    gi_ref,
    counts_ref,
    rin_ref,
    rmid_ref,
    rout_ref,
    hot_ref,
    sems,
):
    copy_in(
        [
            (pos_hbm, pos_ref),
            (kind_hbm, kind_ref),
            (nb_hbm, nb_ref),
            (gi_hbm, gi_ref),
            (counts_hbm, counts_ref),
            (rin_hbm, rin_ref),
            (rmid_hbm, rmid_ref),
            (rout_hbm, rout_ref),
            (embed_hbm, embed_ref),
            (mix_one_hbm, mix_one_ref),
            (vec_hbm, vec_ref),
            (mix_two_hbm, mix_two_ref),
            (read_hbm, read_ref),
        ],
        sems,
    )
    own_ref[0:3, :] = pos_ref[...]
    own_ref[3:4, :] = (kind_ref[...] + 1).astype(F32)
    put_lists(nb_ref, gi_ref, counts_ref, edges_ref, hot_ref)
    build_selector(edges_ref[0 : nb_ref.shape[0], :], sel_ref)
    for layer in range(2):
        w = rin_ref[layer]
        h = high(w)
        lo = w - h
        win_ref[layer] = jnp.concatenate([h, h, lo, lo], axis=0).T.astype(BF16)
        w = rmid_ref[layer]
        h = high(w)
        wmid_ref[layer] = jnp.concatenate([h, h, w - h], axis=0).T.astype(BF16)
        w = rout_ref[layer]
        h = high(w)
        wout_ref[layer] = jnp.concatenate([h, h, w - h], axis=0).T.astype(BF16)


def basis_rows(b):
    h = high(b)
    lo = b - h
    return jnp.concatenate([h, lo, h, lo], axis=0).astype(BF16)


def radial(win, wmid, wout, b):
    v1 = bdot(win, basis_rows(b))
    v2 = bdot(wmid, stack3(v1 * sigmoid(v1)))
    return bdot(wout, stack3(v2 * sigmoid(v2)))


def silu_pair(v, t):
    s = sigmoid(v)
    z = v * s
    return z, (s + z * (1.0 - s)) * t


def radial_pair(win, wmid, wout, b, db):
    z1, t1 = silu_pair(bdot(win, basis_rows(b)), bdot(win, basis_rows(db)))
    z2, t2 = silu_pair(bdot(wmid, stack3(z1)), bdot(wmid, stack3(t1)))
    return bdot(wout, stack3(z2)), bdot(wout, stack3(t2))


def spread_rows(row, rows):
    return jnp.broadcast_to(row, (rows, row.shape[1]))


def geometry(far, own, valid):
    vec = [f - o for f, o in zip(far, own)]
    r2 = vec[0] * vec[0] + vec[1] * vec[1] + vec[2] * vec[2] + SOFTEN
    inv = lax.rsqrt(r2)
    inv = inv * (1.5 - 0.5 * r2 * inv * inv)
    rho = r2 * inv
    unit = [v * inv for v in vec]
    x = jnp.minimum(rho * (1.0 / RADIUS), 1.0)
    y = 1.0 - x
    x2 = x * x
    env = y * y * y * (1.0 + x * (3.0 + x * (6.0 + x * (10.0 + x * 15.0))))
    denv = (-105.0 / RADIUS) * x2 * x2 * y * y
    f = RADIUS * inv * env * valid
    df = RADIUS * inv * (denv - env * inv) * valid
    n = (lax.broadcasted_iota(jnp.int32, rho.shape, 0) + 1).astype(F32)
    turns = n * x
    whole = jnp.floor(turns + 0.5)
    frac = (turns - whole) * jnp.pi
    parity = whole - 2.0 * jnp.floor(0.5 * whole)
    sign = 1.0 - 2.0 * parity
    q = frac * frac
    sin = frac * (
        1.0
        + q * (-1 / 6 + q * (1 / 120 + q * (-1 / 5040 + q * (1 / 362880 + q * (-1 / 39916800)))))
    )
    cos = 1.0 + q * (
        -1 / 2
        + q * (1 / 24 + q * (-1 / 720 + q * (1 / 40320 + q * (-1 / 3628800 + q * (1 / 479001600)))))
    )
    sin = sin * sign
    cos = cos * sign
    return unit, inv, sin * f, sin * df + (n * (jnp.pi / RADIUS)) * cos * f


def kinds(row, species):
    n = row.shape[1]
    numbers = (lax.broadcasted_iota(jnp.int32, (8, n), 0) + 1).astype(F32)
    return jnp.logical_and(spread_rows(row, 8) == numbers, numbers <= F32(species)).astype(F32)


def make_table(table, species, tab_ref):
    parts = []
    for c in range(3):
        p = table[c : c + 1]
        h = high(p)
        m = high(p - h)
        parts += [h, m, p - h - m]
    pad = jnp.zeros((7, table.shape[1]), F32)
    rows = parts + [pad, kinds(table[3:4], species), pad, pad[0:1]]
    tab_ref[...] = jnp.concatenate(rows, axis=0).astype(BF16)


def embed_rows(embed):
    species, width = embed.shape
    e = jnp.concatenate([embed, jnp.zeros((8 - species, width), F32)], axis=0)
    h = high(e)
    return jnp.concatenate([h, e - h], axis=0).T.astype(BF16)


def far_kinds(g, emb):
    hot = g[16:24]
    return bdot(emb, jnp.concatenate([hot, hot], axis=0).astype(BF16))


def far_positions(g):
    return [
        spread_rows(g[3 * c : 3 * c + 1], 8)
        + spread_rows(g[3 * c + 1 : 3 * c + 2], 8)
        + spread_rows(g[3 * c + 2 : 3 * c + 3], 8)
        for c in range(3)
    ]


def edge_geometry(far, own, counts, tiles):
    centre = [jnp.concatenate([spread_rows(own[c : c + 1], 8)] * tiles, axis=1) for c in range(3)]
    valid = jnp.concatenate([(counts > F32(k)).astype(F32) for k in range(tiles)], axis=1)
    return geometry(far, centre, valid)


def messages(w, h, unit, width, tiles):
    atoms = 128
    wa = w[:width] * h
    wb = w[width:] * h
    a_sum = jnp.zeros((width, atoms), F32)
    b_sum = [jnp.zeros((width, atoms), F32) for _ in range(3)]
    for k in range(tiles):
        a_sum = a_sum + wa[:, slot(k)]
        for c in range(3):
            b_sum[c] = b_sum[c] + wb[:, slot(k)] * tile8(unit[c][:, slot(k)], width // 8)
    return a_sum, b_sum


def tile8(x, times):
    return jnp.concatenate([x] * times, axis=0)


def mixed_pre(a, b_all, h0_own, mix_ref):
    atoms = a.shape[1]
    sq = b_all * b_all
    q = sq[:, :atoms] + sq[:, atoms : 2 * atoms] + sq[:, 2 * atoms :]
    return hdot_t(mix_ref[0], a) + hdot_t(mix_ref[1], h0_own) + hdot_t(mix_ref[2], q)


def features(pre, b_all, vec):
    atoms = pre.shape[1]
    v1 = hdot_t(vec, b_all)
    return (
        jnp.concatenate([pre * sigmoid(pre), v1[:, :atoms]], axis=0),
        jnp.concatenate([v1[:, atoms : 2 * atoms], v1[:, 2 * atoms :]], axis=0),
    )


def doubled(x):
    rows = x.shape[0]
    low = lane_low(rows)
    other = roll64(x)
    return jnp.where(low == parity_odd(rows), x, other)


def layer_one_kernel(
    sent_ref,
    come_ref,
    sel_ref,
    embed_ref,
    win_ref,
    wmid_ref,
    wout_ref,
    mix_ref,
    vec_ref,
    feats_ref,
    far_feats_ref,
    near_out,
    tab_ref,
    ftab_ref,
    emb_ref,
    geom_ref,
    basis_ref,
    pre_ref,
    b_ref,
    there_ref,
    sel_far_ref,
):
    atoms = sent_ref.shape[1]
    slots = sel_ref.shape[1] // atoms
    tiles = slots // 2
    width = embed_ref.shape[1]
    embed = embed_ref[...]
    scale = 1.0 / jnp.sqrt(F32(slots))
    ours = far_lanes(4)
    own = sent_ref[0:4]
    near = sent_ref[4:8]
    me = jnp.full(sent_ref.shape, lax.axis_index("space"), jnp.int32)
    has = jnp.logical_and(me > 0, me < lax.axis_size("space") - 1)
    there = jnp.where(parity_odd(sent_ref.shape[0]), come_ref[1], come_ref[0])
    there = jnp.where(has, there, jnp.zeros(sent_ref.shape, F32))
    there_ref[...] = there
    low12 = lane_low(tiles)
    lists = there[8 : 8 + slots]
    first = lists[:tiles]
    second = lists[tiles:]
    odd12 = parity_odd(tiles)
    build_selector(
        jnp.where(
            low12,
            jnp.where(odd12, first, roll64(first)),
            jnp.where(odd12, roll64(second), second),
        ),
        sel_far_ref,
    )
    species = embed.shape[0]
    make_table(
        jnp.concatenate([own, jnp.where(ours, there[0:4], near)], axis=1), species, tab_ref
    )
    make_table(
        jnp.concatenate([there[0:4], jnp.where(ours, there[4:8], own)], axis=1), species, ftab_ref
    )
    emb = embed_rows(embed)
    emb_ref[...] = emb
    h0 = hdot_t(embed, kinds(own[3:4], species)[:species])
    h0_far = hdot_t(embed, kinds(doubled(there[0:8])[3:4], species)[:species])
    g = bdot(tab_ref[...], sel_ref[...])
    gf = bdot(ftab_ref[...], sel_far_ref[...])

    edges = slots * atoms
    half = doubled(there)
    far = [jnp.concatenate(x, axis=1) for x in zip(far_positions(g), far_positions(gf))]
    centre = [
        jnp.concatenate(
            [spread_rows(own[c : c + 1], 8)] * slots + [spread_rows(half[c : c + 1], 8)] * tiles,
            axis=1,
        )
        for c in range(3)
    ]
    counts = spread_rows(sent_ref[8 + slots : 9 + slots, :], 8)
    far_counts = spread_rows(half[8 + slots : 9 + slots], 8) - jnp.where(
        lane_low(8), F32(0), F32(tiles)
    )
    valid = jnp.concatenate(
        [(counts > F32(k)).astype(F32) for k in range(slots)]
        + [(far_counts > F32(k)).astype(F32) for k in range(tiles)],
        axis=1,
    )
    unit, inv, b, db = geometry(far, centre, valid)
    for i, x in enumerate(unit + [inv]):
        geom_ref[i : i + 1, :] = x[0:1, :edges]
    basis_ref[0] = b[:, :edges]
    basis_ref[1] = db[:, :edges]
    hot = jnp.concatenate([g[16:24], gf[16:24]], axis=1)
    h = bdot(emb, jnp.concatenate([hot, hot], axis=0).astype(BF16))
    w = radial(win_ref[0], wmid_ref[0], wout_ref[0], b)
    wa = w[:width] * h
    wb = w[width:] * h

    def summed(first, count):
        sums = [jnp.zeros((width, atoms), F32) for _ in range(4)]
        for k in range(first, first + count):
            x = wb[:, slot(k)]
            sums[0] = sums[0] + wa[:, slot(k)]
            for c in range(3):
                sums[c + 1] = sums[c + 1] + x * tile8(unit[c][:, slot(k)], width // 8)
        return sums

    ours_sum = summed(0, slots)
    theirs = [x + roll64(x) for x in summed(slots, tiles)]
    both = [jnp.concatenate([x, y], axis=1) * scale for x, y in zip(ours_sum, theirs)]
    q = both[1] * both[1] + both[2] * both[2] + both[3] * both[3]
    pre = (
        hdot_t(mix_ref[0], both[0])
        + hdot_t(mix_ref[1], jnp.concatenate([h0, h0_far], axis=1))
        + hdot_t(mix_ref[2], q)
    )
    pre_ref[...] = pre[:, :atoms]
    for c in range(3):
        b_ref[:, slot(c)] = both[c + 1][:, :atoms]
    s1 = pre * sigmoid(pre)
    v1 = hdot_t(vec_ref[...], jnp.concatenate(both[1:], axis=1))
    for domain, ref in ((0, feats_ref), (1, far_feats_ref)):
        ref[0:width] = s1[:, slot(domain)]
        for c in range(3):
            ref[(c + 1) * width : (c + 2) * width] = v1[:, slot(2 * c + domain)]
    low_lanes, high_lanes = packed(feats_ref[0 : 2 * width], feats_ref[2 * width :])
    near_out[...] = jnp.where(parity_odd(2 * width), low_lanes, high_lanes)


def packed(lo_part, hi_part):
    low = lane_low(lo_part.shape[0])
    return (
        jnp.where(low, lo_part, roll64(hi_part)),
        jnp.where(low, roll64(lo_part), hi_part),
    )


def unpacked(tile, high_half):
    other = roll64(tile)
    return jnp.where(high_half, other, tile), jnp.where(high_half, tile, other)


def radial_two_kernel(basis_ref, win_ref, wmid_ref, wout_ref, w_ref, dw_ref):
    w, dw = radial_pair(win_ref[1], wmid_ref[1], wout_ref[1], basis_ref[0], basis_ref[1])
    w_ref[...] = w
    dw_ref[...] = dw


def edge_gradient(unit, inv, drho, du):
    dot = unit[0] * du[0] + unit[1] * du[1] + unit[2] * du[2]
    radial_part = drho - dot * inv
    return [unit[c] * radial_part + du[c] * inv for c in range(3)]


def sum_groups(x):
    total = x[0:8]
    for i in range(1, x.shape[0] // 8):
        total = total + x[8 * i : 8 * i + 8]
    return total


def both_parts(grads):
    x = jnp.concatenate(list(grads), axis=0)
    h = high(x)
    return jnp.concatenate([h, x - h], axis=0).astype(BF16)


def put_positions(ref, base, grads):
    ref[base : base + 48] = both_parts(grads)


def rows8(x):
    sums = [jnp.sum(x[8 * c : 8 * c + 8], axis=0, keepdims=True) for c in range(3)]
    return jnp.concatenate(sums + [jnp.zeros((5, x.shape[1]), F32)], axis=0)


def centre_sum(grads, slots):
    x = jnp.concatenate(list(grads), axis=0)
    total = x[:, slot(0)]
    for k in range(1, slots):
        total = total + x[:, slot(k)]
    return total


def layer_two_kernel(
    feats_ref,
    far_feats_ref,
    near_ref,
    sel_ref,
    geom_ref,
    w_ref,
    dw_ref,
    mix_ref,
    read_ref,
    energy_ref,
    gown_ref,
    gghost_ref,
    near_out,
    far_out,
    gpos_ref,
    gpos_ghost_ref,
    grad_scr,
):
    atoms = feats_ref.shape[1]
    width = mix_ref.shape[1]
    slots = sel_ref.shape[1] // atoms
    rows = 2 * width
    odd = parity_odd(rows)
    ours = far_lanes(rows)
    near_lo, near_hi = unpacked(near_ref[...], odd)
    g_lo = jnp.where(ours, far_feats_ref[0:rows], near_lo)
    g_hi = jnp.where(ours, far_feats_ref[rows:], near_hi)
    feats = feats_ref[...]
    table = jnp.concatenate([feats, jnp.concatenate([g_lo, g_hi], axis=0)], axis=1)
    t_hi, t_lo = split(table)
    sel = sel_ref[...]

    f = bdot(t_hi, sel) + bdot(t_lo, sel)
    unit = [geom_ref[c : c + 1, :] for c in range(3)]
    along = f[width : 2 * width] * spread_rows(unit[0], width)
    along = along + f[2 * width : 3 * width] * spread_rows(unit[1], width)
    along = along + f[3 * width :] * spread_rows(unit[2], width)
    msg = w_ref[0:width] * f[:width] + w_ref[width:] * along
    m = jnp.zeros((width, atoms), F32)
    for k in range(slots):
        m = m + msg[:, slot(k)]
    scale = 1.0 / jnp.sqrt(F32(slots))
    s1 = feats[:width]
    pre = hdot_t(mix_ref[0], m * scale) + hdot_t(mix_ref[1], s1)
    sg = sigmoid(pre)
    s2 = pre * sg
    energy_ref[...] = hdot(read_ref[0:1], s1) + hdot(read_ref[1:2], s2)
    read = read_ref[...].T
    r_one = jnp.broadcast_to(read[:, 0:1], (width, atoms))
    r_two = jnp.broadcast_to(read[:, 1:2], (width, atoms))
    gpre = r_two * (sg + s2 * (1.0 - sg))
    gm = hdot(mix_ref[0], gpre) * scale
    gs_own = r_one + hdot(mix_ref[1], gpre)
    gm_rep = jnp.concatenate([gm] * slots, axis=1)
    ga = w_ref[0:width] * gm_rep
    gb = w_ref[width:] * gm_rep
    for i, x in enumerate([ga] + [gb * spread_rows(u, width) for u in unit]):
        hi, lo = split(x)
        grad_scr[i * width : (i + 1) * width] = hi
        grad_scr[(4 + i) * width : (5 + i) * width] = lo
    drho = gm_rep * (dw_ref[0:width] * f[:width] + dw_ref[width:] * along)
    du = [sum_groups(gb * f[(c + 1) * width : (c + 2) * width]) for c in range(3)]
    gp = edge_gradient(
        [spread_rows(u, 8) for u in unit],
        spread_rows(geom_ref[3:4, :], 8),
        sum_groups(drho),
        du,
    )
    put_positions(grad_scr, 8 * width, gp)
    centre = centre_sum(gp, slots)
    acc = bdot_nt(grad_scr[...], sel_ref[...])
    grads = acc[: 4 * width] + acc[4 * width : 8 * width]
    own = grads[:, :atoms]
    gown_ref[0:width] = own[0:width] + gs_own
    gown_ref[width:] = own[width:]
    ghost = grads[:, atoms:]
    gghost_ref[...] = ghost
    to_upper, to_lower = packed(ghost[:rows], ghost[rows:])
    near_out[...] = jnp.where(odd, to_lower, to_upper)
    far_out[...] = jnp.where(odd, to_upper, to_lower)
    pos = acc[8 * width : 8 * width + 24] + acc[8 * width + 24 :]
    gpos_ref[...] = rows8(pos[:, :atoms] - centre)
    gpos_ghost_ref[...] = rows8(pos[:, atoms:])


def join_kernel(gown_ref, near_ref, far_ref, gpos_ghost_ref, out_ref):
    rows = near_ref.shape[0]
    odd = parity_odd(rows)
    ours = far_lanes(rows)
    zero = jnp.zeros(near_ref.shape, F32)
    lo, hi = unpacked(near_ref[...], jnp.logical_not(odd))
    out_ref[0:rows] = gown_ref[0:rows] + jnp.where(ours, lo, zero)
    out_ref[rows : 2 * rows] = gown_ref[rows:] + jnp.where(ours, hi, zero)
    out_ref[2 * rows : 3 * rows] = far_ref[...]
    out_ref[3 * rows :] = gpos_ghost_ref[...]


def tangent_one_kernel(
    basis_ref,
    tab_ref,
    ftab_ref,
    emb_ref,
    sel_ref,
    there_ref,
    win_ref,
    wmid_ref,
    wout_ref,
    mix_ref,
    embed_ref,
    edge_ref,
    sel_ghost_ref,
    geom_ref,
    pre_ref,
    b_ref,
    sel_scr,
):
    atoms = there_ref.shape[1]
    width = emb_ref.shape[0]
    emb = emb_ref[...]
    slots = sel_ref.shape[1] // atoms
    win, wmid, wout = win_ref[0], wmid_ref[0], wout_ref[0]

    def store(domain, w, dw, h):
        edge_ref[domain, 0:width] = dw[:width] * h
        edge_ref[domain, width : 2 * width] = dw[width:] * h
        edge_ref[domain, 2 * width :] = w[width:] * h

    w, dw = radial_pair(win, wmid, wout, basis_ref[0], basis_ref[1])
    store(0, w, dw, far_kinds(bdot(tab_ref[...], sel_ref[...]), emb))

    there = there_ref[...]
    build_selector(there[8 : 8 + slots], sel_scr)
    sel_ghost_ref[...] = sel_scr[atoms:]
    g = bdot(ftab_ref[...], sel_scr[...])
    far, h = far_positions(g), far_kinds(g, emb)
    counts = spread_rows(there[8 + slots : 9 + slots], 8)
    unit, inv, b, db = edge_geometry(far, there, counts, slots)
    for i, x in enumerate(unit + [inv]):
        geom_ref[i : i + 1, :] = x[0:1]
    w, dw = radial_pair(win, wmid, wout, b, db)
    store(1, w, dw, h)
    a, b = messages(w, h, unit, width, slots)
    scale = 1.0 / jnp.sqrt(F32(slots))
    b_all = jnp.concatenate(b, axis=1) * scale
    species = embed_ref.shape[0]
    onehot = kinds(there[3:4], species)[:species]
    pre_ref[...] = mixed_pre(a * scale, b_all, hdot_t(embed_ref[...], onehot), mix_ref)
    b_ref[...] = b_all


def back_one_kernel(
    sent_ref,
    far_ref,
    gghost_ref,
    sel_ref,
    sel_ghost_ref,
    geom_ref,
    far_geom_ref,
    edge_ref,
    pre_ref,
    far_pre_ref,
    b_ref,
    far_b_ref,
    mix_ref,
    vec_ref,
    gpos_ref,
    gown_out,
    ghost_out,
    pos_scr,
    far_pos_scr,
):
    atoms = gpos_ref.shape[1]
    width = mix_ref.shape[1]
    slots = sel_ref.shape[1] // atoms
    rows = 2 * width
    odd = parity_odd(rows)
    ours = far_lanes(rows)
    zero = jnp.zeros((rows, atoms), F32)
    scale = 1.0 / jnp.sqrt(F32(slots))
    lo, hi = unpacked(far_ref[2 * rows : 3 * rows], odd)
    g_lo = sent_ref[0:rows] + jnp.where(ours, zero, lo)
    g_hi = sent_ref[rows : 2 * rows] + jnp.where(ours, zero, hi)
    f_lo = far_ref[0:rows] + jnp.where(ours, gghost_ref[0:rows], zero)
    f_hi = far_ref[rows : 2 * rows] + jnp.where(ours, gghost_ref[rows:], zero)
    pre = jnp.concatenate([pre_ref[...], far_pre_ref[...]], axis=1)
    sg = sigmoid(pre)
    gpre = jnp.concatenate([g_lo[:width], f_lo[:width]], axis=1) * (sg + pre * sg * (1.0 - sg))
    ga = hdot(mix_ref[0], gpre) * scale
    gq = hdot(mix_ref[2], gpre) * (2.0 * scale)
    gv = jnp.concatenate(
        [g_lo[width:], g_hi[:width], g_hi[width:], f_lo[width:], f_hi[:width], f_hi[width:]],
        axis=1,
    )
    gb_all = hdot(vec_ref[...], gv) * scale
    b_of = [b_ref, far_b_ref]
    geom_of = [geom_ref, far_geom_ref]
    scr_of = [pos_scr, far_pos_scr]
    for domain in range(2):
        ga_d = ga[:, slot(domain)]
        gq_d = gq[:, slot(domain)]
        gb = [
            gb_all[:, slot(3 * domain + c)] + b_of[domain][:, slot(c)] * gq_d for c in range(3)
        ]
        geom = geom_of[domain]
        total = jnp.zeros((24, atoms), F32)
        for k in range(slots):
            unit = [spread_rows(geom[c : c + 1, slot(k)], 8) for c in range(3)]
            u = [tile8(x, width // 8) for x in unit]
            gbu = gb[0] * u[0] + gb[1] * u[1] + gb[2] * u[2]
            drho = (
                edge_ref[domain, 0:width, slot(k)] * ga_d
                + edge_ref[domain, width : 2 * width, slot(k)] * gbu
            )
            carried = edge_ref[domain, 2 * width :, slot(k)]
            du = [sum_groups(carried * gb[c]) for c in range(3)]
            gp = edge_gradient(unit, spread_rows(geom[3:4, slot(k)], 8), sum_groups(drho), du)
            if domain == 0:
                total = total + jnp.concatenate(gp, axis=0)
            scr_of[domain][:, slot(k)] = both_parts(gp)
        if domain == 0:
            centre = total
    acc = bdot_nt(pos_scr[...], sel_ref[...])
    pos = acc[0:24] + acc[24:48]
    ghost_out[...] = rows8(pos[:, atoms:]) + sent_ref[3 * rows :]
    acc = bdot_nt(far_pos_scr[...], sel_ghost_ref[...])
    there = rows8(acc[0:24] + acc[24:48]) + far_ref[3 * rows :]
    there = jnp.where(far_lanes(8), jnp.zeros((8, atoms), F32), there)
    gown_out[...] = gpos_ref[...] + rows8(pos[:, :atoms] - centre) + there


def call(kernel, out_shapes, args, scratch=(), flops=0, transcendentals=0, far_away=0):
    args = [
        pltpu.with_memory_space_constraint(x, pltpu.HBM) if i < far_away else x
        for i, x in enumerate(args)
    ]
    spaces = [pltpu.HBM] * far_away + [pltpu.VMEM] * (len(args) - far_away)
    moved = sum(x.size * x.dtype.itemsize for x in list(args) + list(out_shapes))
    return pl.pallas_call(
        kernel,
        out_shape=out_shapes,
        in_specs=[pl.BlockSpec(memory_space=space) for space in spaces],
        out_specs=[pl.BlockSpec(memory_space=pltpu.VMEM)] * len(out_shapes),
        scratch_shapes=list(scratch),
        cost_estimate=pl.CostEstimate(
            flops=flops, bytes_accessed=moved, transcendentals=transcendentals
        ),
        compiler_params=pltpu.CompilerParams(vmem_limit_bytes=36 * MIB),
    )(*args)


def shape(dims, dtype=F32):
    return jax.ShapeDtypeStruct(dims, dtype)


def body(
    positions,
    species,
    neighbours,
    counts,
    ghost_index,
    embed,
    radial_in,
    radial_mid,
    radial_out,
    mix_one,
    vec_mix,
    mix_two,
    readout,
):
    atoms = positions.shape[1]
    slots = neighbours.shape[0]
    edges = slots * atoms
    nbasis, hidden = radial_in.shape[1:]
    width = embed.shape[1]
    rows = 2 * width
    devices = lax.axis_size("space")
    near_route = [(i, i ^ 1) for i in range(devices)]
    far_route = [(i, ((i + 1) ^ 1) - 1) for i in range(1, devices - 1)]

    def swap_near(x):
        return lax.ppermute(x, "space", near_route)

    def swap_far(x):
        return lax.ppermute(x, "space", far_route)

    def scratch_of(args):
        return [pltpu.VMEM(x.shape, x.dtype) for x in args]

    def shapes_of(args):
        return [shape(x.shape, x.dtype) for x in args]

    near_pos = swap_near(positions)
    near_kind = swap_near(species)
    local = [positions, species[None], neighbours, ghost_index, counts[None]]
    weights = [radial_in, radial_mid, radial_out]
    passed = [embed, mix_one, vec_mix, mix_two, readout]
    moved = local + weights + passed
    own, edge_rows, sel, win, wmid, wout, embed, mix_one, vec_mix, mix_two, readout = call(
        prep_kernel,
        [
            shape((4, atoms)),
            shape((slots + 8, atoms)),
            shape((2 * atoms, edges), BF16),
            shape((2, hidden, 4 * nbasis), BF16),
            shape((2, hidden, 3 * hidden), BF16),
            shape((2, 2 * width, 3 * hidden), BF16),
        ]
        + shapes_of(passed),
        moved,
        scratch=scratch_of(local + weights)
        + [pltpu.VMEM((atoms, edges), BF16), pltpu.SemaphoreType.DMA((len(moved),))],
        flops=10**8,
        far_away=len(moved),
    )
    near_rows = [near_pos, (near_kind + 1).astype(F32)[None]]
    sent = jnp.concatenate([own] + near_rows + [edge_rows], axis=0)
    pairs = [[i, (i + 1) % devices] for i in range(1, devices, 2)]
    come = lax.all_gather(sent, "space", axis_index_groups=pairs)
    feats, far_feats, near_f, tab, ftab, emb, geom, basis, pre, b_all, there = call(
        layer_one_kernel,
        [
            shape((4 * width, atoms)),
            shape((4 * width, atoms)),
            shape((rows, atoms)),
            shape((32, 2 * atoms), BF16),
            shape((32, 2 * atoms), BF16),
            shape((width, 16), BF16),
            shape((8, edges)),
            shape((2, nbasis, edges)),
            shape((width, atoms)),
            shape((width, 3 * atoms)),
            shape((slots + 16, atoms)),
        ],
        [sent, come, sel, embed, win, wmid, wout, mix_one, vec_mix],
        scratch=[pltpu.VMEM((2 * atoms, edges // 2), BF16)],
        flops=2 * 10**9,
    )
    near_f = swap_near(near_f)
    w, dw = call(
        radial_two_kernel,
        [shape((2 * width, edges)), shape((2 * width, edges))],
        [basis, win, wmid, wout],
        flops=2 * 10**9,
    )
    energy, g_own, g_ghost, near_g, far_g, gpos, gpos_ghost = call(
        layer_two_kernel,
        [
            shape((1, atoms)),
            shape((4 * width, atoms)),
            shape((4 * width, atoms)),
            shape((rows, atoms)),
            shape((rows, atoms)),
            shape((8, atoms)),
            shape((8, atoms)),
        ],
        [feats, far_feats, near_f, sel, geom, w, dw, mix_two, readout],
        scratch=[pltpu.VMEM((8 * width + 48, edges), BF16)],
        flops=10**9,
    )
    near_g = swap_near(near_g)
    (sent,) = call(
        join_kernel, [shape((3 * rows + 8, atoms))], [g_own, near_g, far_g, gpos_ghost]
    )
    come = swap_far(sent)
    edge, sel_ghost, far_geom, far_pre, far_b = call(
        tangent_one_kernel,
        [
            shape((2, 3 * width, edges)),
            shape((atoms, edges), BF16),
            shape((8, edges)),
            shape((width, atoms)),
            shape((width, 3 * atoms)),
        ],
        [basis, tab, ftab, emb, sel, there, win, wmid, wout, mix_one, embed],
        scratch=[pltpu.VMEM((2 * atoms, edges), BF16)],
        flops=4 * 10**9,
    )
    centre, ghost = call(
        back_one_kernel,
        [shape((8, atoms)), shape((8, atoms))],
        [
            sent,
            come,
            g_ghost,
            sel,
            sel_ghost,
            geom,
            far_geom,
            edge,
            pre,
            far_pre,
            b_all,
            far_b,
            mix_one,
            vec_mix,
            gpos,
        ],
        scratch=[pltpu.VMEM((48, edges), BF16), pltpu.VMEM((48, edges), BF16)],
        flops=10**9,
    )
    near_p = swap_near(ghost)
    odd = lax.rem(lax.axis_index("space"), 2) == 1
    low = lax.broadcasted_iota(jnp.int32, (3, atoms), 1) < HALF
    back = jnp.where(low == odd, near_p[:3], 0.0)
    return (energy[0], -(centre[:3] + back))


def solution(mesh):
    placed = (
        P(None, "space"),
        P("space"),
        P(None, "space"),
        P("space"),
        P(None, "space"),
        P(),
        P(),
        P(),
        P(),
        P(),
        P(),
        P(),
        P(),
    )
    return jax.shard_map(
        body, mesh=mesh, in_specs=placed, out_specs=(P("space"), P(None, "space")), check_vma=False
    )
```
